32 devices in a mesh: groups: 2 (over y), chan: 4 (over z), win: 2 (over x), sub: 2 (over core).
Axes of the slice: x: 2, y: 2, z: 4, core: 2. Of those that a mesh axis runs over, the one named last changes fastest.
Arguments:
- traces: bfloat16 [4, 2560, 1024], P(('groups', 'win'), 'chan'), parts along dimension 0, may hold values from -240 to 240, as said below
- channel_mask: int32 [5120], P(('groups', 'chan')), parts along dimension 0, may hold values 0 or 1
- smooth_width: int32 [512], replicated, may hold values from 1 to 16, as said below
- source_phase: int32 [8], P('groups'), parts along dimension 0, may hold values from 0 to 7
- pair_list: int32 [8, 5], P('groups'), parts along dimension 0, may hold values 0 or 1
Outputs:
- receiver_stack: float32 [8, 5, 101, 5120], P(('win', 'sub'), None, None, ('groups', 'chan')), parts along dimension 3
- source_stack: float32 [64, 5, 101, 640], P(('groups', 'chan', 'win', 'sub')), parts along dimension 0
The draws below stay inside these ranges and needn't reach their ends.
There are 2 independent parts, one for each index of `groups`. The reference program is written for one: setup_inputs(seed, part) draws one part's arguments, and reference() takes and returns one part's arrays. A program takes and returns all parts, laid end to end along the dimension named above; an argument that names none is the same for every part. Nothing has to cross between parts.
Inputs may be any that keep to these rules, and one draw needn't show every extreme that they name: `traces`: float samples; each channel and each window has a scale of its own. `smooth_width`: every value from 1 to 16 may occur; 16 occurs in every draw.
All inputs are finite; a program needn't handle non-finite values. No bound on the sum of `channel_mask` on one device may be relied on, other than what follows from the above.
Results may differ from the reference program's by a relative error of at most 0.0052.
Values may be sent and summed in bfloat16 or wider, within the bound.
No kernel may reach another device: no remote copies, remote signals or barrier semaphores. Data moves between devices by JAX's collectives and lax.ppermute only.
A program may use at most 192 MiB of HBM per device.

```python
import math
import jax
import jax.numpy as jnp
from jax import lax

NB = 512
MAXLAG = 50
STRIDE = 8
SMAX = 16
REACH = 2
CB = 640
VS = 8
LSAMP = 1024
LAGS = 101
OFFS = 5
NBLK = 4
NCH = 2560
NSRC = 32
WINDOWS = 2


def draw_traces(key, part):
    k_noise, k_chan, k_win = jax.random.split(key, 3)
    chan_scale = jnp.exp(jax.random.uniform(k_chan, (NCH,), jnp.float32, 0.0, math.log(10.0)))
    win_scale = jnp.exp(jax.random.uniform(k_win, (WINDOWS,), jnp.float32, 0.0, math.log(4.0)))
    noise_draw = jnp.clip(jax.random.normal(k_noise, (WINDOWS, NCH, LSAMP), jnp.float32), -6.0, 6.0)
    return (noise_draw * chan_scale[None, :, None] * win_scale[:, None, None]).astype(jnp.bfloat16)


def draw_smooth_width(key, part):
    k_vals, k_pos = jax.random.split(jax.random.fold_in(key, 17))
    widths = jax.random.randint(k_vals, (NB,), 1, SMAX + 1)
    spot_ids = jax.random.randint(k_pos, (2,), 0, NB)
    bin_ids = jnp.arange(NB)
    widths = jnp.where(bin_ids == spot_ids[0], SMAX, widths)
    widths = jnp.where((bin_ids == spot_ids[1]) & (bin_ids != spot_ids[0]), 1, widths)
    return widths.astype(jnp.int32)


def place_ends(entries, stream_key, least, largest):
    place = [jax.random.randint(jax.random.fold_in(stream_key, axis), (), 0, length) for axis, length in enumerate(entries.shape)]
    main_axis = entries.shape.index(max(entries.shape))
    neighbour = place[:main_axis] + [(place[main_axis] + 1) % entries.shape[main_axis]] + place[main_axis + 1:]
    return entries.at[tuple(place)].set(least).at[tuple(neighbour)].set(largest)


def setup_inputs(seed: int = 0, part: int = 0) -> dict:
    keys = jax.random.split(jax.random.key(seed), 6)
    own_keys = jax.random.split(jax.random.fold_in(keys[5], part), 6)
    return {
        "traces": draw_traces(jax.random.fold_in(jax.random.fold_in(keys[5], part), 71), part),
        "channel_mask": place_ends((jax.random.randint(own_keys[1], (NCH,), 0, 8) < 7).astype(jnp.int32), jax.random.fold_in(own_keys[1], 1), 0, 1),
        "smooth_width": draw_smooth_width(jax.random.fold_in(keys[5], 71), part),
        "source_phase": place_ends(jax.random.randint(own_keys[3], (NBLK,), 0, STRIDE), jax.random.fold_in(own_keys[3], 1), 0, STRIDE - 1).astype(jnp.int32),
        "pair_list": place_ends((jax.random.randint(own_keys[4], (NBLK, OFFS), 0, 4) < 3).astype(jnp.int32), jax.random.fold_in(own_keys[4], 1), 0, 1),
    }


FLOOR = 0.25

def dft_tables(samples, bin_ids):
    sample_ids = jnp.arange(samples, dtype=jnp.int32)
    phases = sample_ids[:, None] * bin_ids[None, :] % samples
    angles = phases.astype(jnp.float32) * (2.0 * math.pi / samples)
    return jnp.concatenate([jnp.cos(angles), -jnp.sin(angles)], axis=1)

def lag_tables(samples, bin_ids, maxlag):
    lag_ids = jnp.arange(2 * maxlag + 1, dtype=jnp.int32) - maxlag
    phases = lag_ids[:, None] * bin_ids[None, :] % samples
    angles = phases.astype(jnp.float32) * (2.0 * math.pi / samples)
    return jnp.stack([jnp.cos(angles), -jnp.sin(angles)], axis=1)

def smoothing_weights(row_ids, bin_ids, widths, bin_total):
    nearby = jnp.abs(row_ids[:, None] - bin_ids[None, :]) <= widths[None, :]
    inside = (row_ids >= 0) & (row_ids < bin_total)
    return jnp.where(nearby & inside[:, None], 1.0, 0.0).astype(jnp.float32)

def cross_lags(sources, spectra, lag_tab):
    turned = jnp.stack([sources[:, 1], -sources[:, 0]], axis=1)
    stacked_pair = jnp.stack([sources, turned], axis=0)
    cross_spec = jnp.einsum('pwqvk,wqkc->pkvc', stacked_pair, spectra, precision=lax.Precision.HIGHEST)
    return jnp.einsum('tpk,pkvc->vtc', lag_tab, cross_spec, precision=lax.Precision.HIGHEST)

def reference(traces, channel_mask, smooth_width, source_phase, pair_list):
    bin_ids = jnp.arange(NB, dtype=jnp.int32)
    tables = dft_tables(LSAMP, bin_ids).astype(jnp.bfloat16)
    tables = lax.optimization_barrier(tables).astype(jnp.float32)
    spectrum = jnp.einsum('wcn,nk->wkc', traces.astype(jnp.float32), tables, precision=lax.Precision.HIGHEST) * LSAMP ** (-0.5)
    spectrum = spectrum * channel_mask.astype(jnp.float32)[None, None, :]
    spectrum = spectrum.reshape(WINDOWS, 2, NB, NCH)
    amplitude = jnp.sqrt(spectrum[:, 0] ** 2 + spectrum[:, 1] ** 2)
    weights = smoothing_weights(bin_ids, bin_ids, smooth_width, NB)
    smoothed = jnp.einsum('wjc,jk->wkc', amplitude, weights, precision=lax.Precision.HIGHEST) / lax.optimization_barrier(jnp.sum(weights, axis=0))[None, :, None]
    whitened = (spectrum / jnp.maximum(smoothed, FLOOR)[:, None]).astype(jnp.bfloat16)
    white_full = lax.optimization_barrier(whitened).astype(jnp.float32)
    grouped = white_full.reshape(WINDOWS, 2, NB, NBLK, CB // STRIDE, STRIDE)[:, :, :, :, :VS]
    picker = jnp.where(jnp.arange(STRIDE, dtype=jnp.int32)[None, :] == source_phase[:, None], 1.0, 0.0).astype(jnp.float32)
    sources = jnp.einsum('wqkbvs,bs->bwqvk', grouped, picker, precision=lax.Precision.HIGHEST)
    receivers = jnp.transpose(white_full.reshape(WINDOWS, 2, NB, NBLK, CB), (3, 0, 1, 2, 4))
    lag_tab = lag_tables(LSAMP, bin_ids, MAXLAG)
    factor = (NB * WINDOWS) ** (-0.5)
    stacks = []
    for offset in range(OFFS):
        moved_by = offset - REACH
        moved = jnp.roll(sources, moved_by, axis=0)
        paired = jnp.roll(pair_list[:, offset], moved_by).astype(jnp.float32)

        def one_block(block_items):
            return cross_lags(block_items[0], block_items[1], lag_tab) * block_items[2]
        lags_block = lax.map(one_block, (moved, receivers, paired))
        stacks.append(lags_block * factor)
    stacked = jnp.stack(stacks, axis=0)
    receiver_stack = jnp.transpose(stacked, (2, 0, 3, 1, 4)).reshape(VS, OFFS, LAGS, NCH)
    turned_back = []
    for offset in range(OFFS):
        moved_by = offset - REACH
        turned_back.append(jnp.flip(jnp.roll(stacked[offset], -moved_by, axis=0), axis=2))
    source_stack = jnp.transpose(jnp.stack(turned_back, axis=0), (1, 2, 0, 3, 4)).reshape(NSRC, OFFS, LAGS, CB)
    return (receiver_stack, source_stack)
```

```python
import functools
import math

import jax
import jax.numpy as jnp
import numpy as np
from jax import lax
from jax.experimental import pallas as pl
from jax.experimental.pallas import tpu as pltpu
from jax.sharding import PartitionSpec as P

NB = 512
MAXLAG = 50
STRIDE = 8
REACH = 2
VS = 8
OFFS = 5
LAGS = 2 * MAXLAG + 1
ROWS = 104
FLOOR = 0.25
VMEM = pl.BlockSpec(memory_space=pltpu.VMEM)
SMEM = pl.BlockSpec(memory_space=pltpu.SMEM)
NT = (((1,), (1,)), ((), ()))


def dft_table(samples):
    phases = np.arange(samples)[:, None] * np.arange(NB)[None, :] % samples
    angles = phases * (2.0 * math.pi / samples)
    table = np.concatenate([np.cos(angles), -np.sin(angles)], axis=1)
    return jnp.asarray(table.astype(np.float32), jnp.bfloat16)


def lag_table(samples):
    phases = (np.arange(LAGS) - MAXLAG)[:, None] * np.arange(NB)[None, :] % samples
    angles = phases * (2.0 * math.pi / samples)
    table = np.concatenate([np.cos(angles), np.sin(angles)], axis=1)
    return jnp.asarray(np.pad(table, ((0, ROWS - LAGS), (0, 0))), jnp.float32)


def flip_table(per_device):
    flip = np.zeros((ROWS, ROWS))
    flip[np.arange(LAGS), LAGS - 1 - np.arange(LAGS)] = 1.0
    return jnp.asarray(np.kron(np.eye(per_device), flip), jnp.bfloat16)


def params(mib):
    return pltpu.CompilerParams(vmem_limit_bytes=mib << 20)


def cost(flops, moved):
    return pl.CostEstimate(flops=flops, bytes_accessed=moved, transcendentals=0)


def whiten(rows, table, weights, share):
    samples = rows.shape[1]
    spectrum = jnp.dot(rows, table, preferred_element_type=jnp.float32) * samples ** (-0.5)
    real, imag = spectrum[:, :NB], spectrum[:, NB:]
    amplitude = jnp.sqrt(real * real + imag * imag)
    high = amplitude.astype(jnp.bfloat16)
    low = (amplitude - high.astype(jnp.float32)).astype(jnp.bfloat16)
    total = jnp.dot(high, weights, preferred_element_type=jnp.float32)
    total += jnp.dot(low, weights, preferred_element_type=jnp.float32)
    gain = 1.0 / jnp.maximum(total * share, FLOOR)
    return (real * gain).astype(jnp.bfloat16), (imag * gain).astype(jnp.bfloat16)


def own_kernel(traces, table, widths, out, weights, share):
    reach = widths[...]
    near = lax.broadcasted_iota(jnp.int32, (NB, NB), 0)
    here = lax.broadcasted_iota(jnp.int32, (NB, NB), 1)
    weights[...] = jnp.where(jnp.abs(near - here) <= reach, 1.0, 0.0).astype(jnp.bfloat16)
    bins = lax.broadcasted_iota(jnp.int32, (1, NB), 1)
    count = jnp.minimum(bins + reach, NB - 1) - jnp.maximum(bins - reach, 0) + 1
    share[...] = 1.0 / count.astype(jnp.float32)
    rows_kernel(traces, table, weights, share, out)


def rows_kernel(traces, table, weights, share, out):
    channels = traces.shape[0]
    step = 320 if channels % 320 == 0 else channels

    def body(i, carry):
        rows = pl.ds(pl.multiple_of(i * step, step), step)
        real, imag = whiten(traces[rows, :], table[...], weights[...], share[...])
        out[rows, :NB] = real
        out[rows, NB:] = imag
        return carry

    lax.fori_loop(0, channels // step, body, 0)


def lag_kernel(moves, axes, per_device, picked, table, weights, share, lags, own, rest, first, spectra, turned):
    blocks, windows, subs = axes
    block_at, win_at, sub_at = lax.axis_index("chan"), lax.axis_index("win"), lax.axis_index("sub")
    real, imag = whiten(picked[...], table[...], weights[...], share[...])
    spectra[:, :NB] = real.astype(jnp.float32)
    spectra[:, NB:] = imag.astype(jnp.float32)
    first_source = (win_at * subs + sub_at) * per_device
    cosine, sine = lags[:, :NB], lags[:, NB:]
    span = per_device * ROWS
    for at, moved in enumerate(moves):
        source_block = lax.rem(block_at - moved + blocks, blocks)
        spot = pl.ds(at * span, span)
        for behind in range(windows):
            window = lax.rem(win_at - behind + windows, windows)
            first_row = (source_block * windows + window) * VS + first_source
            up, down = [], []
            for v in range(per_device):
                source = spectra[pl.ds(first_row + v, 1), :]
                real, imag = source[:, :NB], source[:, NB:]
                up.append(real * cosine - imag * sine)
                down.append(real * sine + imag * cosine)
            target = turned if behind == 0 else rest.at[behind - 1]
            target[spot, :NB] = jnp.concatenate(up, axis=0).astype(jnp.bfloat16)
            target[spot, NB:] = jnp.concatenate(down, axis=0).astype(jnp.bfloat16)

    def body(i, carry):
        rows = pl.ds(pl.multiple_of(i * span, span), span)
        first[rows, :] = lax.dot_general(turned[rows, :], own[...], NT, preferred_element_type=jnp.float32)
        return carry

    lax.fori_loop(0, len(moves), body, 0)


def piece_kernel(moves, factor, per_device, *refs):
    count = len(moves)
    rest, first, mask, mine, other = refs[:5]
    pieces, full = refs[5:5 + count], refs[5 + count]
    sub_at = lax.axis_index("sub")
    half = mine.shape[1]
    full[:, pl.ds(pl.multiple_of(sub_at * half, half), half), :] = mine[...]
    full[:, pl.ds(pl.multiple_of((1 - sub_at) * half, half), half), :] = other[...]
    scale = mask[...].astype(jnp.float32) * factor
    span = per_device * ROWS
    for at in range(count):
        rows = pl.ds(at * span, span)
        total = first[rows, :]
        for behind in range(rest.shape[0]):
            total += lax.dot_general(rest[behind, rows, :], full[behind], NT, preferred_element_type=jnp.float32)
        pieces[at][...] = (total * scale).astype(jnp.bfloat16)


def receiver_kernel(moves, blocks, per_device, pairs, *refs):
    pieces, out = refs[:-1], refs[-1]
    block_at = lax.axis_index("chan")
    for e in range(OFFS):
        moved = e - REACH
        piece = pieces[index_of(moves, moved, blocks)][...].astype(jnp.float32)
        pair = pairs[lax.rem(block_at - moved + blocks, blocks), e].astype(jnp.float32)
        for v in range(per_device):
            out[v, e] = piece[v * ROWS:v * ROWS + LAGS, :] * pair


def source_kernel(moves, blocks, per_device, pairs, flip, *refs):
    pieces, out = refs[:-1], refs[-1]
    block_at = lax.axis_index("chan")
    for e in range(OFFS):
        moved = e - REACH
        piece = pieces[index_of(moves, moved, blocks)][...]
        turned = jnp.dot(flip[...], piece, preferred_element_type=jnp.float32)
        pair = pairs[block_at, e].astype(jnp.float32)
        for v in range(per_device):
            out[v, e] = turned[v * ROWS:v * ROWS + LAGS, :] * pair


def index_of(moves, moved, blocks):
    return [(m - moved) % blocks for m in moves].index(0)


def distinct_moves(blocks):
    moves = []
    for moved in (2, -2, 1, -1, 0):
        if all((m - moved) % blocks for m in moves):
            moves.append(moved)
    return moves


def shift(block, axis, distance):
    count = lax.axis_size(axis)
    return lax.ppermute(block, axis, [(i, (i + distance) % count) for i in range(count)])


def on_device(traces, channel_mask, smooth_width, source_phase, pair_list):
    _, channels, samples = traces.shape
    blocks, windows, subs = (lax.axis_size(a) for a in ("chan", "win", "sub"))
    block_at, sub_at = lax.axis_index("chan"), lax.axis_index("sub")
    per_device = VS // (windows * subs)
    moves = distinct_moves(blocks)
    span = per_device * ROWS
    half = channels // subs
    table, lags, flip = dft_table(samples), lag_table(samples), flip_table(per_device)
    factor = (NB * windows) ** (-0.5)

    phase = source_phase[block_at]
    head = traces[0, :VS * STRIDE].reshape(VS, STRIDE, samples)
    picked = lax.dynamic_index_in_dim(head, phase, axis=1, keepdims=False)
    alive = lax.dynamic_index_in_dim(
        channel_mask[:VS * STRIDE].reshape(VS, STRIDE), phase, axis=1, keepdims=False
    )
    picked = picked * alive[:, None].astype(picked.dtype)
    share_out = lax.dynamic_slice_in_dim(traces[0], sub_at * half, half, axis=0)
    moved_halves = [shift(share_out, "win", d) for d in range(1, windows)]
    all_picked = lax.all_gather(picked, ("chan", "win"), axis=0, tiled=True)

    table_flops = 2 * samples * 2 * NB + 4 * NB * NB
    own, weights, share = pl.pallas_call(
        own_kernel,
        out_shape=(
            jax.ShapeDtypeStruct((channels, 2 * NB), jnp.bfloat16),
            jax.ShapeDtypeStruct((NB, NB), jnp.bfloat16),
            jax.ShapeDtypeStruct((1, NB), jnp.float32),
        ),
        in_specs=[VMEM, VMEM, VMEM],
        out_specs=(VMEM, VMEM, VMEM),
        compiler_params=params(24),
        cost_estimate=cost(channels * table_flops, 6 << 20),
        name="whiten_own",
    )(traces[0], table, smooth_width.reshape(1, NB))

    rest, first = pl.pallas_call(
        functools.partial(lag_kernel, moves, (blocks, windows, subs), per_device),
        out_shape=(
            jax.ShapeDtypeStruct((windows - 1, len(moves) * span, 2 * NB), jnp.bfloat16),
            jax.ShapeDtypeStruct((len(moves) * span, channels), jnp.float32),
        ),
        in_specs=[VMEM] * 6,
        out_specs=(VMEM, VMEM),
        scratch_shapes=[
            pltpu.VMEM((blocks * windows * VS, 2 * NB), jnp.float32),
            pltpu.VMEM((len(moves) * span, 2 * NB), jnp.bfloat16),
        ],
        compiler_params=params(32),
        cost_estimate=cost(len(moves) * span * 2 * NB * channels * 2, 9 << 20),
        name="turn_sources",
    )(all_picked, table, weights, share, lags, own)

    mine = [
        pl.pallas_call(
            rows_kernel,
            out_shape=jax.ShapeDtypeStruct((half, 2 * NB), jnp.bfloat16),
            in_specs=[VMEM] * 4,
            out_specs=VMEM,
            compiler_params=params(24),
            cost_estimate=cost(half * table_flops, 4 << 20),
            name="whiten_half",
        )(piece, table, weights, share)
        for piece in moved_halves
    ]
    other = [shift(piece, "sub", 1) for piece in mine]
    pieces = pl.pallas_call(
        functools.partial(piece_kernel, moves, factor, per_device),
        out_shape=tuple(jax.ShapeDtypeStruct((span, channels), jnp.bfloat16) for _ in moves),
        in_specs=[VMEM] * 5,
        out_specs=tuple(VMEM for _ in moves),
        scratch_shapes=[pltpu.VMEM((windows - 1, channels, 2 * NB), jnp.bfloat16)],
        compiler_params=params(32),
        cost_estimate=cost(len(moves) * span * 2 * NB * channels * 2, 9 << 20),
        name="lag_pieces",
    )(rest, first, channel_mask.reshape(1, channels), jnp.stack(mine), jnp.stack(other))

    back = [p if m % blocks == 0 else shift(p, "chan", -m) for m, p in zip(moves, pieces)]
    stack_shape = jax.ShapeDtypeStruct((per_device, OFFS, LAGS, channels), jnp.float32)
    receiver_stack = pl.pallas_call(
        functools.partial(receiver_kernel, moves, blocks, per_device),
        out_shape=stack_shape,
        in_specs=[SMEM] + [VMEM] * len(moves),
        out_specs=VMEM,
        compiler_params=params(16),
        cost_estimate=cost(1 << 20, 4 << 20),
        name="receiver_order",
    )(pair_list, *pieces)
    source_stack = pl.pallas_call(
        functools.partial(source_kernel, moves, blocks, per_device),
        out_shape=stack_shape,
        in_specs=[SMEM] + [VMEM] * (1 + len(moves)),
        out_specs=VMEM,
        compiler_params=params(16),
        cost_estimate=cost(1 << 20, 4 << 20),
        name="source_order",
    )(pair_list, flip, *back)
    return (receiver_stack, source_stack)


def solution(mesh):
    in_specs = (
        P(("groups", "win"), "chan", None),
        P(("groups", "chan")),
        P(),
        P("groups"),
        P("groups", None),
    )
    out_specs = (
        P(("win", "sub"), None, None, ("groups", "chan")),
        P(("groups", "chan", "win", "sub"), None, None, None),
    )
    return jax.shard_map(
        on_device, mesh=mesh, in_specs=in_specs, out_specs=out_specs, check_vma=False
    )
```

```python
import functools
import math

import jax
import jax.numpy as jnp
import numpy as np
from jax import lax
from jax.experimental import pallas as pl
from jax.experimental.pallas import tpu as pltpu
from jax.sharding import PartitionSpec as P

NB = 512
MAXLAG = 50
STRIDE = 8
REACH = 2
VS = 8
OFFS = 5
LAGS = 2 * MAXLAG + 1
FLOOR = 0.25
LANES = 128
VMEM = pl.BlockSpec(memory_space=pltpu.VMEM)
SMEM = pl.BlockSpec(memory_space=pltpu.SMEM)
HBM = pl.BlockSpec(memory_space=pltpu.HBM)
NT = (((1,), (1,)), ((), ()))


def dft_table(samples):
    phases = np.arange(samples)[:, None] * np.arange(NB)[None, :] % samples
    angles = phases * (2.0 * math.pi / samples)
    table = np.concatenate([np.cos(angles), -np.sin(angles)], axis=1)
    return jnp.asarray(table.astype(np.float32), jnp.bfloat16)


def side_rows(per_device):
    return -(-(MAXLAG + 1) * per_device // 8) * 8


def lag_row(tau, per_device):
    return abs(tau) * per_device + (0 if tau >= 0 else side_rows(per_device))


def lag_table(samples, per_device):
    lag = np.arange(side_rows(per_device)) // per_device
    angles = (lag[:, None] * np.arange(NB)[None, :] % samples) * (2.0 * math.pi / samples)
    table = np.concatenate([np.cos(angles), np.sin(angles)], axis=1)
    return jnp.asarray(table, jnp.float32)


def params(mib):
    return pltpu.CompilerParams(vmem_limit_bytes=mib << 20)


def cost(flops, moved):
    return pl.CostEstimate(flops=flops, bytes_accessed=moved, transcendentals=0)


def whiten(rows, table, weights, share):
    samples = rows.shape[1]
    spectrum = jnp.dot(rows, table, preferred_element_type=jnp.float32) * samples ** (-0.5)
    real, imag = spectrum[:, :NB], spectrum[:, NB:]
    amplitude = jnp.sqrt(real * real + imag * imag)
    high = amplitude.astype(jnp.bfloat16)
    low = (amplitude - high.astype(jnp.float32)).astype(jnp.bfloat16)
    total = jnp.dot(high, weights, preferred_element_type=jnp.float32)
    total += jnp.dot(low, weights, preferred_element_type=jnp.float32)
    gain = 1.0 / jnp.maximum(total * share, FLOOR)
    return (real * gain).astype(jnp.bfloat16), (imag * gain).astype(jnp.bfloat16)


def pick_kernel(layout, traces, mask, phases, *refs):
    windows, subs, per_device, chunks = layout
    count = len(chunks)
    small, halves = refs[:windows], refs[windows:windows + count]
    head, wide, sems = refs[windows + count:]
    block_at, win_at, sub_at = lax.axis_index("chan"), lax.axis_index("win"), lax.axis_index("sub")
    first = pltpu.make_async_copy(traces.at[0, pl.ds(0, VS * STRIDE)], head, sems.at[count])
    first.start()
    copies = []
    for i, (start, size) in enumerate(chunks):
        half = size // subs
        rows = pl.ds(pl.multiple_of(start + sub_at * half, half), half)
        copies.append(pltpu.make_async_copy(traces.at[0, rows], halves[i], sems.at[i]))
        copies[-1].start()
    first.wait()
    wide[...] = head[...].astype(jnp.float32)
    phase = phases[block_at]
    for ahead in range(windows):
        owner = lax.rem(win_at + ahead, windows) * subs + sub_at
        for v in range(per_device):
            row = phase + STRIDE * (owner * per_device + v)
            small[ahead][pl.ds(v, 1), :] = wide[pl.ds(row, 1), :] * mask[row].astype(jnp.float32)
    for copy in copies:
        copy.wait()


def own_kernel(traces, table, widths, out, weights, share):
    reach = widths[...]
    near = lax.broadcasted_iota(jnp.int32, (NB, NB), 0)
    here = lax.broadcasted_iota(jnp.int32, (NB, NB), 1)
    weights[...] = jnp.where(jnp.abs(near - here) <= reach, 1.0, 0.0).astype(jnp.bfloat16)
    bins = lax.broadcasted_iota(jnp.int32, (1, NB), 1)
    count = jnp.minimum(bins + reach, NB - 1) - jnp.maximum(bins - reach, 0) + 1
    share[...] = 1.0 / count.astype(jnp.float32)
    channels = traces.shape[0]
    step = 320 if channels % 320 == 0 else channels

    def body(i, carry):
        rows = pl.ds(pl.multiple_of(i * step, step), step)
        real, imag = whiten(traces[rows, :], table[...], weights[...], share[...])
        out[rows, :NB] = real
        out[rows, NB:] = imag
        return carry

    lax.fori_loop(0, channels // step, body, 0)


def turn_kernel(per_device, windows, table, weights, share, lags, *refs):
    picked, turned, spectra = refs[:-2], refs[-2], refs[-1]
    rows = jnp.concatenate([p[...] for p in picked], axis=0).astype(jnp.bfloat16)
    real, imag = whiten(rows, table[...], weights[...], share[...])
    spectra[:, :NB] = real.astype(jnp.float32)
    spectra[:, NB:] = imag.astype(jnp.float32)
    side = side_rows(per_device)
    span = 2 * side
    which = lax.broadcasted_iota(jnp.int32, (8, LANES), 0) % per_device

    def rows_of(first, lane):
        tiled = jnp.zeros((8, LANES), jnp.float32)
        for v in range(per_device):
            row = spectra[first + v:first + v + 1, lane:lane + LANES]
            tiled = jnp.where(which == v, row, tiled)
        return tiled[None]

    for lane in range(0, NB, LANES):
        cosine = lags[:, lane:lane + LANES].reshape(side // 8, 8, LANES)
        sine = lags[:, NB + lane:NB + lane + LANES].reshape(side // 8, 8, LANES)
        for at in range(len(picked)):
            for behind in range(windows):
                first = (at * windows + behind) * per_device
                real, imag = rows_of(first, lane), rows_of(first, NB + lane)
                cr, si, sr, ci = cosine * real, sine * imag, sine * real, cosine * imag
                up = jnp.concatenate([cr - si, cr + si], axis=0).reshape(span, LANES)
                down = jnp.concatenate([ci + sr, ci - sr], axis=0).reshape(span, LANES)
                spot = pl.ds(at * span, span)
                turned[behind, spot, lane:lane + LANES] = up.astype(jnp.bfloat16)
                turned[behind, spot, NB + lane:NB + lane + LANES] = down.astype(jnp.bfloat16)


def chunk_kernel(layout, factor, table, weights, share, turned, own, mask, *refs):
    count, start, size = layout
    others = turned.shape[0] - 1
    halves, pieces = refs[:2 * others], refs[2 * others:2 * others + count]
    raw, white = refs[2 * others + count:]
    sub_at = lax.axis_index("sub")
    half = size // 2
    total = lax.dot_general(turned[0], own[start:start + size, :], NT, preferred_element_type=jnp.float32)
    for i in range(others):
        raw[pl.ds(pl.multiple_of(sub_at * half, half), half), :] = halves[2 * i][...]
        raw[pl.ds(pl.multiple_of((1 - sub_at) * half, half), half), :] = halves[2 * i + 1][...]
        real, imag = whiten(raw[...], table[...], weights[...], share[...])
        white[:, :NB] = real
        white[:, NB:] = imag
        total += lax.dot_general(turned[1 + i], white[...], NT, preferred_element_type=jnp.float32)
    result = total * (mask[:, start:start + size].astype(jnp.float32) * factor)
    span = result.shape[0] // count
    for at in range(count):
        pieces[at][...] = result[at * span:(at + 1) * span, :].astype(jnp.bfloat16)


def stack_kernel(layout, pairs, *refs):
    moves, blocks, per_device, chunks, reverse, chained = layout
    count = len(moves)
    pieces = refs[:count * len(chunks)]
    out, wide, stage, sems = refs[count * len(chunks) + chained:]
    block_at = lax.axis_index("chan")
    copies = []
    for i, (start, size) in enumerate(chunks):
        lanes = slice(start - chunks[0][0], start - chunks[0][0] + size)
        for at in range(count):
            wide[at, :, lanes] = pieces[i * count + at][...].astype(jnp.float32)
    for e in range(OFFS):
        moved = e - REACH
        at = index_of(moves, moved, blocks)
        block = block_at if reverse else lax.rem(block_at - moved + blocks, blocks)
        pair = pairs[block, e].astype(jnp.float32)
        for t in range(LAGS):
            tau = MAXLAG - t if reverse else t - MAXLAG
            row = lag_row(tau, per_device)
            stage[e, t] = wide[at, row:row + per_device, :] * pair
        lanes = pl.ds(chunks[0][0], stage.shape[3])
        copies.append(pltpu.make_async_copy(stage.at[e], out.at[e, :, :, lanes], sems.at[e]))
        copies[-1].start()
    for copy in copies:
        copy.wait()


def index_of(moves, moved, blocks):
    return [(m - moved) % blocks for m in moves].index(0)


def distinct_moves(blocks):
    moves = []
    for moved in (2, -2, 1, -1, 0):
        if all((m - moved) % blocks for m in moves):
            moves.append(moved)
    return moves


def chunks_of(channels):
    if channels % (5 * LANES):
        return [(0, channels)]
    first = channels * 2 // 5
    return [(0, first), (first, channels - first)]


def shift(block, axis, distance):
    count = lax.axis_size(axis)
    return lax.ppermute(block, axis, [(i, (i + distance) % count) for i in range(count)])


def write_stack(pair_list, pieces, moves, blocks, per_device, channels, chunks, reverse, prior):
    width = sum(size for _, size in chunks)
    span = 2 * side_rows(per_device)
    chained = [] if prior is None else [prior]
    operands = len(pieces) + 1
    return pl.pallas_call(
        functools.partial(
            stack_kernel, (moves, blocks, per_device, chunks, reverse, len(chained))
        ),
        out_shape=jax.ShapeDtypeStruct((OFFS, LAGS, per_device, channels), jnp.float32),
        in_specs=[SMEM] + [VMEM] * len(pieces) + [HBM] * len(chained),
        out_specs=HBM,
        scratch_shapes=[
            pltpu.VMEM((len(moves), span, width), jnp.float32),
            pltpu.VMEM((OFFS, LAGS, per_device, width), jnp.float32),
            pltpu.SemaphoreType.DMA((OFFS,)),
        ],
        input_output_aliases={operands: 0} if chained else {},
        compiler_params=params(16),
        cost_estimate=cost(1 << 20, 8 * span * width * OFFS),
        name="source_order" if reverse else "receiver_order",
    )(pair_list, *pieces, *chained)


def on_device(traces, channel_mask, smooth_width, source_phase, pair_list):
    _, channels, samples = traces.shape
    blocks, windows, subs = (lax.axis_size(a) for a in ("chan", "win", "sub"))
    per_device = VS // (windows * subs)
    moves = distinct_moves(blocks)
    span = 2 * side_rows(per_device)
    chunks = chunks_of(channels)
    table, lags = dft_table(samples), lag_table(samples, per_device)
    factor = (NB * windows) ** (-0.5)
    bf16, f32 = jnp.bfloat16, jnp.float32

    picked = pl.pallas_call(
        functools.partial(pick_kernel, (windows, subs, per_device, chunks)),
        out_shape=tuple(jax.ShapeDtypeStruct((per_device, samples), f32) for _ in range(windows))
        + tuple(jax.ShapeDtypeStruct((size // subs, samples), bf16) for _, size in chunks),
        in_specs=[HBM, SMEM, SMEM],
        out_specs=(VMEM,) * (windows + len(chunks)),
        scratch_shapes=[
            pltpu.VMEM((VS * STRIDE, samples), bf16),
            pltpu.VMEM((VS * STRIDE, samples), f32),
            pltpu.SemaphoreType.DMA((len(chunks) + 1,)),
        ],
        compiler_params=params(56),
        cost_estimate=cost(1 << 16, 2 << 20),
        name="pick_rows",
    )(traces, channel_mask, source_phase)
    small, halves = picked[:windows], picked[windows:]
    near = [small[0]] + [shift(small[d], "win", d) for d in range(1, windows)]
    mine = [[shift(h, "win", d) for d in range(1, windows)] for h in halves]
    near = jnp.concatenate(near, axis=0)
    sources = [near if m % blocks == 0 else shift(near, "chan", m) for m in moves]

    table_flops = 2 * samples * 2 * NB + 4 * NB * NB
    own, weights, share = pl.pallas_call(
        own_kernel,
        out_shape=(
            jax.ShapeDtypeStruct((channels, 2 * NB), bf16),
            jax.ShapeDtypeStruct((NB, NB), bf16),
            jax.ShapeDtypeStruct((1, NB), f32),
        ),
        in_specs=[VMEM, VMEM, VMEM],
        out_specs=(VMEM, VMEM, VMEM),
        compiler_params=params(24),
        cost_estimate=cost(channels * table_flops, 6 << 20),
        name="whiten_own",
    )(traces[0], table, smooth_width.reshape(1, NB))

    turned = pl.pallas_call(
        functools.partial(turn_kernel, per_device, windows),
        out_shape=jax.ShapeDtypeStruct((windows, len(moves) * span, 2 * NB), bf16),
        in_specs=[VMEM] * (4 + len(moves)),
        out_specs=VMEM,
        scratch_shapes=[pltpu.VMEM((len(moves) * windows * per_device, 2 * NB), f32)],
        compiler_params=params(24),
        cost_estimate=cost(len(moves) * span * 2 * NB * 1024, 6 << 20),
        name="turn_sources",
    )(table, weights, share, lags, *sources)

    mask_row = channel_mask.reshape(1, channels)
    results, source_stack = [], None
    arrived = []
    for (start, size), received in zip(chunks, mine):
        both = []
        for piece in received:
            both += [piece, shift(piece, "sub", 1)]
        pieces = pl.pallas_call(
            functools.partial(chunk_kernel, (len(moves), start, size), factor),
            out_shape=tuple(jax.ShapeDtypeStruct((span, size), bf16) for _ in moves),
            in_specs=[VMEM] * (6 + len(both)),
            out_specs=tuple(VMEM for _ in moves),
            scratch_shapes=[
                pltpu.VMEM((size, samples), bf16),
                pltpu.VMEM((size, 2 * NB), bf16),
            ],
            compiler_params=params(32),
            cost_estimate=cost(size * (table_flops + len(moves) * span * 8 * NB), 9 << 20),
            name="lag_pieces",
        )(table, weights, share, turned, own, mask_row, *both)
        results += pieces
        arrived.append([p if m % blocks == 0 else shift(p, "chan", -m) for m, p in zip(moves, pieces)])
    write = functools.partial(write_stack, pair_list)
    shape = (moves, blocks, per_device, channels)
    receiver_stack = write(results, *shape, chunks, False, None)
    for chunk, back in zip(chunks, arrived):
        source_stack = write(back, *shape, [chunk], True, source_stack)
    order = (2, 0, 1, 3)
    return (jnp.transpose(receiver_stack, order), jnp.transpose(source_stack, order))


def solution(mesh):
    in_specs = (
        P(("groups", "win"), "chan", None),
        P(("groups", "chan")),
        P(),
        P("groups"),
        P("groups", None),
    )
    out_specs = (
        P(("win", "sub"), None, None, ("groups", "chan")),
        P(("groups", "chan", "win", "sub"), None, None, None),
    )
    return jax.shard_map(
        on_device, mesh=mesh, in_specs=in_specs, out_specs=out_specs, check_vma=False
    )
```

```python
import functools
import math

import jax
import jax.numpy as jnp
import numpy as np
from jax import lax
from jax.experimental import pallas as pl
from jax.experimental.pallas import tpu as pltpu
from jax.sharding import PartitionSpec as P

NB = 512
MAXLAG = 50
STRIDE = 8
REACH = 2
VS = 8
OFFS = 5
LAGS = 2 * MAXLAG + 1
FLOOR = 0.25
LANES = 128
VMEM = pl.BlockSpec(memory_space=pltpu.VMEM)
SMEM = pl.BlockSpec(memory_space=pltpu.SMEM)
HBM = pl.BlockSpec(memory_space=pltpu.HBM)
NT = (((1,), (1,)), ((), ()))


def dft_table(samples):
    phases = np.arange(samples)[:, None] * np.arange(NB)[None, :] % samples
    angles = phases * (2.0 * math.pi / samples)
    table = np.concatenate([np.cos(angles), -np.sin(angles)], axis=1)
    return jnp.asarray(table.astype(np.float32), jnp.bfloat16)


def side_rows(per_device):
    return -(-(MAXLAG + 1) * per_device // 8) * 8


def lag_row(tau, per_device):
    return abs(tau) * per_device + (0 if tau >= 0 else side_rows(per_device))


def lag_table(samples, per_device):
    lag = np.arange(side_rows(per_device)) // per_device
    angles = (lag[:, None] * np.arange(NB)[None, :] % samples) * (2.0 * math.pi / samples)
    table = np.concatenate([np.cos(angles), np.sin(angles)], axis=1)
    return jnp.asarray(table, jnp.float32)


def params(mib):
    return pltpu.CompilerParams(vmem_limit_bytes=mib << 20)


def cost(flops, moved):
    return pl.CostEstimate(flops=flops, bytes_accessed=moved, transcendentals=0)


SHORT, LONG = cost(1 << 20, 1 << 18), cost(1 << 33, 1 << 26)


def whiten(rows, table, weights, share):
    samples = rows.shape[1]
    spectrum = jnp.dot(rows, table, preferred_element_type=jnp.float32) * samples ** (-0.5)
    real, imag = spectrum[:, :NB], spectrum[:, NB:]
    amplitude = jnp.sqrt(real * real + imag * imag)
    high = amplitude.astype(jnp.bfloat16)
    low = (amplitude - high.astype(jnp.float32)).astype(jnp.bfloat16)
    total = jnp.dot(high, weights, preferred_element_type=jnp.float32)
    total += jnp.dot(low, weights, preferred_element_type=jnp.float32)
    gain = 1.0 / jnp.maximum(total * share, FLOOR)
    return (real * gain).astype(jnp.bfloat16), (imag * gain).astype(jnp.bfloat16)


def near_kernel(layout, phases, mask, *refs):
    windows, subs, per_device = layout
    halves, out = refs[:-1], refs[-1]
    block_at, win_at, sub_at = lax.axis_index("chan"), lax.axis_index("win"), lax.axis_index("sub")
    group = per_device * STRIDE
    rows, width = out.shape[0], halves[0].shape[0]
    phase = phases[block_at]

    def ones_at(first, width):
        row = lax.broadcasted_iota(jnp.int32, (rows, width), 0)
        place = lax.broadcasted_iota(jnp.int32, (rows, width), 1)
        return row, place == first + phase + STRIDE * (row % per_device)

    row, here = ones_at((win_at * subs + sub_at) * group, mask.shape[1])
    alive = jnp.sum(jnp.where(here, mask[...].astype(jnp.float32), 0.0), axis=1, keepdims=True)
    row, here = ones_at(win_at * group, width)
    total = jnp.zeros(out.shape, jnp.float32)
    for behind in range(windows):
        chosen = jnp.where(here & (row // per_device == behind), 1.0, 0.0).astype(jnp.bfloat16)
        total += jnp.dot(chosen, halves[behind][...], preferred_element_type=jnp.float32)
    out[...] = total * alive


def setup_kernel(start, traces, table, widths, out, weights, share):
    reach = widths[...]
    near = lax.broadcasted_iota(jnp.int32, (NB, NB), 0)
    here = lax.broadcasted_iota(jnp.int32, (NB, NB), 1)
    weights[...] = jnp.where(jnp.abs(near - here) <= reach, 1.0, 0.0).astype(jnp.bfloat16)
    bins = lax.broadcasted_iota(jnp.int32, (1, NB), 1)
    count = jnp.minimum(bins + reach, NB - 1) - jnp.maximum(bins - reach, 0) + 1
    share[...] = 1.0 / count.astype(jnp.float32)
    own_kernel(start, traces, table, weights, share, out)


def own_kernel(start, traces, table, weights, share, out):
    rows = traces[start:start + out.shape[0], :]
    real, imag = whiten(rows, table[...], weights[...], share[...])
    out[:, :NB] = real
    out[:, NB:] = imag


def turn_kernel(per_device, windows, table, weights, share, lags, *refs):
    picked, turned, spectra = refs[:-2], refs[-2], refs[-1]
    rows = jnp.concatenate([p[...] for p in picked], axis=0).astype(jnp.bfloat16)
    real, imag = whiten(rows, table[...], weights[...], share[...])
    spectra[:, :NB] = real.astype(jnp.float32)
    spectra[:, NB:] = imag.astype(jnp.float32)
    side = side_rows(per_device)
    span = 2 * side
    which = lax.broadcasted_iota(jnp.int32, (8, LANES), 0) % per_device

    def rows_of(first, lane):
        tiled = jnp.zeros((8, LANES), jnp.float32)
        for v in range(per_device):
            row = spectra[first + v:first + v + 1, lane:lane + LANES]
            tiled = jnp.where(which == v, row, tiled)
        return tiled[None]

    for lane in range(0, NB, LANES):
        cosine = lags[:, lane:lane + LANES].reshape(side // 8, 8, LANES)
        sine = lags[:, NB + lane:NB + lane + LANES].reshape(side // 8, 8, LANES)
        for at in range(len(picked)):
            for behind in range(windows):
                first = at * picked[0].shape[0] + behind * per_device
                real, imag = rows_of(first, lane), rows_of(first, NB + lane)
                cr, si, sr, ci = cosine * real, sine * imag, sine * real, cosine * imag
                up = jnp.concatenate([cr - si, cr + si], axis=0).reshape(span, LANES)
                down = jnp.concatenate([ci + sr, ci - sr], axis=0).reshape(span, LANES)
                spot = pl.ds(at * span, span)
                turned[behind, spot, lane:lane + LANES] = up.astype(jnp.bfloat16)
                turned[behind, spot, NB + lane:NB + lane + LANES] = down.astype(jnp.bfloat16)


def chunk_kernel(count, factor, table, weights, share, turned, own, mask, *refs):
    others = turned.shape[0] - 1
    halves, pieces = refs[:2 * others], refs[2 * others:2 * others + count]
    raw, white = refs[2 * others + count:]
    sub_at = lax.axis_index("sub")
    groups, _, group, samples = raw.shape
    total = lax.dot_general(turned[0], own[...], NT, preferred_element_type=jnp.float32)
    for i in range(others):
        for half, place in ((halves[2 * i], sub_at), (halves[2 * i + 1], 1 - sub_at)):
            raw[:, pl.ds(place, 1)] = half[...].reshape(groups, 1, group, samples)
        rows = raw[...].reshape(white.shape[0], samples)
        real, imag = whiten(rows, table[...], weights[...], share[...])
        white[:, :NB] = real
        white[:, NB:] = imag
        total += lax.dot_general(turned[1 + i], white[...], NT, preferred_element_type=jnp.float32)
    result = total * (mask[...].astype(jnp.float32) * factor)
    span = result.shape[0] // count
    for at in range(count):
        pieces[at][...] = result[at * span:(at + 1) * span, :].astype(jnp.bfloat16)


def stack_kernel(layout, pairs, *refs):
    moves, blocks, per_device, chunks, reverse, chained = layout
    count = len(moves)
    pieces = refs[:count * len(chunks)]
    out, wide, stage, sems = refs[count * len(chunks) + chained:]
    block_at = lax.axis_index("chan")
    copies = []
    for i, (start, size) in enumerate(chunks):
        lanes = slice(start - chunks[0][0], start - chunks[0][0] + size)
        for at in range(count):
            wide[at, :, lanes] = pieces[i * count + at][...].astype(jnp.float32)
    for e in range(OFFS):
        moved = e - REACH
        at = index_of(moves, moved, blocks)
        block = block_at if reverse else lax.rem(block_at - moved + blocks, blocks)
        pair = pairs[block, e].astype(jnp.float32)
        for t in range(LAGS):
            tau = MAXLAG - t if reverse else t - MAXLAG
            row = lag_row(tau, per_device)
            stage[e, t] = wide[at, row:row + per_device, :] * pair
        lanes = pl.ds(chunks[0][0], stage.shape[3])
        copies.append(pltpu.make_async_copy(stage.at[e], out.at[e, :, :, lanes], sems.at[e]))
        copies[-1].start()
    for copy in copies:
        copy.wait()


def index_of(moves, moved, blocks):
    return [(m - moved) % blocks for m in moves].index(0)


def distinct_moves(blocks):
    moves = []
    for moved in (2, -2, 1, -1, 0):
        if all((m - moved) % blocks for m in moves):
            moves.append(moved)
    return moves


def chunks_of(channels):
    if channels % (5 * LANES):
        return [(0, channels)]
    first = channels * 2 // 5
    return [(0, first), (first, channels - first)]


def shift(block, axis, distance):
    count = lax.axis_size(axis)
    return lax.ppermute(block, axis, [(i, (i + distance) % count) for i in range(count)])


def write_stack(pair_list, pieces, moves, blocks, per_device, channels, chunks, reverse, prior):
    width = sum(size for _, size in chunks)
    span = 2 * side_rows(per_device)
    chained = [] if prior is None else [prior]
    operands = len(pieces) + 1
    return pl.pallas_call(
        functools.partial(
            stack_kernel, (moves, blocks, per_device, chunks, reverse, len(chained))
        ),
        out_shape=jax.ShapeDtypeStruct((OFFS, LAGS, per_device, channels), jnp.float32),
        in_specs=[SMEM] + [VMEM] * len(pieces) + [HBM] * len(chained),
        out_specs=HBM,
        scratch_shapes=[
            pltpu.VMEM((len(moves), span, width), jnp.float32),
            pltpu.VMEM((OFFS, LAGS, per_device, width), jnp.float32),
            pltpu.SemaphoreType.DMA((OFFS,)),
        ],
        input_output_aliases={operands: 0} if chained else {},
        compiler_params=params(16),
        cost_estimate=LONG,
        name="source_order" if reverse else "receiver_order",
    )(pair_list, *pieces, *chained)


def after(value, *others):
    return lax.optimization_barrier((value, *others))[0]


def on_device(traces, channel_mask, smooth_width, source_phase, pair_list):
    _, channels, samples = traces.shape
    blocks, windows, subs = (lax.axis_size(a) for a in ("chan", "win", "sub"))
    sub_at = lax.axis_index("sub")
    per_device = VS // (windows * subs)
    group = per_device * STRIDE
    moves = distinct_moves(blocks)
    span = 2 * side_rows(per_device)
    chunks = chunks_of(channels)
    table, lags = dft_table(samples), lag_table(samples, per_device)
    factor = (NB * windows) ** (-0.5)
    bf16, f32 = jnp.bfloat16, jnp.float32
    like = jax.ShapeDtypeStruct
    mask_row = channel_mask.reshape(1, channels)

    def half_of(rows):
        grouped = rows.reshape(rows.shape[0] // (subs * group), subs, group, samples)
        half = lax.dynamic_index_in_dim(grouped, sub_at, axis=1, keepdims=False)
        return half.reshape(rows.shape[0] // subs, samples)

    def from_windows(half):
        return [shift(half, "win", d) for d in range(1, windows)]

    def correlate(start, size, own, received, hint):
        both = []
        for piece in received:
            both += [piece, shift(piece, "sub", 1)]
        return pl.pallas_call(
            functools.partial(chunk_kernel, len(moves), factor),
            out_shape=tuple(like((span, size), bf16) for _ in moves),
            in_specs=[VMEM] * (6 + len(both)),
            out_specs=tuple(VMEM for _ in moves),
            scratch_shapes=[
                pltpu.VMEM((size // (subs * group), subs, group, samples), bf16),
                pltpu.VMEM((size, 2 * NB), bf16),
            ],
            compiler_params=params(32),
            cost_estimate=hint,
            name="lag_pieces",
        )(table, weights, share, turned, own, mask_row[:, start:start + size], *both)

    (start, size), *later = chunks
    half = half_of(traces[0, start:start + size])
    received = from_windows(half)
    own, weights, share = pl.pallas_call(
        functools.partial(setup_kernel, start),
        out_shape=(like((size, 2 * NB), bf16), like((NB, NB), bf16), like((1, NB), f32)),
        in_specs=[VMEM, VMEM, VMEM],
        out_specs=(VMEM, VMEM, VMEM),
        compiler_params=params(24),
        cost_estimate=SHORT,
        name="whiten_own",
    )(traces[0], table, smooth_width.reshape(1, NB))

    later_halves = [half_of(after(traces, own)[0, a:a + n]) for a, n in later]
    later_received = [from_windows(h) for h in later_halves]
    near = pl.pallas_call(
        functools.partial(near_kernel, (windows, subs, per_device)),
        out_shape=like((-(-windows * per_device // 8) * 8, samples), f32),
        in_specs=[SMEM] + [VMEM] * (1 + windows),
        out_specs=VMEM,
        compiler_params=params(16),
        cost_estimate=SHORT,
        name="pick_sources",
    )(source_phase, after(mask_row, own), half, *received)
    sources = [near if m % blocks == 0 else shift(near, "chan", m) for m in moves]
    turned = pl.pallas_call(
        functools.partial(turn_kernel, per_device, windows),
        out_shape=like((windows, len(moves) * span, 2 * NB), bf16),
        in_specs=[VMEM] * (4 + len(moves)),
        out_specs=VMEM,
        scratch_shapes=[pltpu.VMEM((len(moves) * near.shape[0], 2 * NB), f32)],
        compiler_params=params(24),
        cost_estimate=SHORT,
        name="turn_sources",
    )(table, weights, share, lags, *sources)
    if later:
        flat = lax.optimization_barrier((own, later_received))
        own, later_received = flat
    pieces = [correlate(start, size, own, received, SHORT)]
    for (start, size), received in zip(later, later_received):
        received = [after(r, pieces[-1]) for r in received]
        own = pl.pallas_call(
            functools.partial(own_kernel, start),
            out_shape=like((size, 2 * NB), bf16),
            in_specs=[VMEM] * 4,
            out_specs=VMEM,
            compiler_params=params(24),
            cost_estimate=LONG,
            name="whiten_own",
        )(after(traces, pieces[-1])[0], table, weights, share)
        pieces.append(correlate(start, size, own, received, LONG))

    write = functools.partial(write_stack, pair_list)
    shape = (moves, blocks, per_device, channels)
    everything = [piece for group in pieces for piece in group]
    receiver_stack = write(everything, *shape, chunks, False, None)
    source_stack = None
    for chunk, group in zip(chunks, pieces):
        back = [p if m % blocks == 0 else shift(p, "chan", -m) for m, p in zip(moves, group)]
        if group is not pieces[-1]:
            back = [after(p, *pieces[-1]) for p in back]
        source_stack = write(back, *shape, [chunk], True, source_stack)
    order = (2, 0, 1, 3)
    return (jnp.transpose(receiver_stack, order), jnp.transpose(source_stack, order))


def solution(mesh):
    in_specs = (
        P(("groups", "win"), "chan", None),
        P(("groups", "chan")),
        P(),
        P("groups"),
        P("groups", None),
    )
    out_specs = (
        P(("win", "sub"), None, None, ("groups", "chan")),
        P(("groups", "chan", "win", "sub"), None, None, None),
    )
    return jax.shard_map(
        on_device, mesh=mesh, in_specs=in_specs, out_specs=out_specs, check_vma=False
    )
```

```python
import functools
import math

import jax
import jax.numpy as jnp
import numpy as np
from jax import lax
from jax.experimental import pallas as pl
from jax.experimental.pallas import tpu as pltpu
from jax.sharding import PartitionSpec as P

NB = 512
MAXLAG = 50
STRIDE = 8
REACH = 2
VS = 8
OFFS = 5
LAGS = 2 * MAXLAG + 1
FLOOR = 0.25
TABLE_PARTS = 4
LANES = 128
VMEM = pl.BlockSpec(memory_space=pltpu.VMEM)
SMEM = pl.BlockSpec(memory_space=pltpu.SMEM)
HBM = pl.BlockSpec(memory_space=pltpu.HBM)
NT = (((1,), (1,)), ((), ()))


def dft_table(samples):
    phases = np.arange(samples)[:, None] * np.arange(NB)[None, :] % samples
    angles = phases * (2.0 * math.pi / samples)
    table = np.concatenate([np.cos(angles), -np.sin(angles)], axis=1)
    return jnp.asarray(table.astype(np.float32), jnp.bfloat16)


def side_rows(per_device):
    return -(-(MAXLAG + 1) * per_device // 8) * 8


def lag_row(tau, per_device):
    return abs(tau) * per_device + (0 if tau >= 0 else side_rows(per_device))


def lag_table(samples, per_device):
    lag = np.arange(side_rows(per_device)) // per_device
    angles = (lag[:, None] * np.arange(NB)[None, :] % samples) * (2.0 * math.pi / samples)
    table = np.concatenate([np.cos(angles), np.sin(angles)], axis=1)
    return jnp.asarray(table, jnp.float32)


def params(mib):
    return pltpu.CompilerParams(vmem_limit_bytes=mib << 20)


def cost(flops, moved):
    return pl.CostEstimate(flops=flops, bytes_accessed=moved, transcendentals=0)


SHORT, LONG = cost(1 << 20, 1 << 18), cost(1 << 33, 1 << 26)


def whiten(rows, table, weights, share):
    samples = rows.shape[1]
    spectrum = jnp.dot(rows, table, preferred_element_type=jnp.float32) * samples ** (-0.5)
    real, imag = spectrum[:, :NB], spectrum[:, NB:]
    amplitude = jnp.sqrt(real * real + imag * imag)
    high = amplitude.astype(jnp.bfloat16)
    low = (amplitude - high.astype(jnp.float32)).astype(jnp.bfloat16)
    total = jnp.dot(high, weights, preferred_element_type=jnp.float32)
    total += jnp.dot(low, weights, preferred_element_type=jnp.float32)
    gain = 1.0 / jnp.maximum(total * share, FLOOR)
    return (real * gain).astype(jnp.bfloat16), (imag * gain).astype(jnp.bfloat16)


def near_kernel(layout, phases, mask, *refs):
    windows, subs, per_device = layout
    halves, out = refs[:-1], refs[-1]
    block_at, win_at, sub_at = lax.axis_index("chan"), lax.axis_index("win"), lax.axis_index("sub")
    group = per_device * STRIDE
    rows, width = out.shape[0], halves[0].shape[0]
    phase = phases[block_at]

    def ones_at(first, width):
        row = lax.broadcasted_iota(jnp.int32, (rows, width), 0)
        place = lax.broadcasted_iota(jnp.int32, (rows, width), 1)
        return row, place == first + phase + STRIDE * (row % per_device)

    row, here = ones_at((win_at * subs + sub_at) * group, mask.shape[1])
    alive = jnp.sum(jnp.where(here, mask[...].astype(jnp.float32), 0.0), axis=1, keepdims=True)
    row, here = ones_at(win_at * group, width)
    total = jnp.zeros(out.shape, jnp.float32)
    for behind in range(windows):
        chosen = jnp.where(here & (row // per_device == behind), 1.0, 0.0).astype(jnp.bfloat16)
        total += jnp.dot(chosen, halves[behind][...], preferred_element_type=jnp.float32)
    out[...] = total * alive


def setup_kernel(chunks, traces, table, widths, *refs):
    owns, (weights, share, rows_kept, table_kept, sems) = refs[:len(chunks)], refs[len(chunks):]
    depth = table.shape[0] // TABLE_PARTS
    needed = chunks[-1][0] + chunks[-1][1]
    rest = rows_kept.shape[0] - needed
    first_rows = pltpu.make_async_copy(traces.at[0, pl.ds(0, needed)], rows_kept.at[pl.ds(0, needed)], sems.at[TABLE_PARTS])
    first_rows.start()
    parts = []
    for i in range(TABLE_PARTS):
        span = pl.ds(i * depth, depth)
        parts.append(pltpu.make_async_copy(table.at[span], table_kept.at[span], sems.at[i]))
        parts[-1].start()
    if rest:
        span = pl.ds(needed, rest)
        last_rows = pltpu.make_async_copy(traces.at[0, span], rows_kept.at[span], sems.at[TABLE_PARTS + 1])
        last_rows.start()
    reach = widths[...]
    near = lax.broadcasted_iota(jnp.int32, (NB, NB), 0)
    here = lax.broadcasted_iota(jnp.int32, (NB, NB), 1)
    weights[...] = jnp.where(jnp.abs(near - here) <= reach, 1.0, 0.0).astype(jnp.bfloat16)
    bins = lax.broadcasted_iota(jnp.int32, (1, NB), 1)
    count = jnp.minimum(bins + reach, NB - 1) - jnp.maximum(bins - reach, 0) + 1
    share[...] = 1.0 / count.astype(jnp.float32)
    first_rows.wait()
    for part in parts:
        part.wait()
    for (start, size), own in zip(chunks, owns):
        own_kernel(start, rows_kept, table_kept, weights, share, own)
    if rest:
        last_rows.wait()


def own_kernel(start, rows, table, weights, share, out):
    real, imag = whiten(rows[start:start + out.shape[0], :], table[...], weights[...], share[...])
    out[:, :NB] = real
    out[:, NB:] = imag


def turn_kernel(per_device, windows, table, weights, share, lags, *refs):
    picked, turned, spectra = refs[:-2], refs[-2], refs[-1]
    rows = jnp.concatenate([p[...] for p in picked], axis=0).astype(jnp.bfloat16)
    real, imag = whiten(rows, table[...], weights[...], share[...])
    spectra[:, :NB] = real.astype(jnp.float32)
    spectra[:, NB:] = imag.astype(jnp.float32)
    side = side_rows(per_device)
    span = 2 * side
    which = lax.broadcasted_iota(jnp.int32, (8, LANES), 0) % per_device

    def rows_of(first, lane):
        tiled = jnp.zeros((8, LANES), jnp.float32)
        for v in range(per_device):
            row = spectra[first + v:first + v + 1, lane:lane + LANES]
            tiled = jnp.where(which == v, row, tiled)
        return tiled[None]

    for lane in range(0, NB, LANES):
        cosine = lags[:, lane:lane + LANES].reshape(side // 8, 8, LANES)
        sine = lags[:, NB + lane:NB + lane + LANES].reshape(side // 8, 8, LANES)
        for at in range(len(picked)):
            for behind in range(windows):
                first = at * picked[0].shape[0] + behind * per_device
                real, imag = rows_of(first, lane), rows_of(first, NB + lane)
                cr, si, sr, ci = cosine * real, sine * imag, sine * real, cosine * imag
                up = jnp.concatenate([cr - si, cr + si], axis=0).reshape(span, LANES)
                down = jnp.concatenate([ci + sr, ci - sr], axis=0).reshape(span, LANES)
                spot = pl.ds(at * span, span)
                turned[behind, spot, lane:lane + LANES] = up.astype(jnp.bfloat16)
                turned[behind, spot, NB + lane:NB + lane + LANES] = down.astype(jnp.bfloat16)


def chunk_kernel(count, factor, table, weights, share, turned, own, mask, *refs):
    others = turned.shape[0] - 1
    halves, pieces = refs[:2 * others], refs[2 * others:2 * others + count]
    raw, white = refs[2 * others + count:]
    sub_at = lax.axis_index("sub")
    groups, _, group, samples = raw.shape
    total = lax.dot_general(turned[0], own[...], NT, preferred_element_type=jnp.float32)
    for i in range(others):
        for half, place in ((halves[2 * i], sub_at), (halves[2 * i + 1], 1 - sub_at)):
            raw[:, pl.ds(place, 1)] = half[...].reshape(groups, 1, group, samples)
        rows = raw[...].reshape(white.shape[0], samples)
        real, imag = whiten(rows, table[...], weights[...], share[...])
        white[:, :NB] = real
        white[:, NB:] = imag
        total += lax.dot_general(turned[1 + i], white[...], NT, preferred_element_type=jnp.float32)
    result = total * (mask[...].astype(jnp.float32) * factor)
    span = result.shape[0] // count
    for at in range(count):
        pieces[at][...] = result[at * span:(at + 1) * span, :].astype(jnp.bfloat16)


def stack_kernel(layout, pairs, *refs):
    moves, blocks, per_device, chunks, reverse, chained = layout
    count = len(moves)
    pieces = refs[:count * len(chunks)]
    out, wide, stage, sems = refs[count * len(chunks) + chained:]
    block_at = lax.axis_index("chan")
    copies = []
    for i, (start, size) in enumerate(chunks):
        lanes = slice(start - chunks[0][0], start - chunks[0][0] + size)
        for at in range(count):
            wide[at, :, lanes] = pieces[i * count + at][...].astype(jnp.float32)
    for e in range(OFFS):
        moved = e - REACH
        at = index_of(moves, moved, blocks)
        block = block_at if reverse else lax.rem(block_at - moved + blocks, blocks)
        pair = pairs[block, e].astype(jnp.float32)
        for t in range(LAGS):
            tau = MAXLAG - t if reverse else t - MAXLAG
            row = lag_row(tau, per_device)
            stage[e, t] = wide[at, row:row + per_device, :] * pair
        lanes = pl.ds(chunks[0][0], stage.shape[3])
        copies.append(pltpu.make_async_copy(stage.at[e], out.at[e, :, :, lanes], sems.at[e]))
        copies[-1].start()
    for copy in copies:
        copy.wait()


def index_of(moves, moved, blocks):
    return [(m - moved) % blocks for m in moves].index(0)


def distinct_moves(blocks):
    moves = []
    for moved in (2, -2, 1, -1, 0):
        if all((m - moved) % blocks for m in moves):
            moves.append(moved)
    return moves


def chunks_of(channels):
    if channels < 3 * LANES or channels % LANES:
        return [(0, channels)]
    middle = (channels - LANES) // (2 * LANES) * LANES
    return [(0, LANES), (LANES, middle), (LANES + middle, channels - LANES - middle)]


def shift(block, axis, distance):
    count = lax.axis_size(axis)
    return lax.ppermute(block, axis, [(i, (i + distance) % count) for i in range(count)])


def write_stack(pair_list, pieces, moves, blocks, per_device, channels, chunks, reverse, prior):
    width = sum(size for _, size in chunks)
    span = 2 * side_rows(per_device)
    chained = [] if prior is None else [prior]
    operands = len(pieces) + 1
    return pl.pallas_call(
        functools.partial(
            stack_kernel, (moves, blocks, per_device, chunks, reverse, len(chained))
        ),
        out_shape=jax.ShapeDtypeStruct((OFFS, LAGS, per_device, channels), jnp.float32),
        in_specs=[SMEM] + [VMEM] * len(pieces) + [HBM] * len(chained),
        out_specs=HBM,
        scratch_shapes=[
            pltpu.VMEM((len(moves), span, width), jnp.float32),
            pltpu.VMEM((OFFS, LAGS, per_device, width), jnp.float32),
            pltpu.SemaphoreType.DMA((OFFS,)),
        ],
        input_output_aliases={operands: 0} if chained else {},
        compiler_params=params(16),
        cost_estimate=LONG,
        name="source_order" if reverse else "receiver_order",
    )(pair_list, *pieces, *chained)


def in_hbm(value):
    return pltpu.with_memory_space_constraint(value, pltpu.HBM)


def after(value, *others):
    return lax.optimization_barrier((value, *others))[0]


def on_device(traces, channel_mask, smooth_width, source_phase, pair_list):
    _, channels, samples = traces.shape
    blocks, windows, subs = (lax.axis_size(a) for a in ("chan", "win", "sub"))
    sub_at = lax.axis_index("sub")
    per_device = VS // (windows * subs)
    group = per_device * STRIDE
    moves = distinct_moves(blocks)
    span = 2 * side_rows(per_device)
    chunks = chunks_of(channels)
    table, lags = dft_table(samples), lag_table(samples, per_device)
    factor = (NB * windows) ** (-0.5)
    bf16, f32 = jnp.bfloat16, jnp.float32
    like = jax.ShapeDtypeStruct
    mask_row = channel_mask.reshape(1, channels)

    def half_of(rows, start, size):
        grouped = rows.reshape(channels // (subs * group), subs, group, samples)
        first, count = start // (subs * group), size // (subs * group)
        half = lax.dynamic_slice(grouped, (first, sub_at, 0, 0), (count, 1, group, samples))
        return half.reshape(size // subs, samples)

    def from_windows(half):
        return [shift(half, "win", d) for d in range(1, windows)]

    def with_other_core(received):
        return [side for piece in received for side in (piece, shift(piece, "sub", 1))]

    def correlate(start, size, own, both, hint):
        return pl.pallas_call(
            functools.partial(chunk_kernel, len(moves), factor),
            out_shape=tuple(like((span, size), bf16) for _ in moves),
            in_specs=[VMEM] * (6 + len(both)),
            out_specs=tuple(VMEM for _ in moves),
            scratch_shapes=[
                pltpu.VMEM((size // (subs * group), subs, group, samples), bf16),
                pltpu.VMEM((size, 2 * NB), bf16),
            ],
            compiler_params=params(32),
            cost_estimate=hint,
            name="lag_pieces",
        )(table, weights, share, turned, own, mask_row[:, start:start + size], *both)

    half = half_of(traces, *chunks[0])
    received = [from_windows(half)]
    *owns, weights, share, rows, table = pl.pallas_call(
        functools.partial(setup_kernel, chunks),
        out_shape=tuple(like((size, 2 * NB), bf16) for _, size in chunks)
        + (like((NB, NB), bf16), like((1, NB), f32))
        + (like((channels, samples), bf16), like(table.shape, bf16)),
        in_specs=[HBM, HBM, VMEM],
        out_specs=(VMEM,) * (len(chunks) + 4),
        scratch_shapes=[pltpu.SemaphoreType.DMA((TABLE_PARTS + 2,))],
        compiler_params=params(24),
        cost_estimate=SHORT,
        name="whiten_own",
    )(in_hbm(traces), in_hbm(table), after(smooth_width, half).reshape(1, NB))
    if len(chunks) > 1:
        received.append(from_windows(half_of(after(rows, *received[0]), *chunks[1])))
    near = pl.pallas_call(
        functools.partial(near_kernel, (windows, subs, per_device)),
        out_shape=like((-(-windows * per_device // 8) * 8, samples), f32),
        in_specs=[SMEM] + [VMEM] * (1 + windows),
        out_specs=VMEM,
        compiler_params=params(16),
        cost_estimate=SHORT,
        name="pick_sources",
    )(source_phase, after(mask_row, weights), half, *received[0])
    received += [from_windows(half_of(after(rows, near), *chunk)) for chunk in chunks[2:]]
    inbound = with_other_core([after(r, near) for r in received[0]])
    sources = [near if m % blocks == 0 else shift(near, "chan", m) for m in moves]
    turned = pl.pallas_call(
        functools.partial(turn_kernel, per_device, windows),
        out_shape=like((windows, len(moves) * span, 2 * NB), bf16),
        in_specs=[VMEM] * (4 + len(moves)),
        out_specs=VMEM,
        scratch_shapes=[pltpu.VMEM((len(moves) * near.shape[0], 2 * NB), f32)],
        compiler_params=params(24),
        cost_estimate=SHORT,
        name="turn_sources",
    )(table, weights, after(share, *inbound), lags, *sources)
    received[1:2] = [[after(r, turned) for r in chunk] for chunk in received[1:2]]
    pieces, arrived = [], []
    for i, (start, size) in enumerate(chunks):
        own = owns[i]
        if i:
            inbound = with_other_core(received[i])
        if pieces:
            own = after(own, *pieces[-1])
        pieces.append(correlate(start, size, own, inbound, LONG if pieces else SHORT))
        ahead = [b for b, m in zip(arrived[-1], moves) if m % blocks] if arrived else []
        ahead = ahead if i < 2 else ahead[:1]
        arrived.append(
            [
                p if m % blocks == 0 else shift(after(p, *ahead), "chan", -m)
                for m, p in zip(moves, pieces[-1])
            ]
        )

    write = functools.partial(write_stack, pair_list)
    shape = (moves, blocks, per_device, channels)
    everything = [piece for group in pieces for piece in group]
    receiver_stack = write(everything, *shape, chunks, False, None)
    source_stack = None
    for i, (chunk, back) in enumerate(zip(chunks, arrived)):
        if i + 1 < len(chunks):
            back = [after(b, *pieces[i + 1]) for b in back]
        source_stack = write(back, *shape, [chunk], True, source_stack)
    order = (2, 0, 1, 3)
    return (jnp.transpose(receiver_stack, order), jnp.transpose(source_stack, order))


def solution(mesh):
    in_specs = (
        P(("groups", "win"), "chan", None),
        P(("groups", "chan")),
        P(),
        P("groups"),
        P("groups", None),
    )
    out_specs = (
        P(("win", "sub"), None, None, ("groups", "chan")),
        P(("groups", "chan", "win", "sub"), None, None, None),
    )
    return jax.shard_map(
        on_device, mesh=mesh, in_specs=in_specs, out_specs=out_specs, check_vma=False
    )
```

```python
import functools
import math

import jax
import jax.numpy as jnp
import numpy as np
from jax import lax
from jax.experimental import pallas as pl
from jax.experimental.pallas import tpu as pltpu
from jax.sharding import PartitionSpec as P

NB = 512
MAXLAG = 50
STRIDE = 8
REACH = 2
VS = 8
OFFS = 5
LAGS = 2 * MAXLAG + 1
FLOOR = 0.25
TABLE_PARTS = 4
LANES = 128
VMEM = pl.BlockSpec(memory_space=pltpu.VMEM)
SMEM = pl.BlockSpec(memory_space=pltpu.SMEM)
HBM = pl.BlockSpec(memory_space=pltpu.HBM)
NT = (((1,), (1,)), ((), ()))


def dft_table(samples):
    phases = np.arange(samples)[:, None] * np.arange(NB)[None, :] % samples
    angles = phases * (2.0 * math.pi / samples)
    table = np.concatenate([np.cos(angles), -np.sin(angles)], axis=1)
    return jnp.asarray(table.astype(np.float32), jnp.bfloat16)


def side_rows(per_device):
    return -(-(MAXLAG + 1) * per_device // 8) * 8


def lag_row(tau, per_device):
    return abs(tau) * per_device + (0 if tau >= 0 else side_rows(per_device))


def lag_table(samples, per_device):
    lag = np.arange(side_rows(per_device)) // per_device
    angles = (lag[:, None] * np.arange(NB)[None, :] % samples) * (2.0 * math.pi / samples)
    table = np.concatenate([np.cos(angles), np.sin(angles)], axis=1)
    return jnp.asarray(table, jnp.float32)


def params(mib):
    return pltpu.CompilerParams(vmem_limit_bytes=mib << 20)


def cost(flops, moved):
    return pl.CostEstimate(flops=flops, bytes_accessed=moved, transcendentals=0)


SHORT, LONG = cost(1 << 20, 1 << 18), cost(1 << 33, 1 << 26)


def whiten(rows, table, weights, share):
    samples = rows.shape[1]
    spectrum = jnp.dot(rows, table, preferred_element_type=jnp.float32) * samples ** (-0.5)
    real, imag = spectrum[:, :NB], spectrum[:, NB:]
    amplitude = jnp.sqrt(real * real + imag * imag)
    high = amplitude.astype(jnp.bfloat16)
    low = (amplitude - high.astype(jnp.float32)).astype(jnp.bfloat16)
    total = jnp.dot(high, weights, preferred_element_type=jnp.float32)
    total += jnp.dot(low, weights, preferred_element_type=jnp.float32)
    gain = 1.0 / jnp.maximum(total * share, FLOOR)
    return (real * gain).astype(jnp.bfloat16), (imag * gain).astype(jnp.bfloat16)


def near_kernel(layout, phases, mask, *refs):
    windows, subs, per_device = layout
    halves, out = refs[:-1], refs[-1]
    block_at, win_at, sub_at = lax.axis_index("chan"), lax.axis_index("win"), lax.axis_index("sub")
    group = per_device * STRIDE
    rows, width = out.shape[1], halves[0].shape[0]
    phase = phases[block_at]

    def ones_at(first, width):
        row = lax.broadcasted_iota(jnp.int32, (rows, width), 0)
        place = lax.broadcasted_iota(jnp.int32, (rows, width), 1)
        return row, place == first + phase + STRIDE * (row % per_device)

    row, here = ones_at((win_at * subs + sub_at) * group, mask.shape[1])
    alive = jnp.sum(jnp.where(here, mask[...].astype(jnp.float32), 0.0), axis=1, keepdims=True)
    row, here = ones_at(win_at * group, width)
    total = jnp.zeros(out.shape[1:], jnp.float32)
    for behind in range(windows):
        chosen = jnp.where(here & (row // per_device == behind), 1.0, 0.0).astype(jnp.bfloat16)
        total += jnp.dot(chosen, halves[behind][...], preferred_element_type=jnp.float32)
    for copy in range(out.shape[0]):
        out[copy] = total * alive


def setup_kernel(chunks, traces, table, widths, *refs):
    owns, (weights, share, rows_kept, table_kept, sems) = refs[:len(chunks)], refs[len(chunks):]
    depth = table.shape[0] // TABLE_PARTS
    needed = chunks[-1][0] + chunks[-1][1]
    rest = rows_kept.shape[0] - needed
    first_rows = pltpu.make_async_copy(traces.at[0, pl.ds(0, needed)], rows_kept.at[pl.ds(0, needed)], sems.at[TABLE_PARTS])
    first_rows.start()
    parts = []
    for i in range(TABLE_PARTS):
        span = pl.ds(i * depth, depth)
        parts.append(pltpu.make_async_copy(table.at[span], table_kept.at[span], sems.at[i]))
        parts[-1].start()
    if rest:
        span = pl.ds(needed, rest)
        last_rows = pltpu.make_async_copy(traces.at[0, span], rows_kept.at[span], sems.at[TABLE_PARTS + 1])
        last_rows.start()
    reach = widths[...]
    near = lax.broadcasted_iota(jnp.int32, (NB, NB), 0)
    here = lax.broadcasted_iota(jnp.int32, (NB, NB), 1)
    weights[...] = jnp.where(jnp.abs(near - here) <= reach, 1.0, 0.0).astype(jnp.bfloat16)
    bins = lax.broadcasted_iota(jnp.int32, (1, NB), 1)
    count = jnp.minimum(bins + reach, NB - 1) - jnp.maximum(bins - reach, 0) + 1
    share[...] = 1.0 / count.astype(jnp.float32)
    first_rows.wait()
    for part in parts:
        part.wait()
    for (start, size), own in zip(chunks, owns):
        own_kernel(start, rows_kept, table_kept, weights, share, own)
    if rest:
        last_rows.wait()


def own_kernel(start, rows, table, weights, share, out):
    real, imag = whiten(rows[start:start + out.shape[0], :], table[...], weights[...], share[...])
    out[:, :NB] = real
    out[:, NB:] = imag


def turn_kernel(per_device, windows, table, weights, share, lags, picked, turned, spectra):
    count, each, samples = picked.shape
    rows = picked[...].reshape(count * each, samples).astype(jnp.bfloat16)
    real, imag = whiten(rows, table[...], weights[...], share[...])
    spectra[:, :NB] = real.astype(jnp.float32)
    spectra[:, NB:] = imag.astype(jnp.float32)
    side = side_rows(per_device)
    span = 2 * side
    which = lax.broadcasted_iota(jnp.int32, (8, LANES), 0) % per_device

    def rows_of(first, lane):
        tiled = jnp.zeros((8, LANES), jnp.float32)
        for v in range(per_device):
            row = spectra[first + v:first + v + 1, lane:lane + LANES]
            tiled = jnp.where(which == v, row, tiled)
        return tiled[None]

    for lane in range(0, NB, LANES):
        cosine = lags[:, lane:lane + LANES].reshape(side // 8, 8, LANES)
        sine = lags[:, NB + lane:NB + lane + LANES].reshape(side // 8, 8, LANES)
        for at in range(count):
            for behind in range(windows):
                first = at * each + behind * per_device
                real, imag = rows_of(first, lane), rows_of(first, NB + lane)
                cr, si, sr, ci = cosine * real, sine * imag, sine * real, cosine * imag
                up = jnp.concatenate([cr - si, cr + si], axis=0).reshape(span, LANES)
                down = jnp.concatenate([ci + sr, ci - sr], axis=0).reshape(span, LANES)
                spot = pl.ds(at * span, span)
                turned[behind, spot, lane:lane + LANES] = up.astype(jnp.bfloat16)
                turned[behind, spot, NB + lane:NB + lane + LANES] = down.astype(jnp.bfloat16)


def chunk_kernel(factor, table, weights, share, turned, own, mask, *refs):
    others = turned.shape[0] - 1
    halves, (pieces, raw, white) = refs[:2 * others], refs[2 * others:]
    sub_at = lax.axis_index("sub")
    groups, _, group, samples = raw.shape
    total = lax.dot_general(turned[0], own[...], NT, preferred_element_type=jnp.float32)
    for i in range(others):
        for half, place in ((halves[2 * i], sub_at), (halves[2 * i + 1], 1 - sub_at)):
            raw[:, pl.ds(place, 1)] = half[...].reshape(groups, 1, group, samples)
        rows = raw[...].reshape(white.shape[0], samples)
        real, imag = whiten(rows, table[...], weights[...], share[...])
        white[:, :NB] = real
        white[:, NB:] = imag
        total += lax.dot_general(turned[1 + i], white[...], NT, preferred_element_type=jnp.float32)
    result = total * (mask[...].astype(jnp.float32) * factor)
    pieces[...] = result.reshape(pieces.shape).astype(jnp.bfloat16)


def stack_kernel(layout, pairs, *refs):
    moves, blocks, per_device, chunks, reverse, chained = layout
    pieces = refs[:len(chunks)]
    out, wide, stage, sems = refs[len(chunks) + chained:]
    block_at = lax.axis_index("chan")
    first = chunks[0][0]
    for piece, (start, size) in zip(pieces, chunks):
        wide[:, :, start - first:start - first + size] = piece[...].astype(jnp.float32)
    copies = []
    for e in range(OFFS):
        moved = e - REACH
        far = lax.rem(block_at + (moved if reverse else -moved) + blocks, blocks)
        at = far if blocks == len(moves) else moves.index(moved)
        pair = pairs[block_at if reverse else far, e].astype(jnp.float32)
        for t in range(LAGS):
            tau = MAXLAG - t if reverse else t - MAXLAG
            row = lag_row(tau, per_device)
            stage[e, t] = wide[at, row:row + per_device, :] * pair
        lanes = pl.ds(first, stage.shape[3])
        copies.append(pltpu.make_async_copy(stage.at[e], out.at[e, :, :, lanes], sems.at[e]))
        copies[-1].start()
    for copy in copies:
        copy.wait()


def distinct_moves(blocks):
    return [2, -2, 1, -1, 0] if blocks >= OFFS else list(range(blocks))


def chunks_of(channels):
    if channels < 2 * LANES or channels % LANES:
        return [(0, channels)]
    first = channels * 2 // 5 // LANES * LANES
    return [(0, first), (first, channels - first)]


def shift(block, axis, distance):
    count = lax.axis_size(axis)
    return lax.ppermute(block, axis, [(i, (i + distance) % count) for i in range(count)])


def along_blocks(parts, moves, back):
    if lax.axis_size("chan") == len(moves):
        return lax.all_to_all(parts, "chan", split_axis=0, concat_axis=0, tiled=True)
    sign = -1 if back else 1
    return jnp.stack([shift(parts[i], "chan", sign * m) if m else parts[i] for i, m in enumerate(moves)])


def write_stack(pair_list, pieces, moves, blocks, per_device, channels, chunks, reverse, prior):
    width = sum(size for _, size in chunks)
    span = 2 * side_rows(per_device)
    chained = [] if prior is None else [prior]
    operands = len(pieces) + 1
    return pl.pallas_call(
        functools.partial(
            stack_kernel, (moves, blocks, per_device, chunks, reverse, len(chained))
        ),
        out_shape=jax.ShapeDtypeStruct((OFFS, LAGS, per_device, channels), jnp.float32),
        in_specs=[SMEM] + [VMEM] * len(pieces) + [HBM] * len(chained),
        out_specs=HBM,
        scratch_shapes=[
            pltpu.VMEM((len(moves), span, width), jnp.float32),
            pltpu.VMEM((OFFS, LAGS, per_device, width), jnp.float32),
            pltpu.SemaphoreType.DMA((OFFS,)),
        ],
        input_output_aliases={operands: 0} if chained else {},
        compiler_params=params(16),
        cost_estimate=LONG,
        name="source_order" if reverse else "receiver_order",
    )(pair_list, *pieces, *chained)


def in_hbm(value):
    return pltpu.with_memory_space_constraint(value, pltpu.HBM)


def after(value, *others):
    return lax.optimization_barrier((value, *others))[0]


def on_device(traces, channel_mask, smooth_width, source_phase, pair_list):
    _, channels, samples = traces.shape
    blocks, windows, subs = (lax.axis_size(a) for a in ("chan", "win", "sub"))
    sub_at = lax.axis_index("sub")
    per_device = VS // (windows * subs)
    group = per_device * STRIDE
    moves = distinct_moves(blocks)
    span = 2 * side_rows(per_device)
    chunks = chunks_of(channels)
    table, lags = dft_table(samples), lag_table(samples, per_device)
    factor = (NB * windows) ** (-0.5)
    bf16, f32 = jnp.bfloat16, jnp.float32
    like = jax.ShapeDtypeStruct
    mask_row = channel_mask.reshape(1, channels)

    def half_of(rows, start, size):
        grouped = rows.reshape(channels // (subs * group), subs, group, samples)
        first, count = start // (subs * group), size // (subs * group)
        half = lax.dynamic_slice(grouped, (first, sub_at, 0, 0), (count, 1, group, samples))
        return half.reshape(size // subs, samples)

    def from_windows(half):
        return [shift(half, "win", d) for d in range(1, windows)]

    def with_other_core(received):
        return [side for piece in received for side in (piece, shift(piece, "sub", 1))]

    def correlate(start, size, own, both, hint):
        return pl.pallas_call(
            functools.partial(chunk_kernel, factor),
            out_shape=like((len(moves), span, size), bf16),
            in_specs=[VMEM] * (6 + len(both)),
            out_specs=VMEM,
            scratch_shapes=[
                pltpu.VMEM((size // (subs * group), subs, group, samples), bf16),
                pltpu.VMEM((size, 2 * NB), bf16),
            ],
            compiler_params=params(32),
            cost_estimate=hint,
            name="lag_pieces",
        )(table, weights, share, turned, own, mask_row[:, start:start + size], *both)

    half = half_of(traces, *chunks[0])
    received = [from_windows(half)]
    *owns, weights, share, rows, table = pl.pallas_call(
        functools.partial(setup_kernel, chunks),
        out_shape=tuple(like((size, 2 * NB), bf16) for _, size in chunks)
        + (like((NB, NB), bf16), like((1, NB), f32))
        + (like((channels, samples), bf16), like(table.shape, bf16)),
        in_specs=[HBM, HBM, VMEM],
        out_specs=(VMEM,) * (len(chunks) + 4),
        scratch_shapes=[pltpu.SemaphoreType.DMA((TABLE_PARTS + 2,))],
        compiler_params=params(24),
        cost_estimate=SHORT,
        name="whiten_own",
    )(in_hbm(traces), in_hbm(table), after(smooth_width, half).reshape(1, NB))
    if len(chunks) > 1:
        received.append(from_windows(half_of(after(rows, *received[0]), *chunks[1])))
    near = pl.pallas_call(
        functools.partial(near_kernel, (windows, subs, per_device)),
        out_shape=like((len(moves), -(-windows * per_device // 8) * 8, samples), f32),
        in_specs=[SMEM] + [VMEM] * (1 + windows),
        out_specs=VMEM,
        compiler_params=params(16),
        cost_estimate=SHORT,
        name="pick_sources",
    )(source_phase, after(mask_row, weights), half, *received[0])
    received += [from_windows(half_of(after(rows, near), *chunk)) for chunk in chunks[2:]]
    inbound = with_other_core([after(r, near) for r in received[0]])
    sources = along_blocks(near, moves, False)
    turned = pl.pallas_call(
        functools.partial(turn_kernel, per_device, windows),
        out_shape=like((windows, len(moves) * span, 2 * NB), bf16),
        in_specs=[VMEM] * 5,
        out_specs=VMEM,
        scratch_shapes=[pltpu.VMEM((len(moves) * near.shape[1], 2 * NB), f32)],
        compiler_params=params(24),
        cost_estimate=SHORT,
        name="turn_sources",
    )(table, weights, after(share, *inbound), lags, sources)
    received[1:2] = [[after(r, turned) for r in chunk] for chunk in received[1:2]]
    pieces, arrived = [], []
    for i, (start, size) in enumerate(chunks):
        own = owns[i]
        if i:
            inbound = with_other_core(received[i])
            own = after(own, pieces[-1])
        pieces.append(correlate(start, size, own, inbound, LONG if i else SHORT))
        arrived.append(along_blocks(pieces[-1], moves, True))
    write = functools.partial(write_stack, pair_list)
    shape = (moves, blocks, per_device, channels)
    receiver_stack = write(pieces, *shape, chunks, False, None)
    source_stack = None
    for i, (chunk, back) in enumerate(zip(chunks, arrived)):
        if i + 1 < len(chunks):
            back = after(back, pieces[i + 1])
        source_stack = write([back], *shape, [chunk], True, source_stack)
    order = (2, 0, 1, 3)
    return (jnp.transpose(receiver_stack, order), jnp.transpose(source_stack, order))


def solution(mesh):
    in_specs = (
        P(("groups", "win"), "chan", None),
        P(("groups", "chan")),
        P(),
        P("groups"),
        P("groups", None),
    )
    out_specs = (
        P(("win", "sub"), None, None, ("groups", "chan")),
        P(("groups", "chan", "win", "sub"), None, None, None),
    )
    return jax.shard_map(
        on_device, mesh=mesh, in_specs=in_specs, out_specs=out_specs, check_vma=False
    )
```

```python
import functools
import math

import jax
import jax.numpy as jnp
import numpy as np
from jax import lax
from jax.experimental import pallas as pl
from jax.experimental.pallas import tpu as pltpu
from jax.sharding import PartitionSpec as P

NB = 512
MAXLAG = 50
STRIDE = 8
REACH = 2
VS = 8
OFFS = 5
LAGS = 2 * MAXLAG + 1
FLOOR = 0.25
TABLE_PARTS = 4
LANES = 128
VMEM = pl.BlockSpec(memory_space=pltpu.VMEM)
SMEM = pl.BlockSpec(memory_space=pltpu.SMEM)
HBM = pl.BlockSpec(memory_space=pltpu.HBM)
NT = (((1,), (1,)), ((), ()))


def dft_table(samples):
    phases = np.arange(samples)[:, None] * np.arange(NB)[None, :] % samples
    angles = phases * (2.0 * math.pi / samples)
    table = np.concatenate([np.cos(angles), -np.sin(angles)], axis=1)
    return jnp.asarray(table.astype(np.float32), jnp.bfloat16)


def side_rows(per_device):
    return -(-(MAXLAG + 1) * per_device // 8) * 8


def lag_row(tau, per_device):
    return abs(tau) * per_device + (0 if tau >= 0 else side_rows(per_device))


def lag_table(samples, per_device):
    lag = np.arange(side_rows(per_device)) // per_device
    angles = (lag[:, None] * np.arange(NB)[None, :] % samples) * (2.0 * math.pi / samples)
    table = np.concatenate([np.cos(angles), np.sin(angles)], axis=1)
    return jnp.asarray(table, jnp.float32)


def params(mib):
    return pltpu.CompilerParams(vmem_limit_bytes=mib << 20)


def cost(flops, moved):
    return pl.CostEstimate(flops=flops, bytes_accessed=moved, transcendentals=0)


SHORT, LONG = cost(1 << 20, 1 << 18), cost(1 << 33, 1 << 26)


def whiten(rows, table, weights, share):
    samples = rows.shape[1]
    spectrum = jnp.dot(rows, table, preferred_element_type=jnp.float32) * samples ** (-0.5)
    real, imag = spectrum[:, :NB], spectrum[:, NB:]
    amplitude = jnp.sqrt(real * real + imag * imag)
    high = amplitude.astype(jnp.bfloat16)
    low = (amplitude - high.astype(jnp.float32)).astype(jnp.bfloat16)
    total = jnp.dot(high, weights, preferred_element_type=jnp.float32)
    total += jnp.dot(low, weights, preferred_element_type=jnp.float32)
    gain = 1.0 / jnp.maximum(total * share, FLOOR)
    return (real * gain).astype(jnp.bfloat16), (imag * gain).astype(jnp.bfloat16)


def near_kernel(layout, phases, mask, *refs):
    windows, subs, per_device = layout
    halves, out = refs[:-1], refs[-1]
    block_at, win_at, sub_at = lax.axis_index("chan"), lax.axis_index("win"), lax.axis_index("sub")
    group = per_device * STRIDE
    rows, width = out.shape[0], halves[0].shape[0]
    phase = phases[block_at]

    def ones_at(first, width):
        row = lax.broadcasted_iota(jnp.int32, (rows, width), 0)
        place = lax.broadcasted_iota(jnp.int32, (rows, width), 1)
        return row, place == first + phase + STRIDE * (row % per_device)

    row, here = ones_at((win_at * subs + sub_at) * group, mask.shape[1])
    alive = jnp.sum(jnp.where(here, mask[...].astype(jnp.float32), 0.0), axis=1, keepdims=True)
    row, here = ones_at(win_at * group, width)
    total = jnp.zeros(out.shape, jnp.float32)
    for behind in range(windows):
        chosen = jnp.where(here & (row // per_device == behind), 1.0, 0.0).astype(jnp.bfloat16)
        total += jnp.dot(chosen, halves[behind][...], preferred_element_type=jnp.float32)
    out[...] = total * alive


def setup_kernel(chunks, traces, table, widths, *refs):
    owns, (weights, share, rows_kept, table_kept, sems) = refs[:len(chunks)], refs[len(chunks):]
    depth = table.shape[0] // TABLE_PARTS
    needed = chunks[-1][0] + chunks[-1][1]
    rest = rows_kept.shape[0] - needed
    first_rows = pltpu.make_async_copy(traces.at[0, pl.ds(0, needed)], rows_kept.at[pl.ds(0, needed)], sems.at[TABLE_PARTS])
    first_rows.start()
    parts = []
    for i in range(TABLE_PARTS):
        span = pl.ds(i * depth, depth)
        parts.append(pltpu.make_async_copy(table.at[span], table_kept.at[span], sems.at[i]))
        parts[-1].start()
    if rest:
        span = pl.ds(needed, rest)
        last_rows = pltpu.make_async_copy(traces.at[0, span], rows_kept.at[span], sems.at[TABLE_PARTS + 1])
        last_rows.start()
    reach = widths[...]
    near = lax.broadcasted_iota(jnp.int32, (NB, NB), 0)
    here = lax.broadcasted_iota(jnp.int32, (NB, NB), 1)
    weights[...] = jnp.where(jnp.abs(near - here) <= reach, 1.0, 0.0).astype(jnp.bfloat16)
    bins = lax.broadcasted_iota(jnp.int32, (1, NB), 1)
    count = jnp.minimum(bins + reach, NB - 1) - jnp.maximum(bins - reach, 0) + 1
    share[...] = 1.0 / count.astype(jnp.float32)
    first_rows.wait()
    for part in parts:
        part.wait()
    for (start, size), own in zip(chunks, owns):
        own_kernel(start, rows_kept, table_kept, weights, share, own)
    if rest:
        last_rows.wait()


def own_kernel(start, rows, table, weights, share, out):
    real, imag = whiten(rows[start:start + out.shape[0], :], table[...], weights[...], share[...])
    out[:, :NB] = real
    out[:, NB:] = imag


def turn_kernel(per_device, windows, table, weights, share, lags, *refs):
    picked, turned, spectra = refs[:-2], refs[-2], refs[-1]
    rows = jnp.concatenate([p[...] for p in picked], axis=0).astype(jnp.bfloat16)
    real, imag = whiten(rows, table[...], weights[...], share[...])
    spectra[:, :NB] = real.astype(jnp.float32)
    spectra[:, NB:] = imag.astype(jnp.float32)
    side = side_rows(per_device)
    span = 2 * side
    which = lax.broadcasted_iota(jnp.int32, (8, LANES), 0) % per_device

    def rows_of(first, lane):
        tiled = jnp.zeros((8, LANES), jnp.float32)
        for v in range(per_device):
            row = spectra[first + v:first + v + 1, lane:lane + LANES]
            tiled = jnp.where(which == v, row, tiled)
        return tiled[None]

    for lane in range(0, NB, LANES):
        cosine = lags[:, lane:lane + LANES].reshape(side // 8, 8, LANES)
        sine = lags[:, NB + lane:NB + lane + LANES].reshape(side // 8, 8, LANES)
        for at in range(len(picked)):
            for behind in range(windows):
                first = at * picked[0].shape[0] + behind * per_device
                real, imag = rows_of(first, lane), rows_of(first, NB + lane)
                cr, si, sr, ci = cosine * real, sine * imag, sine * real, cosine * imag
                up = jnp.concatenate([cr - si, cr + si], axis=0).reshape(span, LANES)
                down = jnp.concatenate([ci + sr, ci - sr], axis=0).reshape(span, LANES)
                spot = pl.ds(at * span, span)
                turned[behind, spot, lane:lane + LANES] = up.astype(jnp.bfloat16)
                turned[behind, spot, NB + lane:NB + lane + LANES] = down.astype(jnp.bfloat16)


def others_kernel(table, weights, share, *refs):
    halves, (white, raw) = refs[:-2], refs[-2:]
    sub_at = lax.axis_index("sub")
    groups, _, group, samples = raw.shape
    for i in range(white.shape[0]):
        for half, place in ((halves[2 * i], sub_at), (halves[2 * i + 1], 1 - sub_at)):
            raw[:, pl.ds(place, 1)] = half[...].reshape(groups, 1, group, samples)
        rows = raw[...].reshape(white.shape[1], samples)
        real, imag = whiten(rows, table[...], weights[...], share[...])
        white[i, :, :NB] = real
        white[i, :, NB:] = imag


def lag_kernel(factor, turned, own, white, mask, *pieces):
    total = lax.dot_general(turned[0], own[...], NT, preferred_element_type=jnp.float32)
    for i in range(white.shape[0]):
        total += lax.dot_general(turned[1 + i], white[i], NT, preferred_element_type=jnp.float32)
    result = total * (mask[...].astype(jnp.float32) * factor)
    span = result.shape[0] // len(pieces)
    for at, piece in enumerate(pieces):
        piece[...] = result[at * span:(at + 1) * span, :].astype(jnp.bfloat16)


def stack_kernel(layout, pairs, *refs):
    moves, blocks, per_device, chunks, reverse, chained = layout
    count = len(moves)
    pieces = refs[:count * len(chunks)]
    out, wide, stage, sems = refs[count * len(chunks) + chained:]
    block_at = lax.axis_index("chan")
    first = chunks[0][0]
    copies = []
    for at, target in enumerate(moves):
        for i, (start, size) in enumerate(chunks):
            wide[at, :, start - first:start - first + size] = pieces[i * count + at][...].astype(jnp.float32)
        for e in range(OFFS):
            moved = e - REACH
            if (moved - target) % blocks:
                continue
            block = block_at if reverse else lax.rem(block_at - moved + blocks, blocks)
            pair = pairs[block, e].astype(jnp.float32)
            for t in range(LAGS):
                tau = MAXLAG - t if reverse else t - MAXLAG
                row = lag_row(tau, per_device)
                stage[e, t] = wide[at, row:row + per_device, :] * pair
            lanes = pl.ds(first, stage.shape[3])
            copies.append(pltpu.make_async_copy(stage.at[e], out.at[e, :, :, lanes], sems.at[e]))
            copies[-1].start()
    for copy in copies:
        copy.wait()


def distinct_moves(blocks):
    moves = []
    for moved in (2, -2, 1, -1, 0):
        if all((m - moved) % blocks for m in moves):
            moves.append(moved)
    return moves


def chunks_of(channels):
    if channels < 2 * LANES or channels % LANES:
        return [(0, channels)]
    first = channels * 2 // 5 // LANES * LANES
    return [(0, first), (first, channels - first)]


def shift(block, axis, distance):
    count = lax.axis_size(axis)
    return lax.ppermute(block, axis, [(i, (i + distance) % count) for i in range(count)])


def write_stack(pair_list, pieces, moves, blocks, per_device, channels, chunks, reverse, prior):
    width = sum(size for _, size in chunks)
    span = 2 * side_rows(per_device)
    chained = [] if prior is None else [prior]
    operands = len(pieces) + 1
    return pl.pallas_call(
        functools.partial(
            stack_kernel, (moves, blocks, per_device, chunks, reverse, len(chained))
        ),
        out_shape=jax.ShapeDtypeStruct((OFFS, LAGS, per_device, channels), jnp.float32),
        in_specs=[SMEM] + [VMEM] * len(pieces) + [HBM] * len(chained),
        out_specs=HBM,
        scratch_shapes=[
            pltpu.VMEM((len(moves), span, width), jnp.float32),
            pltpu.VMEM((OFFS, LAGS, per_device, width), jnp.float32),
            pltpu.SemaphoreType.DMA((OFFS,)),
        ],
        input_output_aliases={operands: 0} if chained else {},
        compiler_params=params(16),
        cost_estimate=LONG,
        name="source_order" if reverse else "receiver_order",
    )(pair_list, *pieces, *chained)


def in_hbm(value):
    return pltpu.with_memory_space_constraint(value, pltpu.HBM)


def after(value, *others):
    return lax.optimization_barrier((value, *others))[0]


def on_device(traces, channel_mask, smooth_width, source_phase, pair_list):
    _, channels, samples = traces.shape
    blocks, windows, subs = (lax.axis_size(a) for a in ("chan", "win", "sub"))
    sub_at = lax.axis_index("sub")
    per_device = VS // (windows * subs)
    group = per_device * STRIDE
    moves = distinct_moves(blocks)
    span = 2 * side_rows(per_device)
    chunks = chunks_of(channels)
    table, lags = dft_table(samples), lag_table(samples, per_device)
    factor = (NB * windows) ** (-0.5)
    bf16, f32 = jnp.bfloat16, jnp.float32
    like = jax.ShapeDtypeStruct
    mask_row = channel_mask.reshape(1, channels)

    def half_of(rows, start, size):
        grouped = rows.reshape(channels // (subs * group), subs, group, samples)
        first, count = start // (subs * group), size // (subs * group)
        half = lax.dynamic_slice(grouped, (first, sub_at, 0, 0), (count, 1, group, samples))
        return half.reshape(size // subs, samples)

    def from_windows(half):
        return [shift(half, "win", d) for d in range(1, windows)]

    def with_other_core(received):
        return [side for piece in received for side in (piece, shift(piece, "sub", 1))]

    def whiten_others(size, both, hint):
        return pl.pallas_call(
            others_kernel,
            out_shape=like((windows - 1, size, 2 * NB), bf16),
            in_specs=[VMEM] * (3 + len(both)),
            out_specs=VMEM,
            scratch_shapes=[pltpu.VMEM((size // (subs * group), subs, group, samples), bf16)],
            compiler_params=params(24),
            cost_estimate=hint,
            name="whiten_others",
        )(table, weights, share, *both)

    def correlate(start, size, own, white, hint):
        return pl.pallas_call(
            functools.partial(lag_kernel, factor),
            out_shape=tuple(like((span, size), bf16) for _ in moves),
            in_specs=[VMEM] * 4,
            out_specs=tuple(VMEM for _ in moves),
            compiler_params=params(24),
            cost_estimate=hint,
            name="lag_pieces",
        )(turned, own, white, mask_row[:, start:start + size])

    half = half_of(traces, *chunks[0])
    received = [from_windows(half)]
    *owns, weights, share, rows, table = pl.pallas_call(
        functools.partial(setup_kernel, chunks),
        out_shape=tuple(like((size, 2 * NB), bf16) for _, size in chunks)
        + (like((NB, NB), bf16), like((1, NB), f32))
        + (like((channels, samples), bf16), like(table.shape, bf16)),
        in_specs=[HBM, HBM, VMEM],
        out_specs=(VMEM,) * (len(chunks) + 4),
        scratch_shapes=[pltpu.SemaphoreType.DMA((TABLE_PARTS + 2,))],
        compiler_params=params(24),
        cost_estimate=SHORT,
        name="whiten_own",
    )(in_hbm(traces), in_hbm(table), after(smooth_width, half).reshape(1, NB))
    if len(chunks) > 1:
        received.append(from_windows(half_of(after(rows, *received[0]), *chunks[1])))
    near = pl.pallas_call(
        functools.partial(near_kernel, (windows, subs, per_device)),
        out_shape=like((-(-windows * per_device // 8) * 8, samples), f32),
        in_specs=[SMEM] + [VMEM] * (1 + windows),
        out_specs=VMEM,
        compiler_params=params(16),
        cost_estimate=SHORT,
        name="pick_sources",
    )(source_phase, after(mask_row, weights), half, *received[0])
    inbound = with_other_core([after(r, near) for r in received[0]])
    white = whiten_others(chunks[0][1], inbound, SHORT)
    sources = [near if m % blocks == 0 else shift(near, "chan", m) for m in moves]
    turned = pl.pallas_call(
        functools.partial(turn_kernel, per_device, windows),
        out_shape=like((windows, len(moves) * span, 2 * NB), bf16),
        in_specs=[VMEM] * (4 + len(moves)),
        out_specs=VMEM,
        scratch_shapes=[pltpu.VMEM((len(moves) * near.shape[0], 2 * NB), f32)],
        compiler_params=params(24),
        cost_estimate=SHORT,
        name="turn_sources",
    )(table, weights, after(share, white), lags, *sources)
    pieces, arrived = [], []
    for i, (start, size) in enumerate(chunks):
        if i:
            white = whiten_others(size, with_other_core([after(r, pieces[-1]) for r in received[i]]), LONG)
        pieces.append(correlate(start, size, owns[i], white, LONG if i else SHORT))
        arrived.append([p if m % blocks == 0 else shift(p, "chan", -m) for m, p in zip(moves, pieces[-1])])
    write = functools.partial(write_stack, pair_list)
    everything = [piece for group in pieces for piece in group]
    receiver_stack = write(everything, moves, blocks, per_device, channels, chunks, False, None)
    source_stack = None
    for i, (chunk, back) in enumerate(zip(chunks, arrived)):
        steps = [list(range(len(moves)))]
        if i + 1 < len(chunks):
            back = [after(b, *pieces[i + 1]) for b in back]
        else:
            steps = [[at for at, m in enumerate(moves) if abs(m) != 2], [at for at, m in enumerate(moves) if abs(m) == 2]]
        for step in steps:
            part = [back[at] for at in step]
            part_moves = [moves[at] for at in step]
            source_stack = write(part, part_moves, blocks, per_device, channels, [chunk], True, source_stack)
    order = (2, 0, 1, 3)
    return (jnp.transpose(receiver_stack, order), jnp.transpose(source_stack, order))


def solution(mesh):
    in_specs = (
        P(("groups", "win"), "chan", None),
        P(("groups", "chan")),
        P(),
        P("groups"),
        P("groups", None),
    )
    out_specs = (
        P(("win", "sub"), None, None, ("groups", "chan")),
        P(("groups", "chan", "win", "sub"), None, None, None),
    )
    return jax.shard_map(
        on_device, mesh=mesh, in_specs=in_specs, out_specs=out_specs, check_vma=False
    )
```

```python
import functools
import math

import jax
import jax.numpy as jnp
import numpy as np
from jax import lax
from jax.experimental import pallas as pl
from jax.experimental.pallas import tpu as pltpu
from jax.sharding import PartitionSpec as P

NB = 512
MAXLAG = 50
STRIDE = 8
REACH = 2
VS = 8
OFFS = 5
LAGS = 2 * MAXLAG + 1
FLOOR = 0.25
TABLE_PARTS = 4
LANES = 128
VMEM = pl.BlockSpec(memory_space=pltpu.VMEM)
SMEM = pl.BlockSpec(memory_space=pltpu.SMEM)
HBM = pl.BlockSpec(memory_space=pltpu.HBM)
NT = (((1,), (1,)), ((), ()))


def dft_table(samples):
    phases = np.arange(samples)[:, None] * np.arange(NB)[None, :] % samples
    angles = phases * (2.0 * math.pi / samples)
    table = np.concatenate([np.cos(angles), -np.sin(angles)], axis=1)
    return jnp.asarray(table.astype(np.float32), jnp.bfloat16)


def side_rows(per_device):
    return -(-(MAXLAG + 1) * per_device // 8) * 8


def lag_row(tau, per_device):
    return abs(tau) * per_device + (0 if tau >= 0 else side_rows(per_device))


def lag_table(samples, per_device):
    lag = np.arange(side_rows(per_device)) // per_device
    angles = (lag[:, None] * np.arange(NB)[None, :] % samples) * (2.0 * math.pi / samples)
    table = np.concatenate([np.cos(angles), np.sin(angles)], axis=1)
    return jnp.asarray(table, jnp.float32)


def params(mib):
    return pltpu.CompilerParams(vmem_limit_bytes=mib << 20)


def cost(flops, moved):
    return pl.CostEstimate(flops=flops, bytes_accessed=moved, transcendentals=0)


SHORT, LONG = cost(1 << 20, 1 << 18), cost(1 << 33, 1 << 26)


def whiten(rows, table, weights, share):
    samples = rows.shape[1]
    spectrum = jnp.dot(rows, table, preferred_element_type=jnp.float32) * samples ** (-0.5)
    real, imag = spectrum[:, :NB], spectrum[:, NB:]
    amplitude = jnp.sqrt(real * real + imag * imag)
    high = amplitude.astype(jnp.bfloat16)
    low = (amplitude - high.astype(jnp.float32)).astype(jnp.bfloat16)
    total = jnp.dot(high, weights, preferred_element_type=jnp.float32)
    total += jnp.dot(low, weights, preferred_element_type=jnp.float32)
    gain = 1.0 / jnp.maximum(total * share, FLOOR)
    return (real * gain).astype(jnp.bfloat16), (imag * gain).astype(jnp.bfloat16)


def near_kernel(layout, phases, mask, *refs):
    windows, subs, per_device = layout
    halves, out = refs[:-1], refs[-1]
    block_at, win_at, sub_at = lax.axis_index("chan"), lax.axis_index("win"), lax.axis_index("sub")
    group = per_device * STRIDE
    rows, width = out.shape[0], halves[0].shape[0]
    phase = phases[block_at]

    def ones_at(first, width):
        row = lax.broadcasted_iota(jnp.int32, (rows, width), 0)
        place = lax.broadcasted_iota(jnp.int32, (rows, width), 1)
        return row, place == first + phase + STRIDE * (row % per_device)

    row, here = ones_at((win_at * subs + sub_at) * group, mask.shape[1])
    alive = jnp.sum(jnp.where(here, mask[...].astype(jnp.float32), 0.0), axis=1, keepdims=True)
    row, here = ones_at(win_at * group, width)
    total = jnp.zeros(out.shape, jnp.float32)
    for behind in range(windows):
        chosen = jnp.where(here & (row // per_device == behind), 1.0, 0.0).astype(jnp.bfloat16)
        total += jnp.dot(chosen, halves[behind][...], preferred_element_type=jnp.float32)
    out[...] = total * alive


def setup_kernel(chunks, traces, table, widths, *refs):
    owns, (weights, share, rows_kept, table_kept, sems) = refs[:len(chunks)], refs[len(chunks):]
    depth = table.shape[0] // TABLE_PARTS
    needed = chunks[-1][0] + chunks[-1][1]
    rest = rows_kept.shape[0] - needed
    first_rows = pltpu.make_async_copy(traces.at[0, pl.ds(0, needed)], rows_kept.at[pl.ds(0, needed)], sems.at[TABLE_PARTS])
    first_rows.start()
    parts = []
    for i in range(TABLE_PARTS):
        span = pl.ds(i * depth, depth)
        parts.append(pltpu.make_async_copy(table.at[span], table_kept.at[span], sems.at[i]))
        parts[-1].start()
    if rest:
        span = pl.ds(needed, rest)
        last_rows = pltpu.make_async_copy(traces.at[0, span], rows_kept.at[span], sems.at[TABLE_PARTS + 1])
        last_rows.start()
    reach = widths[...]
    near = lax.broadcasted_iota(jnp.int32, (NB, NB), 0)
    here = lax.broadcasted_iota(jnp.int32, (NB, NB), 1)
    weights[...] = jnp.where(jnp.abs(near - here) <= reach, 1.0, 0.0).astype(jnp.bfloat16)
    bins = lax.broadcasted_iota(jnp.int32, (1, NB), 1)
    count = jnp.minimum(bins + reach, NB - 1) - jnp.maximum(bins - reach, 0) + 1
    share[...] = 1.0 / count.astype(jnp.float32)
    first_rows.wait()
    for part in parts:
        part.wait()
    for (start, size), own in zip(chunks, owns):
        own_kernel(start, rows_kept, table_kept, weights, share, own)
    if rest:
        last_rows.wait()


def own_kernel(start, rows, table, weights, share, out):
    real, imag = whiten(rows[start:start + out.shape[0], :], table[...], weights[...], share[...])
    out[:, :NB] = real
    out[:, NB:] = imag


def turn_kernel(layout, table, weights, share, lags, *refs):
    per_device, windows, ties, blocks = layout
    picked, turned, spectra = refs[:-2], refs[-2], refs[-1]
    rows = jnp.concatenate([p[...] for p in picked], axis=0).astype(jnp.bfloat16)
    real, imag = whiten(rows, table[...], weights[...], share[...])
    spectra[:, :NB] = real.astype(jnp.float32)
    spectra[:, NB:] = imag.astype(jnp.float32)
    side = side_rows(per_device)
    span = 2 * side
    which = lax.broadcasted_iota(jnp.int32, (8, LANES), 0) % per_device

    def rows_of(first, lane):
        tiled = jnp.zeros((8, LANES), jnp.float32)
        for v in range(per_device):
            row = spectra[first + v:first + v + 1, lane:lane + LANES]
            tiled = jnp.where(which == v, row, tiled)
        return tiled[None]

    for lane in range(0, NB, LANES):
        cosine = lags[:, lane:lane + LANES].reshape(side // 8, 8, LANES)
        sine = lags[:, NB + lane:NB + lane + LANES].reshape(side // 8, 8, LANES)
        for at in range(len(ties)):
            for behind in range(windows):
                first = at * (spectra.shape[0] // len(ties)) + behind * per_device
                real, imag = rows_of(first, lane), rows_of(first, NB + lane)
                cr, si, sr, ci = cosine * real, sine * imag, sine * real, cosine * imag
                up = jnp.concatenate([cr - si, cr + si], axis=0).reshape(span, LANES)
                down = jnp.concatenate([ci + sr, ci - sr], axis=0).reshape(span, LANES)
                spot = pl.ds(at * span, span)
                turned[behind, spot, lane:lane + LANES] = up.astype(jnp.bfloat16)
                turned[behind, spot, NB + lane:NB + lane + LANES] = down.astype(jnp.bfloat16)


def others_kernel(table, weights, share, *refs):
    halves, (white, raw) = refs[:-2], refs[-2:]
    sub_at = lax.axis_index("sub")
    groups, _, group, samples = raw.shape
    for i in range(white.shape[0]):
        for half, place in ((halves[2 * i], sub_at), (halves[2 * i + 1], 1 - sub_at)):
            raw[:, pl.ds(place, 1)] = half[...].reshape(groups, 1, group, samples)
        rows = raw[...].reshape(white.shape[1], samples)
        real, imag = whiten(rows, table[...], weights[...], share[...])
        white[i, :, :NB] = real
        white[i, :, NB:] = imag


def lag_kernel(factor, turned, own, white, mask, *pieces):
    total = lax.dot_general(turned[0], own[...], NT, preferred_element_type=jnp.float32)
    for i in range(white.shape[0]):
        total += lax.dot_general(turned[1 + i], white[i], NT, preferred_element_type=jnp.float32)
    result = total * (mask[...].astype(jnp.float32) * factor)
    span = result.shape[0] // len(pieces)
    for at, piece in enumerate(pieces):
        piece[...] = result[at * span:(at + 1) * span, :].astype(jnp.bfloat16)


def stack_kernel(layout, pairs, *refs):
    ties, blocks, per_device, chunks, reverse, chained = layout
    count = len(ties)
    pieces = refs[:count * len(chunks)]
    out, wide, stage, sems = refs[count * len(chunks) + chained:]
    block_at = lax.axis_index("chan")
    first, width = chunks[0][0], stage.shape[3]
    lanes = pl.ds(first, width)
    listed = pairs[...].astype(jnp.float32)
    row = lax.broadcasted_iota(jnp.int32, listed.shape, 0)
    column = lax.broadcasted_iota(jnp.int32, listed.shape, 1)
    copies = []
    for at, tie in enumerate(ties):
        for i, (start, size) in enumerate(chunks):
            wide[at, :, start - first:start - first + size] = pieces[i * count + at][...].astype(jnp.float32)
        block = block_at if reverse else partner(block_at, blocks, tie)
        for e in offsets_of(block_at, blocks, tie, reverse):
            chosen = jnp.where((row == block) & (column == e), listed, 0.0)
            pair = jnp.broadcast_to(jnp.sum(chosen, keepdims=True), (per_device, width))
            slot = len(copies)
            for t in range(LAGS):
                tau = MAXLAG - t if reverse else t - MAXLAG
                spot = lag_row(tau, per_device)
                stage[slot, t] = wide[at, spot:spot + per_device, :] * pair
            copies.append(pltpu.make_async_copy(stage.at[slot], out.at[e, :, :, lanes], sems.at[slot]))
            copies[-1].start()
    for copy in copies:
        copy.wait()


def ties_of(blocks):
    if blocks == 4:
        return [("xor", i) for i in range(4)]
    ties = []
    for moved in (0, 1, -1, 2, -2):
        if all((m - moved) % blocks for _, m in ties):
            ties.append(("shift", moved))
    return ties


def partner(block, blocks, tie, back=False):
    kind, step = tie
    if kind == "xor":
        return block ^ step
    return (block + (step if back else -step) + blocks) % blocks


def offsets_of(block, blocks, tie, back):
    kind, step = tie
    if kind == "shift":
        return [e for e in range(OFFS) if (e - REACH - step) % blocks == 0]
    if step % 2 == 0:
        return [e for e in range(OFFS) if abs(e - REACH) == step]
    ahead = (block ^ step) - block if back else block - (block ^ step)
    return [jnp.where((ahead + blocks) % blocks == 1, REACH + 1, REACH - 1)]


def exchange(value, blocks, tie, back=False):
    return lax.ppermute(value, "chan", [(partner(b, blocks, tie, back), b) for b in range(blocks)])


def chunks_of(channels):
    if channels < 2 * LANES or channels % LANES:
        return [(0, channels)]
    first = channels * 2 // 5 // LANES * LANES
    return [(0, first), (first, channels - first)]


def shift(block, axis, distance):
    count = lax.axis_size(axis)
    return lax.ppermute(block, axis, [(i, (i + distance) % count) for i in range(count)])


def write_stack(pair_list, pieces, ties, blocks, per_device, channels, chunks, reverse, prior):
    width = sum(size for _, size in chunks)
    span = 2 * side_rows(per_device)
    slots = sum(len(offsets_of(0, blocks, tie, reverse)) for tie in ties)
    chained = [] if prior is None else [prior]
    operands = len(pieces) + 1
    return pl.pallas_call(
        functools.partial(
            stack_kernel, (ties, blocks, per_device, chunks, reverse, len(chained))
        ),
        out_shape=jax.ShapeDtypeStruct((OFFS, LAGS, per_device, channels), jnp.float32),
        in_specs=[VMEM] * operands + [HBM] * len(chained),
        out_specs=HBM,
        scratch_shapes=[
            pltpu.VMEM((len(ties), span, width), jnp.float32),
            pltpu.VMEM((slots, LAGS, per_device, width), jnp.float32),
            pltpu.SemaphoreType.DMA((slots,)),
        ],
        input_output_aliases={operands: 0} if chained else {},
        compiler_params=params(16),
        cost_estimate=LONG,
        name="source_order" if reverse else "receiver_order",
    )(pair_list, *pieces, *chained)


def in_hbm(value):
    return pltpu.with_memory_space_constraint(value, pltpu.HBM)


def after(value, *others):
    return lax.optimization_barrier((value, *others))[0]


def on_device(traces, channel_mask, smooth_width, source_phase, pair_list):
    _, channels, samples = traces.shape
    blocks, windows, subs = (lax.axis_size(a) for a in ("chan", "win", "sub"))
    sub_at = lax.axis_index("sub")
    per_device = VS // (windows * subs)
    group = per_device * STRIDE
    ties = ties_of(blocks)
    span = 2 * side_rows(per_device)
    chunks = chunks_of(channels)
    table, lags = dft_table(samples), lag_table(samples, per_device)
    factor = (NB * windows) ** (-0.5)
    bf16, f32 = jnp.bfloat16, jnp.float32
    like = jax.ShapeDtypeStruct
    mask_row = channel_mask.reshape(1, channels)

    def half_of(rows, start, size):
        grouped = rows.reshape(channels // (subs * group), subs, group, samples)
        first, count = start // (subs * group), size // (subs * group)
        half = lax.dynamic_slice(grouped, (first, sub_at, 0, 0), (count, 1, group, samples))
        return half.reshape(size // subs, samples)

    def from_windows(half):
        return [shift(half, "win", d) for d in range(1, windows)]

    def with_other_core(received):
        return [side for piece in received for side in (piece, shift(piece, "sub", 1))]

    def whiten_others(size, both, hint):
        return pl.pallas_call(
            others_kernel,
            out_shape=like((windows - 1, size, 2 * NB), bf16),
            in_specs=[VMEM] * (3 + len(both)),
            out_specs=VMEM,
            scratch_shapes=[pltpu.VMEM((size // (subs * group), subs, group, samples), bf16)],
            compiler_params=params(24),
            cost_estimate=hint,
            name="whiten_others",
        )(table, weights, share, *both)

    def correlate(start, size, own, white, hint):
        return pl.pallas_call(
            functools.partial(lag_kernel, factor),
            out_shape=tuple(like((span, size), bf16) for _ in ties),
            in_specs=[VMEM] * 4,
            out_specs=tuple(VMEM for _ in ties),
            compiler_params=params(24),
            cost_estimate=hint,
            name="lag_pieces",
        )(turned, own, white, mask_row[:, start:start + size])

    half = half_of(traces, *chunks[0])
    received = [from_windows(half)]
    *owns, weights, share, rows, table = pl.pallas_call(
        functools.partial(setup_kernel, chunks),
        out_shape=tuple(like((size, 2 * NB), bf16) for _, size in chunks)
        + (like((NB, NB), bf16), like((1, NB), f32))
        + (like((channels, samples), bf16), like(table.shape, bf16)),
        in_specs=[HBM, HBM, VMEM],
        out_specs=(VMEM,) * (len(chunks) + 4),
        scratch_shapes=[pltpu.SemaphoreType.DMA((TABLE_PARTS + 2,))],
        compiler_params=params(24),
        cost_estimate=SHORT,
        name="whiten_own",
    )(in_hbm(traces), in_hbm(table), after(smooth_width, half).reshape(1, NB))
    if len(chunks) > 1:
        received.append(from_windows(half_of(after(rows, *received[0]), *chunks[1])))
    near = pl.pallas_call(
        functools.partial(near_kernel, (windows, subs, per_device)),
        out_shape=like((-(-windows * per_device // 8) * 8, samples), f32),
        in_specs=[SMEM] + [VMEM] * (1 + windows),
        out_specs=VMEM,
        compiler_params=params(16),
        cost_estimate=SHORT,
        name="pick_sources",
    )(source_phase, after(mask_row, weights), half, *received[0])
    inbound = with_other_core([after(r, near) for r in received[0]])
    white = whiten_others(chunks[0][1], inbound, SHORT)
    if ties[1][0] == "xor":
        two = jnp.concatenate([near, exchange(near, blocks, ties[1])], axis=0)
        sources = [two, exchange(two, blocks, ties[2])]
    else:
        sources = [exchange(near, blocks, tie) if tie[1] else near for tie in ties]
    turned = pl.pallas_call(
        functools.partial(turn_kernel, (per_device, windows, ties, blocks)),
        out_shape=like((windows, len(ties) * span, 2 * NB), bf16),
        in_specs=[VMEM] * (4 + len(sources)),
        out_specs=VMEM,
        scratch_shapes=[pltpu.VMEM((len(ties) * near.shape[0], 2 * NB), f32)],
        compiler_params=params(24),
        cost_estimate=SHORT,
        name="turn_sources",
    )(table, weights, after(share, white), lags, *sources)
    pieces, arrived = [], []
    for i, (start, size) in enumerate(chunks):
        if i:
            white = whiten_others(size, with_other_core([after(r, pieces[-1]) for r in received[i]]), LONG)
        pieces.append(correlate(start, size, owns[i], white, LONG if i else SHORT))
        ahead = arrived[-1][1:2] if i else []
        sent = [after(p, *ahead) for p in pieces[-1]]
        arrived.append([exchange(p, blocks, tie, True) if tie[1] else p for tie, p in zip(ties, sent)])
    write = functools.partial(write_stack, pair_list)
    everything = [piece for group in pieces for piece in group]
    receiver_stack = write(everything, ties, blocks, per_device, channels, chunks, False, None)
    source_stack = None
    for i, (chunk, back) in enumerate(zip(chunks, arrived)):
        steps = [list(range(len(ties)))]
        if i + 1 < len(chunks):
            back = [after(b, *pieces[i + 1]) for b in back]
        elif len(ties) > 2:
            steps = [[0, 1], list(range(2, len(ties)))]
        for step in steps:
            part, part_ties = [back[at] for at in step], [ties[at] for at in step]
            source_stack = write(part, part_ties, blocks, per_device, channels, [chunk], True, source_stack)
    order = (2, 0, 1, 3)
    return (jnp.transpose(receiver_stack, order), jnp.transpose(source_stack, order))


def solution(mesh):
    in_specs = (
        P(("groups", "win"), "chan", None),
        P(("groups", "chan")),
        P(),
        P("groups"),
        P("groups", None),
    )
    out_specs = (
        P(("win", "sub"), None, None, ("groups", "chan")),
        P(("groups", "chan", "win", "sub"), None, None, None),
    )
    return jax.shard_map(
        on_device, mesh=mesh, in_specs=in_specs, out_specs=out_specs, check_vma=False
    )
```

```python
import functools
import math

import jax
import jax.numpy as jnp
import numpy as np
from jax import lax
from jax.experimental import pallas as pl
from jax.experimental.pallas import tpu as pltpu
from jax.sharding import PartitionSpec as P

NB = 512
MAXLAG = 50
STRIDE = 8
REACH = 2
VS = 8
OFFS = 5
LAGS = 2 * MAXLAG + 1
FLOOR = 0.25
TABLE_PARTS = 4
LANES = 128
VMEM = pl.BlockSpec(memory_space=pltpu.VMEM)
SMEM = pl.BlockSpec(memory_space=pltpu.SMEM)
HBM = pl.BlockSpec(memory_space=pltpu.HBM)
NT = (((1,), (1,)), ((), ()))


def dft_table(samples):
    phases = np.arange(samples)[:, None] * np.arange(NB)[None, :] % samples
    angles = phases * (2.0 * math.pi / samples)
    table = np.concatenate([np.cos(angles), -np.sin(angles)], axis=1)
    return jnp.asarray(table.astype(np.float32), jnp.bfloat16)


def side_rows(per_device):
    return -(-(MAXLAG + 1) * per_device // 8) * 8


def lag_row(tau, per_device):
    return abs(tau) * per_device + (0 if tau >= 0 else side_rows(per_device))


def lag_table(samples, per_device):
    lag = np.arange(side_rows(per_device)) // per_device
    angles = (lag[:, None] * np.arange(NB)[None, :] % samples) * (2.0 * math.pi / samples)
    table = np.concatenate([np.cos(angles), np.sin(angles)], axis=1)
    return jnp.asarray(table, jnp.float32)


def params(mib):
    return pltpu.CompilerParams(vmem_limit_bytes=mib << 20)


def cost(flops, moved):
    return pl.CostEstimate(flops=flops, bytes_accessed=moved, transcendentals=0)


SHORT, LONG = cost(1 << 20, 1 << 18), cost(1 << 33, 1 << 26)


def whiten(rows, table, weights, share):
    samples = rows.shape[1]
    spectrum = jnp.dot(rows, table, preferred_element_type=jnp.float32) * samples ** (-0.5)
    real, imag = spectrum[:, :NB], spectrum[:, NB:]
    amplitude = jnp.sqrt(real * real + imag * imag)
    high = amplitude.astype(jnp.bfloat16)
    low = (amplitude - high.astype(jnp.float32)).astype(jnp.bfloat16)
    total = jnp.dot(high, weights, preferred_element_type=jnp.float32)
    total += jnp.dot(low, weights, preferred_element_type=jnp.float32)
    gain = 1.0 / jnp.maximum(total * share, FLOOR)
    return (real * gain).astype(jnp.bfloat16), (imag * gain).astype(jnp.bfloat16)


def near_kernel(layout, phases, mask, *refs):
    windows, subs, per_device = layout
    halves, out = refs[:-1], refs[-1]
    block_at, win_at, sub_at = lax.axis_index("chan"), lax.axis_index("win"), lax.axis_index("sub")
    group = per_device * STRIDE
    rows, width = out.shape[0], halves[0].shape[0]
    phase = phases[block_at]

    def ones_at(first, width):
        row = lax.broadcasted_iota(jnp.int32, (rows, width), 0)
        place = lax.broadcasted_iota(jnp.int32, (rows, width), 1)
        return row, place == first + phase + STRIDE * (row % per_device)

    row, here = ones_at((win_at * subs + sub_at) * group, mask.shape[1])
    alive = jnp.sum(jnp.where(here, mask[...].astype(jnp.float32), 0.0), axis=1, keepdims=True)
    row, here = ones_at(win_at * group, width)
    total = jnp.zeros(out.shape, jnp.float32)
    for behind in range(windows):
        chosen = jnp.where(here & (row // per_device == behind), 1.0, 0.0).astype(jnp.bfloat16)
        total += jnp.dot(chosen, halves[behind][...], preferred_element_type=jnp.float32)
    out[...] = total * alive


def setup_kernel(chunks, traces, table, widths, *refs):
    owns, (weights, share, rows_kept, table_kept, sems, *scratch) = refs[:len(chunks)], refs[len(chunks):]
    depth = table.shape[0] // TABLE_PARTS
    needed = chunks[-1][0] + chunks[-1][1]
    rest = rows_kept.shape[0] - needed
    first_rows = pltpu.make_async_copy(traces.at[0, pl.ds(0, needed)], rows_kept.at[pl.ds(0, needed)], sems.at[TABLE_PARTS])
    first_rows.start()
    parts = []
    for i in range(TABLE_PARTS):
        span = pl.ds(i * depth, depth)
        parts.append(pltpu.make_async_copy(table.at[span], table_kept.at[span], sems.at[i]))
        parts[-1].start()
    if rest:
        span = pl.ds(needed, rest)
        last_rows = pltpu.make_async_copy(traces.at[0, span], rows_kept.at[span], sems.at[TABLE_PARTS + 1])
        last_rows.start()
    widths_kept, = scratch
    fetched = pltpu.make_async_copy(widths, widths_kept, sems.at[TABLE_PARTS + 2])
    fetched.start()
    fetched.wait()
    reach = widths_kept[...]
    near = lax.broadcasted_iota(jnp.int32, (NB, NB), 0)
    here = lax.broadcasted_iota(jnp.int32, (NB, NB), 1)
    weights[...] = jnp.where(jnp.abs(near - here) <= reach, 1.0, 0.0).astype(jnp.bfloat16)
    bins = lax.broadcasted_iota(jnp.int32, (1, NB), 1)
    count = jnp.minimum(bins + reach, NB - 1) - jnp.maximum(bins - reach, 0) + 1
    share[...] = 1.0 / count.astype(jnp.float32)
    first_rows.wait()
    for part in parts:
        part.wait()
    for (start, size), own in zip(chunks, owns):
        own_kernel(start, rows_kept, table_kept, weights, share, own)
    if rest:
        last_rows.wait()


def own_kernel(start, rows, table, weights, share, out):
    real, imag = whiten(rows[start:start + out.shape[0], :], table[...], weights[...], share[...])
    out[:, :NB] = real
    out[:, NB:] = imag


def turn_kernel(layout, table, weights, share, lags, *refs):
    per_device, windows, ties, blocks = layout
    picked, turned, spectra = refs[:-2], refs[-2], refs[-1]
    rows = jnp.concatenate([p[...] for p in picked], axis=0).astype(jnp.bfloat16)
    real, imag = whiten(rows, table[...], weights[...], share[...])
    spectra[:, :NB] = real.astype(jnp.float32)
    spectra[:, NB:] = imag.astype(jnp.float32)
    side = side_rows(per_device)
    span = 2 * side
    which = lax.broadcasted_iota(jnp.int32, (8, LANES), 0) % per_device

    def rows_of(first, lane):
        tiled = jnp.zeros((8, LANES), jnp.float32)
        for v in range(per_device):
            row = spectra[first + v:first + v + 1, lane:lane + LANES]
            tiled = jnp.where(which == v, row, tiled)
        return tiled[None]

    for lane in range(0, NB, LANES):
        cosine = lags[:, lane:lane + LANES].reshape(side // 8, 8, LANES)
        sine = lags[:, NB + lane:NB + lane + LANES].reshape(side // 8, 8, LANES)
        for at in range(len(ties)):
            for behind in range(windows):
                first = at * (spectra.shape[0] // len(ties)) + behind * per_device
                real, imag = rows_of(first, lane), rows_of(first, NB + lane)
                cr, si, sr, ci = cosine * real, sine * imag, sine * real, cosine * imag
                up = jnp.concatenate([cr - si, cr + si], axis=0).reshape(span, LANES)
                down = jnp.concatenate([ci + sr, ci - sr], axis=0).reshape(span, LANES)
                spot = pl.ds(at * span, span)
                turned[behind, spot, lane:lane + LANES] = up.astype(jnp.bfloat16)
                turned[behind, spot, NB + lane:NB + lane + LANES] = down.astype(jnp.bfloat16)


def others_kernel(table, weights, share, *refs):
    parts, (white, raw) = refs[:-2], refs[-2:]
    sub_at = lax.axis_index("sub")
    groups, _, group, samples = raw.shape
    each = len(parts) // white.shape[0]
    for i in range(white.shape[0]):
        if each == 1:
            rows = parts[i][...]
        else:
            for half, place in ((parts[2 * i], sub_at), (parts[2 * i + 1], 1 - sub_at)):
                raw[:, pl.ds(place, 1)] = half[...].reshape(groups, 1, group, samples)
            rows = raw[...].reshape(white.shape[1], samples)
        real, imag = whiten(rows, table[...], weights[...], share[...])
        white[i, :, :NB] = real
        white[i, :, NB:] = imag


def lag_kernel(factor, turned, own, white, mask, *pieces):
    total = lax.dot_general(turned[0], own[...], NT, preferred_element_type=jnp.float32)
    for i in range(white.shape[0]):
        total += lax.dot_general(turned[1 + i], white[i], NT, preferred_element_type=jnp.float32)
    result = total * (mask[...].astype(jnp.float32) * factor)
    span = result.shape[0] // len(pieces)
    for at, piece in enumerate(pieces):
        piece[...] = result[at * span:(at + 1) * span, :].astype(jnp.bfloat16)


def stack_kernel(layout, pairs, *refs):
    ties, blocks, per_device, chunks, reverse, chained = layout
    count = len(ties)
    pieces = refs[:count * len(chunks)]
    out, wide, stage, sems = refs[count * len(chunks) + chained:]
    block_at = lax.axis_index("chan")
    first, width = chunks[0][0], stage.shape[3]
    lanes = pl.ds(first, width)
    listed = pairs[...].astype(jnp.float32)
    row = lax.broadcasted_iota(jnp.int32, listed.shape, 0)
    column = lax.broadcasted_iota(jnp.int32, listed.shape, 1)
    copies = []
    for at, tie in enumerate(ties):
        for i, (start, size) in enumerate(chunks):
            wide[at, :, start - first:start - first + size] = pieces[i * count + at][...].astype(jnp.float32)
        block = block_at if reverse else partner(block_at, blocks, tie)
        for e in offsets_of(block_at, blocks, tie, reverse):
            chosen = jnp.where((row == block) & (column == e), listed, 0.0)
            pair = jnp.broadcast_to(jnp.sum(chosen, keepdims=True), (per_device, width))
            slot = len(copies)
            for t in range(LAGS):
                tau = MAXLAG - t if reverse else t - MAXLAG
                spot = lag_row(tau, per_device)
                stage[slot, t] = wide[at, spot:spot + per_device, :] * pair
            copies.append(pltpu.make_async_copy(stage.at[slot], out.at[e, :, :, lanes], sems.at[slot]))
            copies[-1].start()
    for copy in copies:
        copy.wait()


def ties_of(blocks):
    if blocks == 4:
        return [("xor", i) for i in range(4)]
    ties = []
    for moved in (0, 1, -1, 2, -2):
        if all((m - moved) % blocks for _, m in ties):
            ties.append(("shift", moved))
    return ties


def partner(block, blocks, tie, back=False):
    kind, step = tie
    if kind == "xor":
        return block ^ step
    return (block + (step if back else -step) + blocks) % blocks


def offsets_of(block, blocks, tie, back):
    kind, step = tie
    if kind == "shift":
        return [e for e in range(OFFS) if (e - REACH - step) % blocks == 0]
    if step % 2 == 0:
        return [e for e in range(OFFS) if abs(e - REACH) == step]
    ahead = (block ^ step) - block if back else block - (block ^ step)
    return [jnp.where((ahead + blocks) % blocks == 1, REACH + 1, REACH - 1)]


def exchange(value, blocks, tie, back=False):
    return lax.ppermute(value, "chan", [(partner(b, blocks, tie, back), b) for b in range(blocks)])


def chunks_of(channels):
    if channels < 2 * LANES or channels % LANES:
        return [(0, channels)]
    first = channels * 3 // 5 // LANES * LANES
    return [(0, first), (first, channels - first)]


def shift(block, axis, distance):
    count = lax.axis_size(axis)
    return lax.ppermute(block, axis, [(i, (i + distance) % count) for i in range(count)])


def write_stack(pair_list, pieces, ties, blocks, per_device, channels, chunks, reverse, prior):
    width = sum(size for _, size in chunks)
    span = 2 * side_rows(per_device)
    slots = sum(len(offsets_of(0, blocks, tie, reverse)) for tie in ties)
    chained = [] if prior is None else [prior]
    operands = len(pieces) + 1
    return pl.pallas_call(
        functools.partial(
            stack_kernel, (ties, blocks, per_device, chunks, reverse, len(chained))
        ),
        out_shape=jax.ShapeDtypeStruct((OFFS, LAGS, per_device, channels), jnp.float32),
        in_specs=[VMEM] * operands + [HBM] * len(chained),
        out_specs=HBM,
        scratch_shapes=[
            pltpu.VMEM((len(ties), span, width), jnp.float32),
            pltpu.VMEM((slots, LAGS, per_device, width), jnp.float32),
            pltpu.SemaphoreType.DMA((slots,)),
        ],
        input_output_aliases={operands: 0} if chained else {},
        compiler_params=params(16),
        cost_estimate=SHORT,
        name="source_order" if reverse else "receiver_order",
    )(pair_list, *pieces, *chained)


def in_hbm(value):
    return pltpu.with_memory_space_constraint(value, pltpu.HBM)


def after(value, *others):
    return lax.optimization_barrier((value, *others))[0]


def on_device(traces, channel_mask, smooth_width, source_phase, pair_list):
    _, channels, samples = traces.shape
    blocks, windows, subs = (lax.axis_size(a) for a in ("chan", "win", "sub"))
    sub_at = lax.axis_index("sub")
    per_device = VS // (windows * subs)
    group = per_device * STRIDE
    ties = ties_of(blocks)
    span = 2 * side_rows(per_device)
    chunks = chunks_of(channels)
    table, lags = dft_table(samples), lag_table(samples, per_device)
    factor = (NB * windows) ** (-0.5)
    bf16, f32 = jnp.bfloat16, jnp.float32
    like = jax.ShapeDtypeStruct
    mask_row = channel_mask.reshape(1, channels)

    def half_of(rows, start, size):
        grouped = rows.reshape(channels // (subs * group), subs, group, samples)
        first, count = start // (subs * group), size // (subs * group)
        half = lax.dynamic_slice(grouped, (first, sub_at, 0, 0), (count, 1, group, samples))
        return half.reshape(size // subs, samples)

    def from_windows(half):
        return [shift(half, "win", d) for d in range(1, windows)]

    def with_other_core(received):
        return [side for piece in received for side in (piece, shift(piece, "sub", 1))]

    def whiten_others(size, both, hint):
        return pl.pallas_call(
            others_kernel,
            out_shape=like((windows - 1, size, 2 * NB), bf16),
            in_specs=[VMEM] * (3 + len(both)),
            out_specs=VMEM,
            scratch_shapes=[pltpu.VMEM((size // (subs * group), subs, group, samples), bf16)],
            compiler_params=params(24),
            cost_estimate=hint,
            name="whiten_others",
        )(table, weights, share, *both)

    def correlate(start, size, own, white, hint):
        return pl.pallas_call(
            functools.partial(lag_kernel, factor),
            out_shape=tuple(like((span, size), bf16) for _ in ties),
            in_specs=[VMEM] * 4,
            out_specs=tuple(VMEM for _ in ties),
            compiler_params=params(24),
            cost_estimate=hint,
            name="lag_pieces",
        )(turned, own, white, mask_row[:, start:start + size])

    half = half_of(traces, *chunks[0])
    received = [from_windows(half)]
    *owns, weights, share, rows, table = pl.pallas_call(
        functools.partial(setup_kernel, chunks),
        out_shape=tuple(like((size, 2 * NB), bf16) for _, size in chunks)
        + (like((NB, NB), bf16), like((1, NB), f32))
        + (like((channels, samples), bf16), like(table.shape, bf16)),
        in_specs=[HBM, HBM, HBM],
        out_specs=(VMEM,) * (len(chunks) + 4),
        scratch_shapes=[pltpu.SemaphoreType.DMA((TABLE_PARTS + 3,)), pltpu.VMEM((1, NB), jnp.int32)],
        compiler_params=params(24),
        cost_estimate=SHORT,
        name="whiten_own",
    )(in_hbm(traces), in_hbm(table), in_hbm(after(smooth_width, half).reshape(1, NB)))
    if len(chunks) > 1:
        received += [from_windows(after(rows, *received[0])[a:a + n]) for a, n in chunks[1:]]
    near = pl.pallas_call(
        functools.partial(near_kernel, (windows, subs, per_device)),
        out_shape=like((-(-windows * per_device // 8) * 8, samples), f32),
        in_specs=[SMEM] + [VMEM] * (1 + windows),
        out_specs=VMEM,
        compiler_params=params(16),
        cost_estimate=SHORT,
        name="pick_sources",
    )(source_phase, after(mask_row, weights), half, *received[0])
    inbound = with_other_core([after(r, near) for r in received[0]])
    white = whiten_others(chunks[0][1], inbound, SHORT)
    if ties[1][0] == "xor":
        two = jnp.concatenate([near, exchange(near, blocks, ties[1])], axis=0)
        sources = [two, exchange(two, blocks, ties[2])]
    else:
        sources = [exchange(near, blocks, tie) if tie[1] else near for tie in ties]
    turned = pl.pallas_call(
        functools.partial(turn_kernel, (per_device, windows, ties, blocks)),
        out_shape=like((windows, len(ties) * span, 2 * NB), bf16),
        in_specs=[VMEM] * (4 + len(sources)),
        out_specs=VMEM,
        scratch_shapes=[pltpu.VMEM((len(ties) * near.shape[0], 2 * NB), f32)],
        compiler_params=params(24),
        cost_estimate=SHORT,
        name="turn_sources",
    )(table, weights, after(share, white), lags, *sources)
    pieces, arrived = [], []
    for i, (start, size) in enumerate(chunks):
        if i:
            white = whiten_others(size, [after(r, *pieces[-1]) for r in received[i]], LONG)
        pieces.append(correlate(start, size, owns[i], white, LONG if i else SHORT))
        ahead = arrived[-1][1:2] if i else []
        sent = [after(p, *ahead) for p in pieces[-1]]
        arrived.append([exchange(p, blocks, tie, True) if tie[1] else p for tie, p in zip(ties, sent)])
    write = functools.partial(write_stack, pair_list)
    everything = [piece for group in pieces for piece in group]
    receiver_stack = write(everything, ties, blocks, per_device, channels, chunks, False, None)
    source_stack = None
    for i, (chunk, back) in enumerate(zip(chunks, arrived)):
        steps = [list(range(len(ties)))]
        if i + 1 < len(chunks):
            back = [after(b, *pieces[i + 1]) for b in back]
        elif len(ties) > 2:
            steps = [[0, 1], list(range(2, len(ties)))]
        for step in steps:
            part, part_ties = [back[at] for at in step], [ties[at] for at in step]
            source_stack = write(part, part_ties, blocks, per_device, channels, [chunk], True, source_stack)
    order = (2, 0, 1, 3)
    return (jnp.transpose(receiver_stack, order), jnp.transpose(source_stack, order))


def solution(mesh):
    in_specs = (
        P(("groups", "win"), "chan", None),
        P(("groups", "chan")),
        P(),
        P("groups"),
        P("groups", None),
    )
    out_specs = (
        P(("win", "sub"), None, None, ("groups", "chan")),
        P(("groups", "chan", "win", "sub"), None, None, None),
    )
    return jax.shard_map(
        on_device, mesh=mesh, in_specs=in_specs, out_specs=out_specs, check_vma=False
    )
```

```python
import functools
import math

import jax
import jax.numpy as jnp
import numpy as np
from jax import lax
from jax.experimental import pallas as pl
from jax.experimental.pallas import tpu as pltpu
from jax.sharding import PartitionSpec as P

NB = 512
MAXLAG = 50
STRIDE = 8
REACH = 2
VS = 8
OFFS = 5
LAGS = 2 * MAXLAG + 1
FLOOR = 0.25
TABLE_PARTS = 4
LANES = 128
VMEM = pl.BlockSpec(memory_space=pltpu.VMEM)
SMEM = pl.BlockSpec(memory_space=pltpu.SMEM)
HBM = pl.BlockSpec(memory_space=pltpu.HBM)
NT = (((1,), (1,)), ((), ()))


def dft_table(samples):
    phases = np.arange(samples)[:, None] * np.arange(NB)[None, :] % samples
    angles = phases * (2.0 * math.pi / samples)
    table = np.concatenate([np.cos(angles), -np.sin(angles)], axis=1)
    return jnp.asarray(table.astype(np.float32), jnp.bfloat16)


def side_rows(per_device):
    return -(-(MAXLAG + 1) * per_device // 8) * 8


def lag_row(tau, per_device):
    return abs(tau) * per_device + (0 if tau >= 0 else side_rows(per_device))


def lag_table(samples, per_device):
    lag = np.arange(side_rows(per_device)) // per_device
    angles = (lag[:, None] * np.arange(NB)[None, :] % samples) * (2.0 * math.pi / samples)
    table = np.concatenate([np.cos(angles), np.sin(angles)], axis=1)
    return jnp.asarray(table, jnp.float32)


def params(mib):
    return pltpu.CompilerParams(vmem_limit_bytes=mib << 20)


def cost(flops, moved):
    return pl.CostEstimate(flops=flops, bytes_accessed=moved, transcendentals=0)


SHORT, LONG = cost(1 << 20, 1 << 18), cost(1 << 33, 1 << 26)


def whiten(rows, table, weights, share):
    samples = rows.shape[1]
    spectrum = jnp.dot(rows, table, preferred_element_type=jnp.float32) * samples ** (-0.5)
    real, imag = spectrum[:, :NB], spectrum[:, NB:]
    amplitude = jnp.sqrt(real * real + imag * imag)
    high = amplitude.astype(jnp.bfloat16)
    low = (amplitude - high.astype(jnp.float32)).astype(jnp.bfloat16)
    total = jnp.dot(high, weights, preferred_element_type=jnp.float32)
    total += jnp.dot(low, weights, preferred_element_type=jnp.float32)
    gain = 1.0 / jnp.maximum(total * share, FLOOR)
    return (real * gain).astype(jnp.bfloat16), (imag * gain).astype(jnp.bfloat16)


def near_kernel(layout, phases, mask, *refs):
    windows, subs, per_device = layout
    halves, out = refs[:-1], refs[-1]
    block_at, win_at, sub_at = lax.axis_index("chan"), lax.axis_index("win"), lax.axis_index("sub")
    group = per_device * STRIDE
    rows, width = out.shape[0], halves[0].shape[0]
    phase = phases[block_at]

    def ones_at(first, width):
        row = lax.broadcasted_iota(jnp.int32, (rows, width), 0)
        place = lax.broadcasted_iota(jnp.int32, (rows, width), 1)
        return row, place == first + phase + STRIDE * (row % per_device)

    row, here = ones_at((win_at * subs + sub_at) * group, mask.shape[1])
    alive = jnp.sum(jnp.where(here, mask[...].astype(jnp.float32), 0.0), axis=1, keepdims=True)
    row, here = ones_at(win_at * group, width)
    total = jnp.zeros(out.shape, jnp.float32)
    for behind in range(windows):
        chosen = jnp.where(here & (row // per_device == behind), 1.0, 0.0).astype(jnp.bfloat16)
        total += jnp.dot(chosen, halves[behind][...], preferred_element_type=jnp.float32)
    out[...] = total * alive


def setup_kernel(chunks, traces, table, widths, *refs):
    owns, (weights, share, rows_kept, table_kept, sems, *scratch) = refs[:len(chunks)], refs[len(chunks):]
    depth = table.shape[0] // TABLE_PARTS
    needed = chunks[-1][0] + chunks[-1][1]
    rest = rows_kept.shape[0] - needed
    first_rows = pltpu.make_async_copy(traces.at[0, pl.ds(0, needed)], rows_kept.at[pl.ds(0, needed)], sems.at[TABLE_PARTS])
    first_rows.start()
    parts = []
    for i in range(TABLE_PARTS):
        span = pl.ds(i * depth, depth)
        parts.append(pltpu.make_async_copy(table.at[span], table_kept.at[span], sems.at[i]))
        parts[-1].start()
    if rest:
        span = pl.ds(needed, rest)
        last_rows = pltpu.make_async_copy(traces.at[0, span], rows_kept.at[span], sems.at[TABLE_PARTS + 1])
        last_rows.start()
    widths_kept, = scratch
    fetched = pltpu.make_async_copy(widths, widths_kept, sems.at[TABLE_PARTS + 2])
    fetched.start()
    fetched.wait()
    reach = widths_kept[...]
    near = lax.broadcasted_iota(jnp.int32, (NB, NB), 0)
    here = lax.broadcasted_iota(jnp.int32, (NB, NB), 1)
    weights[...] = jnp.where(jnp.abs(near - here) <= reach, 1.0, 0.0).astype(jnp.bfloat16)
    bins = lax.broadcasted_iota(jnp.int32, (1, NB), 1)
    count = jnp.minimum(bins + reach, NB - 1) - jnp.maximum(bins - reach, 0) + 1
    share[...] = 1.0 / count.astype(jnp.float32)
    first_rows.wait()
    for part in parts:
        part.wait()
    for (start, size), own in zip(chunks, owns):
        own_kernel(start, rows_kept, table_kept, weights, share, own)
    if rest:
        last_rows.wait()


def own_kernel(start, rows, table, weights, share, out):
    real, imag = whiten(rows[start:start + out.shape[0], :], table[...], weights[...], share[...])
    out[:, :NB] = real
    out[:, NB:] = imag


def turn_kernel(layout, table, weights, share, lags, *refs):
    per_device, windows, ties, blocks = layout
    picked, turned, spectra = refs[:-2], refs[-2], refs[-1]
    rows = jnp.concatenate([p[...] for p in picked], axis=0).astype(jnp.bfloat16)
    real, imag = whiten(rows, table[...], weights[...], share[...])
    spectra[:, :NB] = real.astype(jnp.float32)
    spectra[:, NB:] = imag.astype(jnp.float32)
    side = side_rows(per_device)
    span = 2 * side
    which = lax.broadcasted_iota(jnp.int32, (8, LANES), 0) % per_device

    def rows_of(first, lane):
        tiled = jnp.zeros((8, LANES), jnp.float32)
        for v in range(per_device):
            row = spectra[first + v:first + v + 1, lane:lane + LANES]
            tiled = jnp.where(which == v, row, tiled)
        return tiled[None]

    for lane in range(0, NB, LANES):
        cosine = lags[:, lane:lane + LANES].reshape(side // 8, 8, LANES)
        sine = lags[:, NB + lane:NB + lane + LANES].reshape(side // 8, 8, LANES)
        for at in range(len(ties)):
            for behind in range(windows):
                first = at * (spectra.shape[0] // len(ties)) + behind * per_device
                real, imag = rows_of(first, lane), rows_of(first, NB + lane)
                cr, si, sr, ci = cosine * real, sine * imag, sine * real, cosine * imag
                up = jnp.concatenate([cr - si, cr + si], axis=0).reshape(span, LANES)
                down = jnp.concatenate([ci + sr, ci - sr], axis=0).reshape(span, LANES)
                spot = pl.ds(at * span, span)
                turned[behind, spot, lane:lane + LANES] = up.astype(jnp.bfloat16)
                turned[behind, spot, NB + lane:NB + lane + LANES] = down.astype(jnp.bfloat16)


def others_kernel(table, weights, share, *refs):
    parts, (white, raw) = refs[:-2], refs[-2:]
    sub_at = lax.axis_index("sub")
    groups, _, group, samples = raw.shape
    each = len(parts) // white.shape[0]
    for i in range(white.shape[0]):
        if each == 1:
            rows = parts[i][...]
        else:
            for half, place in ((parts[2 * i], sub_at), (parts[2 * i + 1], 1 - sub_at)):
                raw[:, pl.ds(place, 1)] = half[...].reshape(groups, 1, group, samples)
            rows = raw[...].reshape(white.shape[1], samples)
        real, imag = whiten(rows, table[...], weights[...], share[...])
        white[i, :, :NB] = real
        white[i, :, NB:] = imag


def lag_kernel(factor, turned, own, white, mask, *pieces):
    total = lax.dot_general(turned[0], own[...], NT, preferred_element_type=jnp.float32)
    for i in range(white.shape[0]):
        total += lax.dot_general(turned[1 + i], white[i], NT, preferred_element_type=jnp.float32)
    result = total * (mask[...].astype(jnp.float32) * factor)
    span = result.shape[0] // len(pieces)
    for at, piece in enumerate(pieces):
        piece[...] = result[at * span:(at + 1) * span, :].astype(jnp.bfloat16)


def stack_kernel(layout, pairs, *refs):
    ties, blocks, per_device, chunks, reverse, chained = layout
    count = len(ties)
    pieces = refs[:count * len(chunks)]
    out, wide, stage, sems = refs[count * len(chunks) + chained:]
    block_at = lax.axis_index("chan")
    first, width = chunks[0][0], stage.shape[3]
    lanes = pl.ds(first, width)
    listed = pairs[...].astype(jnp.float32)
    row = lax.broadcasted_iota(jnp.int32, listed.shape, 0)
    column = lax.broadcasted_iota(jnp.int32, listed.shape, 1)
    copies = []
    for at, tie in enumerate(ties):
        for i, (start, size) in enumerate(chunks):
            wide[at, :, start - first:start - first + size] = pieces[i * count + at][...].astype(jnp.float32)
        block = block_at if reverse else partner(block_at, blocks, tie)
        for e in offsets_of(block_at, blocks, tie, reverse):
            chosen = jnp.where((row == block) & (column == e), listed, 0.0)
            pair = jnp.broadcast_to(jnp.sum(chosen, keepdims=True), (per_device, width))
            slot = len(copies)
            for t in range(LAGS):
                tau = MAXLAG - t if reverse else t - MAXLAG
                spot = lag_row(tau, per_device)
                stage[slot, t] = wide[at, spot:spot + per_device, :] * pair
            copies.append(pltpu.make_async_copy(stage.at[slot], out.at[e, :, :, lanes], sems.at[slot]))
            copies[-1].start()
    for copy in copies:
        copy.wait()


def ties_of(blocks):
    if blocks == 4:
        return [("xor", i) for i in range(4)]
    ties = []
    for moved in (0, 1, -1, 2, -2):
        if all((m - moved) % blocks for _, m in ties):
            ties.append(("shift", moved))
    return ties


def partner(block, blocks, tie, back=False):
    kind, step = tie
    if kind == "xor":
        return block ^ step
    return (block + (step if back else -step) + blocks) % blocks


def offsets_of(block, blocks, tie, back):
    kind, step = tie
    if kind == "shift":
        return [e for e in range(OFFS) if (e - REACH - step) % blocks == 0]
    if step % 2 == 0:
        return [e for e in range(OFFS) if abs(e - REACH) == step]
    ahead = (block ^ step) - block if back else block - (block ^ step)
    return [jnp.where((ahead + blocks) % blocks == 1, REACH + 1, REACH - 1)]


def exchange(value, blocks, tie, back=False):
    return lax.ppermute(value, "chan", [(partner(b, blocks, tie, back), b) for b in range(blocks)])


def chunks_of(channels):
    if channels < 2 * LANES or channels % LANES:
        return [(0, channels)]
    first = channels * 2 // 5 // LANES * LANES
    return [(0, first), (first, channels - first)]


def shift(block, axis, distance):
    count = lax.axis_size(axis)
    return lax.ppermute(block, axis, [(i, (i + distance) % count) for i in range(count)])


def write_stack(pair_list, pieces, ties, blocks, per_device, channels, chunks, reverse, prior):
    width = sum(size for _, size in chunks)
    span = 2 * side_rows(per_device)
    slots = sum(len(offsets_of(0, blocks, tie, reverse)) for tie in ties)
    chained = [] if prior is None else [prior]
    operands = len(pieces) + 1
    return pl.pallas_call(
        functools.partial(
            stack_kernel, (ties, blocks, per_device, chunks, reverse, len(chained))
        ),
        out_shape=jax.ShapeDtypeStruct((OFFS, LAGS, per_device, channels), jnp.float32),
        in_specs=[VMEM] * operands + [HBM] * len(chained),
        out_specs=HBM,
        scratch_shapes=[
            pltpu.VMEM((len(ties), span, width), jnp.float32),
            pltpu.VMEM((slots, LAGS, per_device, width), jnp.float32),
            pltpu.SemaphoreType.DMA((slots,)),
        ],
        input_output_aliases={operands: 0} if chained else {},
        compiler_params=params(16),
        cost_estimate=LONG,
        name="source_order" if reverse else "receiver_order",
    )(pair_list, *pieces, *chained)


def in_hbm(value):
    return pltpu.with_memory_space_constraint(value, pltpu.HBM)


def after(value, *others):
    return lax.optimization_barrier((value, *others))[0]


def on_device(traces, channel_mask, smooth_width, source_phase, pair_list):
    _, channels, samples = traces.shape
    blocks, windows, subs = (lax.axis_size(a) for a in ("chan", "win", "sub"))
    sub_at = lax.axis_index("sub")
    per_device = VS // (windows * subs)
    group = per_device * STRIDE
    ties = ties_of(blocks)
    span = 2 * side_rows(per_device)
    chunks = chunks_of(channels)
    table, lags = dft_table(samples), lag_table(samples, per_device)
    factor = (NB * windows) ** (-0.5)
    bf16, f32 = jnp.bfloat16, jnp.float32
    like = jax.ShapeDtypeStruct
    mask_row = channel_mask.reshape(1, channels)

    def half_of(rows, start, size):
        grouped = rows.reshape(channels // (subs * group), subs, group, samples)
        first, count = start // (subs * group), size // (subs * group)
        half = lax.dynamic_slice(grouped, (first, sub_at, 0, 0), (count, 1, group, samples))
        return half.reshape(size // subs, samples)

    def from_windows(half):
        return [shift(half, "win", d) for d in range(1, windows)]

    def with_other_core(received):
        return [side for piece in received for side in (piece, shift(piece, "sub", 1))]

    def whiten_others(size, both, hint):
        return pl.pallas_call(
            others_kernel,
            out_shape=like((windows - 1, size, 2 * NB), bf16),
            in_specs=[VMEM] * (3 + len(both)),
            out_specs=VMEM,
            scratch_shapes=[pltpu.VMEM((size // (subs * group), subs, group, samples), bf16)],
            compiler_params=params(24),
            cost_estimate=hint,
            name="whiten_others",
        )(table, weights, share, *both)

    def correlate(start, size, own, white, hint):
        return pl.pallas_call(
            functools.partial(lag_kernel, factor),
            out_shape=tuple(like((span, size), bf16) for _ in ties),
            in_specs=[VMEM] * 4,
            out_specs=tuple(VMEM for _ in ties),
            compiler_params=params(24),
            cost_estimate=hint,
            name="lag_pieces",
        )(turned, own, white, mask_row[:, start:start + size])

    half = half_of(traces, *chunks[0])
    received = [from_windows(half)]
    own, weights, share, rows, table = pl.pallas_call(
        functools.partial(setup_kernel, chunks[:1]),
        out_shape=(like((chunks[0][1], 2 * NB), bf16), like((NB, NB), bf16), like((1, NB), f32))
        + (like((channels, samples), bf16), like(table.shape, bf16)),
        in_specs=[HBM, HBM, HBM],
        out_specs=(VMEM,) * 5,
        scratch_shapes=[pltpu.SemaphoreType.DMA((TABLE_PARTS + 3,)), pltpu.VMEM((1, NB), jnp.int32)],
        compiler_params=params(24),
        cost_estimate=SHORT,
        name="whiten_own",
    )(in_hbm(traces), in_hbm(table), in_hbm(after(smooth_width, half).reshape(1, NB)))
    received += [from_windows(after(rows, share)[a:a + n]) for a, n in chunks[1:]]
    near = pl.pallas_call(
        functools.partial(near_kernel, (windows, subs, per_device)),
        out_shape=like((-(-windows * per_device // 8) * 8, samples), f32),
        in_specs=[SMEM] + [VMEM] * (1 + windows),
        out_specs=VMEM,
        compiler_params=params(16),
        cost_estimate=SHORT,
        name="pick_sources",
    )(source_phase, after(mask_row, weights), half, *received[0])
    owns = [own]
    for start, size in chunks[1:]:
        owns.append(
            pl.pallas_call(
                functools.partial(own_kernel, start),
                out_shape=like((size, 2 * NB), bf16),
                in_specs=[VMEM] * 4,
                out_specs=VMEM,
                compiler_params=params(24),
                cost_estimate=LONG,
                name="whiten_own",
            )(after(rows, near), table, weights, share)
        )
    inbound = with_other_core(received[0])
    white = whiten_others(chunks[0][1], inbound, SHORT)
    if ties[1][0] == "xor":
        two = jnp.concatenate([after(near, *owns[1:]), exchange(near, blocks, ties[1])], axis=0)
        sources = [two, exchange(two, blocks, ties[2])]
    else:
        sources = [exchange(near, blocks, tie) if tie[1] else near for tie in ties]
    turned = pl.pallas_call(
        functools.partial(turn_kernel, (per_device, windows, ties, blocks)),
        out_shape=like((windows, len(ties) * span, 2 * NB), bf16),
        in_specs=[VMEM] * (4 + len(sources)),
        out_specs=VMEM,
        scratch_shapes=[pltpu.VMEM((len(ties) * near.shape[0], 2 * NB), f32)],
        compiler_params=params(24),
        cost_estimate=SHORT,
        name="turn_sources",
    )(table, weights, after(share, white), lags, *sources)
    pieces, arrived = [], []
    for i, (start, size) in enumerate(chunks):
        if i:
            white = whiten_others(size, [after(r, *pieces[-1]) for r in received[i]], LONG)
        pieces.append(correlate(start, size, owns[i], white, LONG if i else SHORT))
        ahead = arrived[-1][1:] if i else []
        sent = [after(p, *ahead) for p in pieces[-1]]
        arrived.append([exchange(p, blocks, tie, True) if tie[1] else p for tie, p in zip(ties, sent)])
    write = functools.partial(write_stack, pair_list)
    everything = [piece for group in pieces for piece in group]
    receiver_stack = write(everything, ties, blocks, per_device, channels, chunks, False, None)
    source_stack = None
    for i, (chunk, back) in enumerate(zip(chunks, arrived)):
        steps = [list(range(len(ties)))]
        if i + 1 < len(chunks):
            back = [after(b, *pieces[i + 1]) for b in back]
        elif len(ties) > 2:
            steps = [[0, 1], list(range(2, len(ties)))]
        for step in steps:
            part, part_ties = [back[at] for at in step], [ties[at] for at in step]
            source_stack = write(part, part_ties, blocks, per_device, channels, [chunk], True, source_stack)
    order = (2, 0, 1, 3)
    return (jnp.transpose(receiver_stack, order), jnp.transpose(source_stack, order))


def solution(mesh):
    in_specs = (
        P(("groups", "win"), "chan", None),
        P(("groups", "chan")),
        P(),
        P("groups"),
        P("groups", None),
    )
    out_specs = (
        P(("win", "sub"), None, None, ("groups", "chan")),
        P(("groups", "chan", "win", "sub"), None, None, None),
    )
    return jax.shard_map(
        on_device, mesh=mesh, in_specs=in_specs, out_specs=out_specs, check_vma=False
    )
```

```python
import functools
import math

import jax
import jax.numpy as jnp
import numpy as np
from jax import lax
from jax.experimental import pallas as pl
from jax.experimental.pallas import tpu as pltpu
from jax.sharding import PartitionSpec as P

NB = 512
MAXLAG = 50
STRIDE = 8
REACH = 2
VS = 8
OFFS = 5
LAGS = 2 * MAXLAG + 1
FLOOR = 0.25
TABLE_PARTS = 4
LANES = 128
VMEM = pl.BlockSpec(memory_space=pltpu.VMEM)
SMEM = pl.BlockSpec(memory_space=pltpu.SMEM)
HBM = pl.BlockSpec(memory_space=pltpu.HBM)
NT = (((1,), (1,)), ((), ()))


def dft_table(samples):
    phases = np.arange(samples)[:, None] * np.arange(NB)[None, :] % samples
    angles = phases * (2.0 * math.pi / samples)
    table = np.concatenate([np.cos(angles), -np.sin(angles)], axis=1)
    return jnp.asarray(table.astype(np.float32), jnp.bfloat16)


def side_rows(per_device):
    return -(-(MAXLAG + 1) * per_device // 8) * 8


def lag_row(tau, per_device):
    return abs(tau) * per_device + (0 if tau >= 0 else side_rows(per_device))


def lag_table(samples, per_device):
    lag = np.arange(side_rows(per_device)) // per_device
    angles = (lag[:, None] * np.arange(NB)[None, :] % samples) * (2.0 * math.pi / samples)
    table = np.concatenate([np.cos(angles), np.sin(angles)], axis=1)
    return jnp.asarray(table, jnp.float32)


def params(mib):
    return pltpu.CompilerParams(vmem_limit_bytes=mib << 20)


def cost(flops, moved):
    return pl.CostEstimate(flops=flops, bytes_accessed=moved, transcendentals=0)


SHORT, LONG = cost(1 << 20, 1 << 18), cost(1 << 33, 1 << 26)


def whiten(rows, table, weights, share):
    samples = rows.shape[1]
    spectrum = jnp.dot(rows, table, preferred_element_type=jnp.float32) * samples ** (-0.5)
    real, imag = spectrum[:, :NB], spectrum[:, NB:]
    amplitude = jnp.sqrt(real * real + imag * imag)
    high = amplitude.astype(jnp.bfloat16)
    low = (amplitude - high.astype(jnp.float32)).astype(jnp.bfloat16)
    total = jnp.dot(high, weights, preferred_element_type=jnp.float32)
    total += jnp.dot(low, weights, preferred_element_type=jnp.float32)
    gain = 1.0 / jnp.maximum(total * share, FLOOR)
    return (real * gain).astype(jnp.bfloat16), (imag * gain).astype(jnp.bfloat16)


def near_kernel(layout, phases, mask, *refs):
    windows, subs, per_device = layout
    halves, out = refs[:-1], refs[-1]
    block_at, win_at, sub_at = lax.axis_index("chan"), lax.axis_index("win"), lax.axis_index("sub")
    group = per_device * STRIDE
    rows, width = out.shape[0], halves[0].shape[0]
    phase = phases[block_at]

    def ones_at(first, width):
        row = lax.broadcasted_iota(jnp.int32, (rows, width), 0)
        place = lax.broadcasted_iota(jnp.int32, (rows, width), 1)
        return row, place == first + phase + STRIDE * (row % per_device)

    row, here = ones_at((win_at * subs + sub_at) * group, mask.shape[1])
    alive = jnp.sum(jnp.where(here, mask[...].astype(jnp.float32), 0.0), axis=1, keepdims=True)
    row, here = ones_at(win_at * group, width)
    total = jnp.zeros(out.shape, jnp.float32)
    for behind in range(windows):
        chosen = jnp.where(here & (row // per_device == behind), 1.0, 0.0).astype(jnp.bfloat16)
        total += jnp.dot(chosen, halves[behind][...], preferred_element_type=jnp.float32)
    out[...] = total * alive


def setup_kernel(chunks, traces, table, widths, *refs):
    owns, (weights, share, rows_kept, table_kept, sems, *scratch) = refs[:len(chunks)], refs[len(chunks):]
    depth = table.shape[0] // TABLE_PARTS
    needed = chunks[-1][0] + chunks[-1][1]
    rest = rows_kept.shape[0] - needed
    first_rows = pltpu.make_async_copy(traces.at[0, pl.ds(0, needed)], rows_kept.at[pl.ds(0, needed)], sems.at[TABLE_PARTS])
    first_rows.start()
    parts = []
    for i in range(TABLE_PARTS):
        span = pl.ds(i * depth, depth)
        parts.append(pltpu.make_async_copy(table.at[span], table_kept.at[span], sems.at[i]))
        parts[-1].start()
    if rest:
        span = pl.ds(needed, rest)
        last_rows = pltpu.make_async_copy(traces.at[0, span], rows_kept.at[span], sems.at[TABLE_PARTS + 1])
        last_rows.start()
    widths_kept, = scratch
    fetched = pltpu.make_async_copy(widths, widths_kept, sems.at[TABLE_PARTS + 2])
    fetched.start()
    fetched.wait()
    reach = widths_kept[...]
    near = lax.broadcasted_iota(jnp.int32, (NB, NB), 0)
    here = lax.broadcasted_iota(jnp.int32, (NB, NB), 1)
    weights[...] = jnp.where(jnp.abs(near - here) <= reach, 1.0, 0.0).astype(jnp.bfloat16)
    bins = lax.broadcasted_iota(jnp.int32, (1, NB), 1)
    count = jnp.minimum(bins + reach, NB - 1) - jnp.maximum(bins - reach, 0) + 1
    share[...] = 1.0 / count.astype(jnp.float32)
    first_rows.wait()
    for part in parts:
        part.wait()
    for (start, size), own in zip(chunks, owns):
        own_kernel(start, rows_kept, table_kept, weights, share, own)
    if rest:
        last_rows.wait()


def own_kernel(start, rows, table, weights, share, out):
    real, imag = whiten(rows[start:start + out.shape[0], :], table[...], weights[...], share[...])
    out[:, :NB] = real
    out[:, NB:] = imag


def turn_kernel(layout, table, weights, share, lags, *refs):
    per_device, windows, ties, blocks = layout
    picked, turned, spectra = refs[:-2], refs[-2], refs[-1]
    rows = jnp.concatenate([p[...] for p in picked], axis=0).astype(jnp.bfloat16)
    real, imag = whiten(rows, table[...], weights[...], share[...])
    spectra[:, :NB] = real.astype(jnp.float32)
    spectra[:, NB:] = imag.astype(jnp.float32)
    side = side_rows(per_device)
    span = 2 * side
    which = lax.broadcasted_iota(jnp.int32, (8, LANES), 0) % per_device

    def rows_of(first, lane):
        tiled = jnp.zeros((8, LANES), jnp.float32)
        for v in range(per_device):
            row = spectra[first + v:first + v + 1, lane:lane + LANES]
            tiled = jnp.where(which == v, row, tiled)
        return tiled[None]

    for lane in range(0, NB, LANES):
        cosine = lags[:, lane:lane + LANES].reshape(side // 8, 8, LANES)
        sine = lags[:, NB + lane:NB + lane + LANES].reshape(side // 8, 8, LANES)
        for at in range(len(ties)):
            for behind in range(windows):
                first = at * (spectra.shape[0] // len(ties)) + behind * per_device
                real, imag = rows_of(first, lane), rows_of(first, NB + lane)
                cr, si, sr, ci = cosine * real, sine * imag, sine * real, cosine * imag
                up = jnp.concatenate([cr - si, cr + si], axis=0).reshape(span, LANES)
                down = jnp.concatenate([ci + sr, ci - sr], axis=0).reshape(span, LANES)
                spot = pl.ds(at * span, span)
                turned[behind, spot, lane:lane + LANES] = up.astype(jnp.bfloat16)
                turned[behind, spot, NB + lane:NB + lane + LANES] = down.astype(jnp.bfloat16)


def others_kernel(table, weights, share, *refs):
    parts, (white, raw) = refs[:-2], refs[-2:]
    sub_at = lax.axis_index("sub")
    groups, _, group, samples = raw.shape
    each = len(parts) // white.shape[0]
    for i in range(white.shape[0]):
        if each == 1:
            rows = parts[i][...]
        else:
            for half, place in ((parts[2 * i], sub_at), (parts[2 * i + 1], 1 - sub_at)):
                raw[:, pl.ds(place, 1)] = half[...].reshape(groups, 1, group, samples)
            rows = raw[...].reshape(white.shape[1], samples)
        real, imag = whiten(rows, table[...], weights[...], share[...])
        white[i, :, :NB] = real
        white[i, :, NB:] = imag


def lag_kernel(factor, turned, own, white, mask, *pieces):
    total = lax.dot_general(turned[0], own[...], NT, preferred_element_type=jnp.float32)
    for i in range(white.shape[0]):
        total += lax.dot_general(turned[1 + i], white[i], NT, preferred_element_type=jnp.float32)
    result = total * (mask[...].astype(jnp.float32) * factor)
    span = result.shape[0] // len(pieces)
    for at, piece in enumerate(pieces):
        piece[...] = result[at * span:(at + 1) * span, :].astype(jnp.bfloat16)


def stack_kernel(layout, pairs, *refs):
    ties, blocks, per_device, chunks, reverse, chained = layout
    count = len(ties)
    pieces = refs[:count * len(chunks)]
    out, wide, stage, sems = refs[count * len(chunks) + chained:]
    block_at = lax.axis_index("chan")
    first, width = chunks[0][0], stage.shape[3]
    lanes = pl.ds(first, width)
    listed = pairs[...].astype(jnp.float32)
    row = lax.broadcasted_iota(jnp.int32, listed.shape, 0)
    column = lax.broadcasted_iota(jnp.int32, listed.shape, 1)
    copies = []
    for at, tie in enumerate(ties):
        for i, (start, size) in enumerate(chunks):
            wide[at, :, start - first:start - first + size] = pieces[i * count + at][...].astype(jnp.float32)
        block = block_at if reverse else partner(block_at, blocks, tie)
        for e in offsets_of(block_at, blocks, tie, reverse):
            chosen = jnp.where((row == block) & (column == e), listed, 0.0)
            pair = jnp.broadcast_to(jnp.sum(chosen, keepdims=True), (per_device, width))
            slot = len(copies)
            for t in range(LAGS):
                tau = MAXLAG - t if reverse else t - MAXLAG
                spot = lag_row(tau, per_device)
                stage[slot, t] = wide[at, spot:spot + per_device, :] * pair
            copies.append(pltpu.make_async_copy(stage.at[slot], out.at[e, :, :, lanes], sems.at[slot]))
            copies[-1].start()
    for copy in copies:
        copy.wait()


def ties_of(blocks):
    if blocks == 4:
        return [("xor", i) for i in range(4)]
    ties = []
    for moved in (0, 1, -1, 2, -2):
        if all((m - moved) % blocks for _, m in ties):
            ties.append(("shift", moved))
    return ties


def partner(block, blocks, tie, back=False):
    kind, step = tie
    if kind == "xor":
        return block ^ step
    return (block + (step if back else -step) + blocks) % blocks


def offsets_of(block, blocks, tie, back):
    kind, step = tie
    if kind == "shift":
        return [e for e in range(OFFS) if (e - REACH - step) % blocks == 0]
    if step % 2 == 0:
        return [e for e in range(OFFS) if abs(e - REACH) == step]
    ahead = (block ^ step) - block if back else block - (block ^ step)
    return [jnp.where((ahead + blocks) % blocks == 1, REACH + 1, REACH - 1)]


def exchange(value, blocks, tie, back=False):
    return lax.ppermute(value, "chan", [(partner(b, blocks, tie, back), b) for b in range(blocks)])


def chunks_of(channels):
    if channels < 2 * LANES or channels % LANES:
        return [(0, channels)]
    first = channels * 2 // 5 // LANES * LANES
    return [(0, first), (first, channels - first)]


def shift(block, axis, distance):
    count = lax.axis_size(axis)
    return lax.ppermute(block, axis, [(i, (i + distance) % count) for i in range(count)])


def write_stack(pair_list, pieces, ties, blocks, per_device, channels, chunks, reverse, prior):
    width = sum(size for _, size in chunks)
    span = 2 * side_rows(per_device)
    slots = sum(len(offsets_of(0, blocks, tie, reverse)) for tie in ties)
    chained = [] if prior is None else [prior]
    operands = len(pieces) + 1
    return pl.pallas_call(
        functools.partial(
            stack_kernel, (ties, blocks, per_device, chunks, reverse, len(chained))
        ),
        out_shape=jax.ShapeDtypeStruct((OFFS, LAGS, per_device, channels), jnp.float32),
        in_specs=[VMEM] * operands + [HBM] * len(chained),
        out_specs=HBM,
        scratch_shapes=[
            pltpu.VMEM((len(ties), span, width), jnp.float32),
            pltpu.VMEM((slots, LAGS, per_device, width), jnp.float32),
            pltpu.SemaphoreType.DMA((slots,)),
        ],
        input_output_aliases={operands: 0} if chained else {},
        compiler_params=params(16),
        cost_estimate=SHORT if reverse else LONG,
        name="source_order" if reverse else "receiver_order",
    )(pair_list, *pieces, *chained)


def in_hbm(value):
    return pltpu.with_memory_space_constraint(value, pltpu.HBM)


def after(value, *others):
    return lax.optimization_barrier((value, *others))[0]


def on_device(traces, channel_mask, smooth_width, source_phase, pair_list):
    _, channels, samples = traces.shape
    blocks, windows, subs = (lax.axis_size(a) for a in ("chan", "win", "sub"))
    sub_at = lax.axis_index("sub")
    per_device = VS // (windows * subs)
    group = per_device * STRIDE
    ties = ties_of(blocks)
    span = 2 * side_rows(per_device)
    chunks = chunks_of(channels)
    table, lags = dft_table(samples), lag_table(samples, per_device)
    factor = (NB * windows) ** (-0.5)
    bf16, f32 = jnp.bfloat16, jnp.float32
    like = jax.ShapeDtypeStruct
    mask_row = channel_mask.reshape(1, channels)

    def half_of(rows, start, size):
        grouped = rows.reshape(channels // (subs * group), subs, group, samples)
        first, count = start // (subs * group), size // (subs * group)
        half = lax.dynamic_slice(grouped, (first, sub_at, 0, 0), (count, 1, group, samples))
        return half.reshape(size // subs, samples)

    def from_windows(half):
        return [shift(half, "win", d) for d in range(1, windows)]

    def with_other_core(received):
        return [side for piece in received for side in (piece, shift(piece, "sub", 1))]

    def whiten_others(size, both, hint):
        return pl.pallas_call(
            others_kernel,
            out_shape=like((windows - 1, size, 2 * NB), bf16),
            in_specs=[VMEM] * (3 + len(both)),
            out_specs=VMEM,
            scratch_shapes=[pltpu.VMEM((size // (subs * group), subs, group, samples), bf16)],
            compiler_params=params(24),
            cost_estimate=hint,
            name="whiten_others",
        )(table, weights, share, *both)

    def correlate(start, size, own, white, hint):
        return pl.pallas_call(
            functools.partial(lag_kernel, factor),
            out_shape=tuple(like((span, size), bf16) for _ in ties),
            in_specs=[VMEM] * 4,
            out_specs=tuple(VMEM for _ in ties),
            compiler_params=params(24),
            cost_estimate=hint,
            name="lag_pieces",
        )(turned, own, white, mask_row[:, start:start + size])

    half = half_of(traces, *chunks[0])
    received = [from_windows(half)]
    own, weights, share, rows, table = pl.pallas_call(
        functools.partial(setup_kernel, chunks[:1]),
        out_shape=(like((chunks[0][1], 2 * NB), bf16), like((NB, NB), bf16), like((1, NB), f32))
        + (like((channels, samples), bf16), like(table.shape, bf16)),
        in_specs=[HBM, HBM, HBM],
        out_specs=(VMEM,) * 5,
        scratch_shapes=[pltpu.SemaphoreType.DMA((TABLE_PARTS + 3,)), pltpu.VMEM((1, NB), jnp.int32)],
        compiler_params=params(24),
        cost_estimate=SHORT,
        name="whiten_own",
    )(in_hbm(traces), in_hbm(table), in_hbm(after(smooth_width, half).reshape(1, NB)))
    received += [from_windows(after(rows, share)[a:a + n]) for a, n in chunks[1:]]
    near = pl.pallas_call(
        functools.partial(near_kernel, (windows, subs, per_device)),
        out_shape=like((-(-windows * per_device // 8) * 8, samples), f32),
        in_specs=[SMEM] + [VMEM] * (1 + windows),
        out_specs=VMEM,
        compiler_params=params(16),
        cost_estimate=SHORT,
        name="pick_sources",
    )(source_phase, after(mask_row, weights), half, *received[0])
    owns = [own]
    for start, size in chunks[1:]:
        owns.append(
            pl.pallas_call(
                functools.partial(own_kernel, start),
                out_shape=like((size, 2 * NB), bf16),
                in_specs=[VMEM] * 4,
                out_specs=VMEM,
                compiler_params=params(24),
                cost_estimate=LONG,
                name="whiten_own",
            )(after(rows, near), table, weights, share)
        )
    inbound = with_other_core(received[0])
    white = whiten_others(chunks[0][1], inbound, SHORT)
    if ties[1][0] == "xor":
        two = jnp.concatenate([after(near, *owns[1:]), exchange(near, blocks, ties[1])], axis=0)
        sources = [two, exchange(two, blocks, ties[2])]
    else:
        sources = [exchange(near, blocks, tie) if tie[1] else near for tie in ties]
    turned = pl.pallas_call(
        functools.partial(turn_kernel, (per_device, windows, ties, blocks)),
        out_shape=like((windows, len(ties) * span, 2 * NB), bf16),
        in_specs=[VMEM] * (4 + len(sources)),
        out_specs=VMEM,
        scratch_shapes=[pltpu.VMEM((len(ties) * near.shape[0], 2 * NB), f32)],
        compiler_params=params(24),
        cost_estimate=SHORT,
        name="turn_sources",
    )(table, weights, after(share, white), lags, *sources)
    pieces, arrived = [], []
    for i, (start, size) in enumerate(chunks):
        if i:
            white = whiten_others(size, [after(r, *pieces[-1]) for r in received[i]], LONG)
        pieces.append(correlate(start, size, owns[i], white, LONG if i else SHORT))
        ahead = arrived[-1][-1:] if i else []
        sent = [after(p, *ahead) for p in pieces[-1]]
        arrived.append([exchange(p, blocks, tie, True) if tie[1] else p for tie, p in zip(ties, sent)])
    write = functools.partial(write_stack, pair_list)
    everything = [piece for group in pieces for piece in group]
    receiver_stack = write(everything, ties, blocks, per_device, channels, chunks, False, None)
    source_stack = None
    for i, (chunk, back) in enumerate(zip(chunks, arrived)):
        if i + 1 < len(chunks):
            back = [after(b, *pieces[i + 1]) for b in back]
        source_stack = write(back, ties, blocks, per_device, channels, [chunk], True, source_stack)
    order = (2, 0, 1, 3)
    return (jnp.transpose(receiver_stack, order), jnp.transpose(source_stack, order))


def solution(mesh):
    in_specs = (
        P(("groups", "win"), "chan", None),
        P(("groups", "chan")),
        P(),
        P("groups"),
        P("groups", None),
    )
    out_specs = (
        P(("win", "sub"), None, None, ("groups", "chan")),
        P(("groups", "chan", "win", "sub"), None, None, None),
    )
    return jax.shard_map(
        on_device, mesh=mesh, in_specs=in_specs, out_specs=out_specs, check_vma=False
    )
```

```python
import functools
import math

import jax
import jax.numpy as jnp
import numpy as np
from jax import lax
from jax.experimental import pallas as pl
from jax.experimental.pallas import tpu as pltpu
from jax.sharding import PartitionSpec as P

NB = 512
MAXLAG = 50
STRIDE = 8
REACH = 2
VS = 8
OFFS = 5
LAGS = 2 * MAXLAG + 1
FLOOR = 0.25
TABLE_PARTS = 4
LANES = 128
VMEM = pl.BlockSpec(memory_space=pltpu.VMEM)
SMEM = pl.BlockSpec(memory_space=pltpu.SMEM)
HBM = pl.BlockSpec(memory_space=pltpu.HBM)
NT = (((1,), (1,)), ((), ()))


def dft_table(samples):
    phases = np.arange(samples)[:, None] * np.arange(NB)[None, :] % samples
    angles = phases * (2.0 * math.pi / samples)
    table = np.concatenate([np.cos(angles), -np.sin(angles)], axis=1)
    return jnp.asarray(table.astype(np.float32), jnp.bfloat16)


def side_rows(per_device):
    return -(-(MAXLAG + 1) * per_device // 8) * 8


def lag_row(tau, per_device):
    return abs(tau) * per_device + (0 if tau >= 0 else side_rows(per_device))


def lag_table(samples, per_device):
    lag = np.arange(side_rows(per_device)) // per_device
    angles = (lag[:, None] * np.arange(NB)[None, :] % samples) * (2.0 * math.pi / samples)
    table = np.concatenate([np.cos(angles), np.sin(angles)], axis=1)
    return jnp.asarray(table, jnp.float32)


def params(mib):
    return pltpu.CompilerParams(vmem_limit_bytes=mib << 20)


def cost(flops, moved):
    return pl.CostEstimate(flops=flops, bytes_accessed=moved, transcendentals=0)


SHORT, LONG = cost(1 << 20, 1 << 18), cost(1 << 33, 1 << 26)


def whiten(rows, table, weights, share):
    samples = rows.shape[1]
    spectrum = jnp.dot(rows, table, preferred_element_type=jnp.float32) * samples ** (-0.5)
    real, imag = spectrum[:, :NB], spectrum[:, NB:]
    amplitude = jnp.sqrt(real * real + imag * imag)
    high = amplitude.astype(jnp.bfloat16)
    low = (amplitude - high.astype(jnp.float32)).astype(jnp.bfloat16)
    total = jnp.dot(high, weights, preferred_element_type=jnp.float32)
    total += jnp.dot(low, weights, preferred_element_type=jnp.float32)
    gain = 1.0 / jnp.maximum(total * share, FLOOR)
    return (real * gain).astype(jnp.bfloat16), (imag * gain).astype(jnp.bfloat16)


def near_kernel(layout, phases, mask, *refs):
    windows, subs, per_device = layout
    halves, out = refs[:-1], refs[-1]
    block_at, win_at, sub_at = lax.axis_index("chan"), lax.axis_index("win"), lax.axis_index("sub")
    group = per_device * STRIDE
    rows, width = out.shape[0], halves[0].shape[0]
    phase = phases[block_at]

    def ones_at(first, width):
        row = lax.broadcasted_iota(jnp.int32, (rows, width), 0)
        place = lax.broadcasted_iota(jnp.int32, (rows, width), 1)
        return row, place == first + phase + STRIDE * (row % per_device)

    row, here = ones_at((win_at * subs + sub_at) * group, mask.shape[1])
    alive = jnp.sum(jnp.where(here, mask[...].astype(jnp.float32), 0.0), axis=1, keepdims=True)
    row, here = ones_at(win_at * group, width)
    total = jnp.zeros(out.shape, jnp.float32)
    for behind in range(windows):
        chosen = jnp.where(here & (row // per_device == behind), 1.0, 0.0).astype(jnp.bfloat16)
        total += jnp.dot(chosen, halves[behind][...], preferred_element_type=jnp.float32)
    out[...] = total * alive


def setup_kernel(chunks, traces, table, widths, *refs):
    owns, (weights, share, rows_kept, table_kept, sems, *scratch) = refs[:len(chunks)], refs[len(chunks):]
    depth = table.shape[0] // TABLE_PARTS
    needed = chunks[-1][0] + chunks[-1][1]
    rest = rows_kept.shape[0] - needed
    first_rows = pltpu.make_async_copy(traces.at[0, pl.ds(0, needed)], rows_kept.at[pl.ds(0, needed)], sems.at[TABLE_PARTS])
    first_rows.start()
    parts = []
    for i in range(TABLE_PARTS):
        span = pl.ds(i * depth, depth)
        parts.append(pltpu.make_async_copy(table.at[span], table_kept.at[span], sems.at[i]))
        parts[-1].start()
    if rest:
        span = pl.ds(needed, rest)
        last_rows = pltpu.make_async_copy(traces.at[0, span], rows_kept.at[span], sems.at[TABLE_PARTS + 1])
        last_rows.start()
    widths_kept, = scratch
    fetched = pltpu.make_async_copy(widths, widths_kept, sems.at[TABLE_PARTS + 2])
    fetched.start()
    fetched.wait()
    reach = widths_kept[...]
    near = lax.broadcasted_iota(jnp.int32, (NB, NB), 0)
    here = lax.broadcasted_iota(jnp.int32, (NB, NB), 1)
    weights[...] = jnp.where(jnp.abs(near - here) <= reach, 1.0, 0.0).astype(jnp.bfloat16)
    bins = lax.broadcasted_iota(jnp.int32, (1, NB), 1)
    count = jnp.minimum(bins + reach, NB - 1) - jnp.maximum(bins - reach, 0) + 1
    share[...] = 1.0 / count.astype(jnp.float32)
    first_rows.wait()
    for part in parts:
        part.wait()
    for (start, size), own in zip(chunks, owns):
        own_kernel(start, rows_kept, table_kept, weights, share, own)
    if rest:
        last_rows.wait()


def own_kernel(start, rows, table, weights, share, out):
    real, imag = whiten(rows[start:start + out.shape[0], :], table[...], weights[...], share[...])
    out[:, :NB] = real
    out[:, NB:] = imag


def turn_kernel(layout, table, weights, share, lags, *refs):
    per_device, windows, count = layout
    picked, turned, spectra = refs[:-2], refs[-2], refs[-1]
    rows = jnp.concatenate([p[...].astype(jnp.float32) for p in picked], axis=0).astype(jnp.bfloat16)
    real, imag = whiten(rows, table[...], weights[...], share[...])
    spectra[:, :NB] = real.astype(jnp.float32)
    spectra[:, NB:] = imag.astype(jnp.float32)
    side = side_rows(per_device)
    span = 2 * side
    which = lax.broadcasted_iota(jnp.int32, (8, LANES), 0) % per_device

    def rows_of(first, lane):
        tiled = jnp.zeros((8, LANES), jnp.float32)
        for v in range(per_device):
            row = spectra[first + v:first + v + 1, lane:lane + LANES]
            tiled = jnp.where(which == v, row, tiled)
        return tiled[None]

    for lane in range(0, NB, LANES):
        cosine = lags[:, lane:lane + LANES].reshape(side // 8, 8, LANES)
        sine = lags[:, NB + lane:NB + lane + LANES].reshape(side // 8, 8, LANES)
        for at in range(count):
            for behind in range(windows):
                first = (at * windows + behind) * per_device
                real, imag = rows_of(first, lane), rows_of(first, NB + lane)
                cr, si, sr, ci = cosine * real, sine * imag, sine * real, cosine * imag
                up = jnp.concatenate([cr - si, cr + si], axis=0).reshape(span, LANES)
                down = jnp.concatenate([ci + sr, ci - sr], axis=0).reshape(span, LANES)
                spot = pl.ds(at * span, span)
                turned[behind, spot, lane:lane + LANES] = up.astype(jnp.bfloat16)
                turned[behind, spot, NB + lane:NB + lane + LANES] = down.astype(jnp.bfloat16)


def others_kernel(table, weights, share, *refs):
    parts, (white, raw) = refs[:-2], refs[-2:]
    sub_at = lax.axis_index("sub")
    groups, _, group, samples = raw.shape
    each = len(parts) // white.shape[0]
    for i in range(white.shape[0]):
        if each == 1:
            rows = parts[i][...]
        else:
            for half, place in ((parts[2 * i], sub_at), (parts[2 * i + 1], 1 - sub_at)):
                raw[:, pl.ds(place, 1)] = half[...].reshape(groups, 1, group, samples)
            rows = raw[...].reshape(white.shape[1], samples)
        real, imag = whiten(rows, table[...], weights[...], share[...])
        white[i, :, :NB] = real
        white[i, :, NB:] = imag


def lag_product(turned, own, white):
    total = lax.dot_general(turned[0], own[...], NT, preferred_element_type=jnp.float32)
    for i in range(white.shape[0]):
        total += lax.dot_general(turned[1 + i], white[i], NT, preferred_element_type=jnp.float32)
    return total


def lag_kernel(factor, turned, own, white, mask, *pieces):
    result = lag_product(turned, own, white) * (mask[...].astype(jnp.float32) * factor)
    span = result.shape[0] // len(pieces)
    for at, piece in enumerate(pieces):
        piece[...] = result[at * span:(at + 1) * span, :].astype(jnp.bfloat16)


def put_slots(layout, listed, wide, out, stage, sems, slot):
    tie, blocks, per_device, first, reverse = layout
    block_at = lax.axis_index("chan")
    row = lax.broadcasted_iota(jnp.int32, listed.shape, 0)
    column = lax.broadcasted_iota(jnp.int32, listed.shape, 1)
    width = stage.shape[3]
    block = block_at if reverse else partner(block_at, blocks, tie)
    copies = []
    for e in offsets_of(block_at, blocks, tie, reverse):
        chosen = jnp.where((row == block) & (column == e), listed, 0.0)
        pair = jnp.broadcast_to(jnp.sum(chosen, keepdims=True), (per_device, width))
        for t in range(LAGS):
            tau = MAXLAG - t if reverse else t - MAXLAG
            spot = lag_row(tau, per_device)
            stage[slot, t] = wide[spot:spot + per_device, :] * pair
        target = out.at[e, :, :, pl.ds(first, width)]
        copies.append(pltpu.make_async_copy(stage.at[slot], target, sems.at[slot]))
        copies[-1].start()
        slot += 1
    return copies


def receiver_kernel(layout, pairs, turned, mask, *refs):
    ties, blocks, per_device, chunks, factor = layout
    count = len(chunks)
    owns, whites, pieces = refs[:count], refs[count:2 * count], refs[2 * count:-5]
    out, source_out, wide, stage, sems = refs[-5:]
    listed = pairs[...].astype(jnp.float32)
    copies = []
    for at, tie in enumerate(ties):
        for i, (start, size) in enumerate(chunks):
            lanes = slice(start, start + size)
            if at:
                wide[at, :, lanes] = pieces[i * (len(ties) - 1) + at - 1][...].astype(jnp.float32)
            else:
                wide[at, :, lanes] = lag_product(turned, owns[i], whites[i]) * (mask[:, lanes].astype(jnp.float32) * factor)
        turns = [(out, False)] + ([] if at else [(source_out, True)])
        for target, reverse in turns:
            part = (tie, blocks, per_device, 0, reverse)
            copies += put_slots(part, listed, wide.at[at], target, stage, sems, len(copies))
    for copy in copies:
        copy.wait()


def source_kernel(layout, pairs, *refs):
    ties, blocks, per_device, first = layout
    pieces, (_, out, wide, stage, sems) = refs[:len(ties)], refs[len(ties):]
    listed = pairs[...].astype(jnp.float32)
    copies = []
    for at, tie in enumerate(ties):
        wide[at] = pieces[at][...].astype(jnp.float32)
        part = (tie, blocks, per_device, first, True)
        copies += put_slots(part, listed, wide.at[at], out, stage, sems, len(copies))
    for copy in copies:
        copy.wait()


def ties_of(blocks):
    if blocks == 4:
        return [("xor", i) for i in range(4)]
    ties = []
    for moved in (0, 1, -1, 2, -2):
        if all((m - moved) % blocks for _, m in ties):
            ties.append(("shift", moved))
    return ties


def partner(block, blocks, tie, back=False):
    kind, step = tie
    if kind == "xor":
        return block ^ step
    return (block + (step if back else -step) + blocks) % blocks


def offsets_of(block, blocks, tie, back):
    kind, step = tie
    if kind == "shift":
        return [e for e in range(OFFS) if (e - REACH - step) % blocks == 0]
    if step % 2 == 0:
        return [e for e in range(OFFS) if abs(e - REACH) == step]
    ahead = (block ^ step) - block if back else block - (block ^ step)
    return [jnp.where((ahead + blocks) % blocks == 1, REACH + 1, REACH - 1)]


def exchange(value, blocks, tie, back=False):
    return lax.ppermute(value, "chan", [(partner(b, blocks, tie, back), b) for b in range(blocks)])


def chunks_of(channels):
    if channels < 2 * LANES or channels % LANES:
        return [(0, channels)]
    first = channels * 2 // 5 // LANES * LANES
    return [(0, first), (first, channels - first)]


def shift(block, axis, distance):
    count = lax.axis_size(axis)
    return lax.ppermute(block, axis, [(i, (i + distance) % count) for i in range(count)])


def slots_of(ties, blocks):
    return sum(len(offsets_of(0, blocks, tie, False)) for tie in ties)


def in_hbm(value):
    return pltpu.with_memory_space_constraint(value, pltpu.HBM)


def after(value, *others):
    return lax.optimization_barrier((value, *others))[0]


def on_device(traces, channel_mask, smooth_width, source_phase, pair_list):
    _, channels, samples = traces.shape
    blocks, windows, subs = (lax.axis_size(a) for a in ("chan", "win", "sub"))
    sub_at = lax.axis_index("sub")
    per_device = VS // (windows * subs)
    group = per_device * STRIDE
    ties = ties_of(blocks)
    span = 2 * side_rows(per_device)
    chunks = chunks_of(channels)
    table, lags = dft_table(samples), lag_table(samples, per_device)
    factor = (NB * windows) ** (-0.5)
    bf16, f32 = jnp.bfloat16, jnp.float32
    like = jax.ShapeDtypeStruct
    mask_row = channel_mask.reshape(1, channels)

    def half_of(rows, start, size):
        grouped = rows.reshape(channels // (subs * group), subs, group, samples)
        first, count = start // (subs * group), size // (subs * group)
        half = lax.dynamic_slice(grouped, (first, sub_at, 0, 0), (count, 1, group, samples))
        return half.reshape(size // subs, samples)

    def from_windows(half):
        return [shift(half, "win", d) for d in range(1, windows)]

    def with_other_core(received):
        return [side for piece in received for side in (piece, shift(piece, "sub", 1))]

    def whiten_others(size, both, hint):
        return pl.pallas_call(
            others_kernel,
            out_shape=like((windows - 1, size, 2 * NB), bf16),
            in_specs=[VMEM] * (3 + len(both)),
            out_specs=VMEM,
            scratch_shapes=[pltpu.VMEM((size // (subs * group), subs, group, samples), bf16)],
            compiler_params=params(24),
            cost_estimate=hint,
            name="whiten_others",
        )(table, weights, share, *both)

    def correlate(start, size, turned, own, white, hint):
        count = turned.shape[1] // span
        return pl.pallas_call(
            functools.partial(lag_kernel, factor),
            out_shape=tuple(like((span, size), bf16) for _ in range(count)),
            in_specs=[VMEM] * 4,
            out_specs=(VMEM,) * count,
            compiler_params=params(24),
            cost_estimate=hint,
            name="lag_pieces",
        )(turned, own, white, mask_row[:, start:start + size])

    half = half_of(traces, *chunks[0])
    received = [from_windows(half)]
    *owns, weights, share, rows, table = pl.pallas_call(
        functools.partial(setup_kernel, chunks),
        out_shape=tuple(like((size, 2 * NB), bf16) for _, size in chunks)
        + (like((NB, NB), bf16), like((1, NB), f32))
        + (like((channels, samples), bf16), like(table.shape, bf16)),
        in_specs=[HBM, HBM, HBM],
        out_specs=(VMEM,) * (len(chunks) + 4),
        scratch_shapes=[pltpu.SemaphoreType.DMA((TABLE_PARTS + 3,)), pltpu.VMEM((1, NB), jnp.int32)],
        compiler_params=params(24),
        cost_estimate=SHORT,
        name="whiten_own",
    )(in_hbm(traces), in_hbm(table), in_hbm(after(smooth_width, half).reshape(1, NB)))
    received += [from_windows(after(rows, *received[0])[a:a + n]) for a, n in chunks[1:]]
    near = pl.pallas_call(
        functools.partial(near_kernel, (windows, subs, per_device)),
        out_shape=like((windows * per_device, samples), f32),
        in_specs=[SMEM] + [VMEM] * (1 + windows),
        out_specs=VMEM,
        compiler_params=params(16),
        cost_estimate=SHORT,
        name="pick_sources",
    )(source_phase, after(mask_row, weights), half, *received[0])

    def turn(sources, which, hint, *first):
        rows_each = windows * per_device
        return pl.pallas_call(
            functools.partial(turn_kernel, (per_device, windows, len(which))),
            out_shape=like((windows, len(which) * span, 2 * NB), bf16),
            in_specs=[VMEM] * (4 + len(sources)),
            out_specs=VMEM,
            scratch_shapes=[pltpu.VMEM((len(which) * rows_each, 2 * NB), f32)],
            compiler_params=params(24),
            cost_estimate=hint,
            name="turn_sources",
        )(table, weights, after(share, *first), lags, *sources)

    turned_own = turn([near], ties[:1], LONG)
    inbound = with_other_core(received[0])
    white = whiten_others(chunks[0][1], inbound, SHORT)
    if ties[1][0] == "xor":
        beside = exchange(near, blocks, ties[1])
        two = jnp.concatenate([after(near, turned_own), beside], axis=0).astype(bf16)
        sources = [beside, exchange(two, blocks, ties[2])]
    else:
        sources = [exchange(near, blocks, tie) for tie in ties[1:]]
    turned = turn(sources, ties[1:], SHORT, white)
    pieces, arrived, whites = [], [], [white]
    for i, (start, size) in enumerate(chunks):
        if i:
            whites.append(whiten_others(size, [after(r, *pieces[-1]) for r in received[i]], LONG))
        pieces.append(correlate(start, size, turned, owns[i], whites[i], LONG if i else SHORT))
        ahead = arrived[-1][-1:] if i else []
        sent = [after(p, *ahead) for p in pieces[-1]]
        arrived.append([exchange(p, blocks, tie, True) for tie, p in zip(ties[1:], sent)])
    stack = like((OFFS, LAGS, per_device, channels), f32)

    def scratch(count, slots, width):
        return [
            pltpu.VMEM((count, span, width), f32),
            pltpu.VMEM((slots, LAGS, per_device, width), f32),
            pltpu.SemaphoreType.DMA((slots,)),
        ]

    remote = [piece for group in pieces for piece in group]
    receiver_stack, source_stack = pl.pallas_call(
        functools.partial(receiver_kernel, (ties, blocks, per_device, chunks, factor)),
        out_shape=(stack, stack),
        in_specs=[VMEM] * (3 + 2 * len(chunks) + len(remote)),
        out_specs=(HBM, HBM),
        scratch_shapes=scratch(len(ties), slots_of(ties, blocks) + 1, channels),
        compiler_params=params(24),
        cost_estimate=LONG,
        name="receiver_order",
    )(pair_list, turned_own, mask_row, *owns, *whites, *remote)
    slots = slots_of(ties[1:], blocks)
    for (start, size), back in zip(chunks, arrived):
        source_stack = pl.pallas_call(
            functools.partial(source_kernel, (ties[1:], blocks, per_device, start)),
            out_shape=stack,
            in_specs=[VMEM] * (1 + len(back)) + [HBM],
            out_specs=HBM,
            scratch_shapes=scratch(len(back), slots, size),
            input_output_aliases={1 + len(back): 0},
            compiler_params=params(16),
            cost_estimate=SHORT,
            name="source_order",
        )(pair_list, *back, source_stack)
    order = (2, 0, 1, 3)
    return (jnp.transpose(receiver_stack, order), jnp.transpose(source_stack, order))


def solution(mesh):
    in_specs = (
        P(("groups", "win"), "chan", None),
        P(("groups", "chan")),
        P(),
        P("groups"),
        P("groups", None),
    )
    out_specs = (
        P(("win", "sub"), None, None, ("groups", "chan")),
        P(("groups", "chan", "win", "sub"), None, None, None),
    )
    return jax.shard_map(
        on_device, mesh=mesh, in_specs=in_specs, out_specs=out_specs, check_vma=False
    )
```

```python
import functools
import math

import jax
import jax.numpy as jnp
import numpy as np
from jax import lax
from jax.experimental import pallas as pl
from jax.experimental.pallas import tpu as pltpu
from jax.sharding import PartitionSpec as P

NB = 512
MAXLAG = 50
STRIDE = 8
REACH = 2
VS = 8
OFFS = 5
LAGS = 2 * MAXLAG + 1
FLOOR = 0.25
TABLE_PARTS = 4
LANES = 128
VMEM = pl.BlockSpec(memory_space=pltpu.VMEM)
SMEM = pl.BlockSpec(memory_space=pltpu.SMEM)
HBM = pl.BlockSpec(memory_space=pltpu.HBM)
NT = (((1,), (1,)), ((), ()))


def dft_table(samples):
    phases = np.arange(samples)[:, None] * np.arange(NB)[None, :] % samples
    angles = phases * (2.0 * math.pi / samples)
    table = np.concatenate([np.cos(angles), -np.sin(angles)], axis=1)
    return jnp.asarray(table.astype(np.float32), jnp.bfloat16)


def side_rows(per_device):
    return -(-(MAXLAG + 1) * per_device // 8) * 8


def lag_row(tau, per_device):
    return abs(tau) * per_device + (0 if tau >= 0 else side_rows(per_device))


def lag_table(samples, per_device):
    lag = np.arange(side_rows(per_device)) // per_device
    angles = (lag[:, None] * np.arange(NB)[None, :] % samples) * (2.0 * math.pi / samples)
    table = np.concatenate([np.cos(angles), np.sin(angles)], axis=1)
    return jnp.asarray(table, jnp.float32)


def params(mib):
    return pltpu.CompilerParams(vmem_limit_bytes=mib << 20)


def cost(flops, moved):
    return pl.CostEstimate(flops=flops, bytes_accessed=moved, transcendentals=0)


SHORT, LONG = cost(1 << 20, 1 << 18), cost(1 << 33, 1 << 26)


def whiten(rows, table, weights, share):
    samples = rows.shape[1]
    spectrum = jnp.dot(rows, table, preferred_element_type=jnp.float32) * samples ** (-0.5)
    real, imag = spectrum[:, :NB], spectrum[:, NB:]
    amplitude = jnp.sqrt(real * real + imag * imag)
    high = amplitude.astype(jnp.bfloat16)
    low = (amplitude - high.astype(jnp.float32)).astype(jnp.bfloat16)
    total = jnp.dot(high, weights, preferred_element_type=jnp.float32)
    total += jnp.dot(low, weights, preferred_element_type=jnp.float32)
    gain = 1.0 / jnp.maximum(total * share, FLOOR)
    return (real * gain).astype(jnp.bfloat16), (imag * gain).astype(jnp.bfloat16)


def near_kernel(layout, phases, mask, *refs):
    windows, subs, per_device = layout
    halves, out = refs[:-1], refs[-1]
    block_at, win_at, sub_at = lax.axis_index("chan"), lax.axis_index("win"), lax.axis_index("sub")
    group = per_device * STRIDE
    rows, width = out.shape[0], halves[0].shape[0]
    phase = phases[block_at]

    def ones_at(first, width):
        row = lax.broadcasted_iota(jnp.int32, (rows, width), 0)
        place = lax.broadcasted_iota(jnp.int32, (rows, width), 1)
        return row, place == first + phase + STRIDE * (row % per_device)

    row, here = ones_at((win_at * subs + sub_at) * group, mask.shape[1])
    alive = jnp.sum(jnp.where(here, mask[...].astype(jnp.float32), 0.0), axis=1, keepdims=True)
    row, here = ones_at(win_at * group, width)
    total = jnp.zeros(out.shape, jnp.float32)
    for behind in range(windows):
        chosen = jnp.where(here & (row // per_device == behind), 1.0, 0.0).astype(jnp.bfloat16)
        total += jnp.dot(chosen, halves[behind][...], preferred_element_type=jnp.float32)
    out[...] = total * alive


def setup_kernel(chunks, traces, table, widths, *refs):
    owns, (weights, share, rows_kept, table_kept, sems, *scratch) = refs[:len(chunks)], refs[len(chunks):]
    depth = table.shape[0] // TABLE_PARTS
    needed = chunks[-1][0] + chunks[-1][1]
    rest = rows_kept.shape[0] - needed
    first_rows = pltpu.make_async_copy(traces.at[0, pl.ds(0, needed)], rows_kept.at[pl.ds(0, needed)], sems.at[TABLE_PARTS])
    first_rows.start()
    parts = []
    for i in range(TABLE_PARTS):
        span = pl.ds(i * depth, depth)
        parts.append(pltpu.make_async_copy(table.at[span], table_kept.at[span], sems.at[i]))
        parts[-1].start()
    if rest:
        span = pl.ds(needed, rest)
        last_rows = pltpu.make_async_copy(traces.at[0, span], rows_kept.at[span], sems.at[TABLE_PARTS + 1])
        last_rows.start()
    widths_kept, = scratch
    fetched = pltpu.make_async_copy(widths, widths_kept, sems.at[TABLE_PARTS + 2])
    fetched.start()
    fetched.wait()
    reach = widths_kept[...]
    near = lax.broadcasted_iota(jnp.int32, (NB, NB), 0)
    here = lax.broadcasted_iota(jnp.int32, (NB, NB), 1)
    weights[...] = jnp.where(jnp.abs(near - here) <= reach, 1.0, 0.0).astype(jnp.bfloat16)
    bins = lax.broadcasted_iota(jnp.int32, (1, NB), 1)
    count = jnp.minimum(bins + reach, NB - 1) - jnp.maximum(bins - reach, 0) + 1
    share[...] = 1.0 / count.astype(jnp.float32)
    first_rows.wait()
    for part in parts:
        part.wait()
    for (start, size), own in zip(chunks, owns):
        own_kernel(start, rows_kept, table_kept, weights, share, own)
    if rest:
        last_rows.wait()


def own_kernel(start, rows, table, weights, share, out):
    real, imag = whiten(rows[start:start + out.shape[0], :], table[...], weights[...], share[...])
    out[:, :NB] = real
    out[:, NB:] = imag


def turn_kernel(layout, table, weights, share, lags, *refs):
    per_device, windows, count = layout
    picked, turned, spectra = refs[:-2], refs[-2], refs[-1]
    rows = jnp.concatenate([p[...].astype(jnp.float32) for p in picked], axis=0).astype(jnp.bfloat16)
    real, imag = whiten(rows, table[...], weights[...], share[...])
    spectra[:, :NB] = real.astype(jnp.float32)
    spectra[:, NB:] = imag.astype(jnp.float32)
    side = side_rows(per_device)
    span = 2 * side
    which = lax.broadcasted_iota(jnp.int32, (8, LANES), 0) % per_device

    def rows_of(first, lane):
        tiled = jnp.zeros((8, LANES), jnp.float32)
        for v in range(per_device):
            row = spectra[first + v:first + v + 1, lane:lane + LANES]
            tiled = jnp.where(which == v, row, tiled)
        return tiled[None]

    for lane in range(0, NB, LANES):
        cosine = lags[:, lane:lane + LANES].reshape(side // 8, 8, LANES)
        sine = lags[:, NB + lane:NB + lane + LANES].reshape(side // 8, 8, LANES)
        for at in range(count):
            for behind in range(windows):
                first = (at * windows + behind) * per_device
                real, imag = rows_of(first, lane), rows_of(first, NB + lane)
                cr, si, sr, ci = cosine * real, sine * imag, sine * real, cosine * imag
                up = jnp.concatenate([cr - si, cr + si], axis=0).reshape(span, LANES)
                down = jnp.concatenate([ci + sr, ci - sr], axis=0).reshape(span, LANES)
                spot = pl.ds(at * span, span)
                turned[behind, spot, lane:lane + LANES] = up.astype(jnp.bfloat16)
                turned[behind, spot, NB + lane:NB + lane + LANES] = down.astype(jnp.bfloat16)


def others_kernel(table, weights, share, *refs):
    parts, (white, raw) = refs[:-2], refs[-2:]
    sub_at = lax.axis_index("sub")
    groups, _, group, samples = raw.shape
    each = len(parts) // white.shape[0]
    for i in range(white.shape[0]):
        if each == 1:
            rows = parts[i][...]
        else:
            for half, place in ((parts[2 * i], sub_at), (parts[2 * i + 1], 1 - sub_at)):
                raw[:, pl.ds(place, 1)] = half[...].reshape(groups, 1, group, samples)
            rows = raw[...].reshape(white.shape[1], samples)
        real, imag = whiten(rows, table[...], weights[...], share[...])
        white[i, :, :NB] = real
        white[i, :, NB:] = imag


def lag_product(turned, own, white):
    total = lax.dot_general(turned[0], own[...], NT, preferred_element_type=jnp.float32)
    for i in range(white.shape[0]):
        total += lax.dot_general(turned[1 + i], white[i], NT, preferred_element_type=jnp.float32)
    return total


def lag_kernel(factor, turned, own, white, mask, *pieces):
    result = lag_product(turned, own, white) * (mask[...].astype(jnp.float32) * factor)
    span = result.shape[0] // len(pieces)
    for at, piece in enumerate(pieces):
        piece[...] = result[at * span:(at + 1) * span, :].astype(jnp.bfloat16)


def put_slots(layout, listed, wide, out, stage, sems, slot):
    tie, blocks, per_device, first, reverse = layout
    block_at = lax.axis_index("chan")
    row = lax.broadcasted_iota(jnp.int32, listed.shape, 0)
    column = lax.broadcasted_iota(jnp.int32, listed.shape, 1)
    width = stage.shape[3]
    block = block_at if reverse else partner(block_at, blocks, tie)
    copies = []
    for e in offsets_of(block_at, blocks, tie, reverse):
        chosen = jnp.where((row == block) & (column == e), listed, 0.0)
        pair = jnp.broadcast_to(jnp.sum(chosen, keepdims=True), (per_device, width))
        for t in range(LAGS):
            tau = MAXLAG - t if reverse else t - MAXLAG
            spot = lag_row(tau, per_device)
            stage[slot, t] = wide[spot:spot + per_device, :] * pair
        target = out.at[e, :, :, pl.ds(first, width)]
        copies.append(pltpu.make_async_copy(stage.at[slot], target, sems.at[slot]))
        copies[-1].start()
        slot += 1
    return copies


def receiver_kernel(layout, pairs, turned, mask, *refs):
    ties, blocks, per_device, chunks, factor = layout
    count = len(chunks)
    owns, whites, pieces = refs[:count], refs[count:2 * count], refs[2 * count:-5]
    out, source_out, wide, stage, sems = refs[-5:]
    listed = pairs[...].astype(jnp.float32)
    copies = []
    for at, tie in enumerate(ties):
        for i, (start, size) in enumerate(chunks):
            lanes = slice(start, start + size)
            if at:
                wide[at, :, lanes] = pieces[i * (len(ties) - 1) + at - 1][...].astype(jnp.float32)
            else:
                wide[at, :, lanes] = lag_product(turned, owns[i], whites[i]) * (mask[:, lanes].astype(jnp.float32) * factor)
        turns = [(out, False)] + ([] if at else [(source_out, True)])
        for target, reverse in turns:
            part = (tie, blocks, per_device, 0, reverse)
            copies += put_slots(part, listed, wide.at[at], target, stage, sems, len(copies))
    for copy in copies:
        copy.wait()


def source_kernel(layout, pairs, *refs):
    ties, blocks, per_device, first = layout
    pieces, (_, out, wide, stage, sems) = refs[:len(ties)], refs[len(ties):]
    listed = pairs[...].astype(jnp.float32)
    copies = []
    for at, tie in enumerate(ties):
        wide[at] = pieces[at][...].astype(jnp.float32)
        part = (tie, blocks, per_device, first, True)
        copies += put_slots(part, listed, wide.at[at], out, stage, sems, len(copies))
    for copy in copies:
        copy.wait()


def ties_of(blocks):
    if blocks == 4:
        return [("xor", i) for i in range(4)]
    ties = []
    for moved in (0, 1, -1, 2, -2):
        if all((m - moved) % blocks for _, m in ties):
            ties.append(("shift", moved))
    return ties


def partner(block, blocks, tie, back=False):
    kind, step = tie
    if kind == "xor":
        return block ^ step
    return (block + (step if back else -step) + blocks) % blocks


def offsets_of(block, blocks, tie, back):
    kind, step = tie
    if kind == "shift":
        return [e for e in range(OFFS) if (e - REACH - step) % blocks == 0]
    if step % 2 == 0:
        return [e for e in range(OFFS) if abs(e - REACH) == step]
    ahead = (block ^ step) - block if back else block - (block ^ step)
    return [jnp.where((ahead + blocks) % blocks == 1, REACH + 1, REACH - 1)]


def exchange(value, blocks, tie, back=False):
    return lax.ppermute(value, "chan", [(partner(b, blocks, tie, back), b) for b in range(blocks)])


def chunks_of(channels):
    if channels < 2 * LANES or channels % LANES:
        return [(0, channels)]
    first = channels * 2 // 5 // LANES * LANES
    return [(0, first), (first, channels - first)]


def shift(block, axis, distance):
    count = lax.axis_size(axis)
    return lax.ppermute(block, axis, [(i, (i + distance) % count) for i in range(count)])


def slots_of(ties, blocks):
    return sum(len(offsets_of(0, blocks, tie, False)) for tie in ties)


def in_hbm(value):
    return pltpu.with_memory_space_constraint(value, pltpu.HBM)


def after(value, *others):
    return lax.optimization_barrier((value, *others))[0]


def on_device(traces, channel_mask, smooth_width, source_phase, pair_list):
    _, channels, samples = traces.shape
    blocks, windows, subs = (lax.axis_size(a) for a in ("chan", "win", "sub"))
    sub_at = lax.axis_index("sub")
    per_device = VS // (windows * subs)
    group = per_device * STRIDE
    ties = ties_of(blocks)
    span = 2 * side_rows(per_device)
    chunks = chunks_of(channels)
    table, lags = dft_table(samples), lag_table(samples, per_device)
    factor = (NB * windows) ** (-0.5)
    bf16, f32 = jnp.bfloat16, jnp.float32
    like = jax.ShapeDtypeStruct
    mask_row = channel_mask.reshape(1, channels)

    def half_of(rows, start, size):
        grouped = rows.reshape(channels // (subs * group), subs, group, samples)
        first, count = start // (subs * group), size // (subs * group)
        half = lax.dynamic_slice(grouped, (first, sub_at, 0, 0), (count, 1, group, samples))
        return half.reshape(size // subs, samples)

    def from_windows(half):
        return [shift(half, "win", d) for d in range(1, windows)]

    def with_other_core(received):
        return [side for piece in received for side in (piece, shift(piece, "sub", 1))]

    def whiten_others(size, both, hint):
        return pl.pallas_call(
            others_kernel,
            out_shape=like((windows - 1, size, 2 * NB), bf16),
            in_specs=[VMEM] * (3 + len(both)),
            out_specs=VMEM,
            scratch_shapes=[pltpu.VMEM((size // (subs * group), subs, group, samples), bf16)],
            compiler_params=params(24),
            cost_estimate=hint,
            name="whiten_others",
        )(table, weights, share, *both)

    def correlate(start, size, turned, own, white, hint):
        count = turned.shape[1] // span
        return pl.pallas_call(
            functools.partial(lag_kernel, factor),
            out_shape=tuple(like((span, size), bf16) for _ in range(count)),
            in_specs=[VMEM] * 4,
            out_specs=(VMEM,) * count,
            compiler_params=params(24),
            cost_estimate=hint,
            name="lag_pieces",
        )(turned, own, white, mask_row[:, start:start + size])

    half = half_of(traces, *chunks[0])
    lead = min(half.shape[0], 2 * VS * STRIDE // subs)
    first_rows = from_windows(half[:lead])
    *owns, weights, share, rows, table = pl.pallas_call(
        functools.partial(setup_kernel, chunks[:1]),
        out_shape=tuple(like((size, 2 * NB), bf16) for _, size in chunks[:1])
        + (like((NB, NB), bf16), like((1, NB), f32))
        + (like((channels, samples), bf16), like(table.shape, bf16)),
        in_specs=[HBM, HBM, HBM],
        out_specs=(VMEM,) * 5,
        scratch_shapes=[pltpu.SemaphoreType.DMA((TABLE_PARTS + 3,)), pltpu.VMEM((1, NB), jnp.int32)],
        compiler_params=params(24),
        cost_estimate=SHORT,
        name="whiten_own",
    )(in_hbm(traces), in_hbm(table), in_hbm(after(smooth_width, half).reshape(1, NB)))
    received = [first_rows]
    if lead < half.shape[0]:
        other_rows = from_windows(after(half[lead:], share))
        received = [[jnp.concatenate(both, axis=0) for both in zip(first_rows, other_rows)]]
    for start, size in chunks[1:]:
        received.append(from_windows(after(rows, *received[0])[start:start + size]))
    near = pl.pallas_call(
        functools.partial(near_kernel, (windows, subs, per_device)),
        out_shape=like((windows * per_device, samples), f32),
        in_specs=[SMEM] + [VMEM] * (1 + windows),
        out_specs=VMEM,
        compiler_params=params(16),
        cost_estimate=SHORT,
        name="pick_sources",
    )(source_phase, after(mask_row, weights), half[:lead], *first_rows)

    def turn(sources, which, hint, *first):
        rows_each = windows * per_device
        return pl.pallas_call(
            functools.partial(turn_kernel, (per_device, windows, len(which))),
            out_shape=like((windows, len(which) * span, 2 * NB), bf16),
            in_specs=[VMEM] * (4 + len(sources)),
            out_specs=VMEM,
            scratch_shapes=[pltpu.VMEM((len(which) * rows_each, 2 * NB), f32)],
            compiler_params=params(24),
            cost_estimate=hint,
            name="turn_sources",
        )(table, weights, after(share, *first), lags, *sources)

    turned_own = turn([near], ties[:1], LONG)
    inbound = with_other_core([after(r, near) for r in received[0]])
    white = whiten_others(chunks[0][1], inbound, SHORT)
    if ties[1][0] == "xor":
        beside = exchange(near, blocks, ties[1])
        two = jnp.concatenate([after(near, turned_own), beside], axis=0).astype(bf16)
        sources = [beside, exchange(two, blocks, ties[2])]
    else:
        sources = [exchange(near, blocks, tie) for tie in ties[1:]]
    turned = turn(sources, ties[1:], SHORT, white)
    pieces, arrived, whites = [], [], [white]
    for i, (start, size) in enumerate(chunks):
        if i:
            owns.append(
                pl.pallas_call(
                    functools.partial(own_kernel, start),
                    out_shape=like((size, 2 * NB), bf16),
                    in_specs=[VMEM] * 4,
                    out_specs=VMEM,
                    compiler_params=params(24),
                    cost_estimate=SHORT,
                    name="whiten_own",
                )(after(rows, *pieces[-1]), table, weights, share)
            )
            whites.append(whiten_others(size, [after(r, *pieces[-1]) for r in received[i]], LONG))
        pieces.append(correlate(start, size, turned, owns[i], whites[i], LONG if i else SHORT))
        ahead = arrived[-1][-1:] if i else []
        sent = [after(p, *ahead) for p in pieces[-1]]
        arrived.append([exchange(p, blocks, tie, True) for tie, p in zip(ties[1:], sent)])
    stack = like((OFFS, LAGS, per_device, channels), f32)

    def scratch(count, slots, width):
        return [
            pltpu.VMEM((count, span, width), f32),
            pltpu.VMEM((slots, LAGS, per_device, width), f32),
            pltpu.SemaphoreType.DMA((slots,)),
        ]

    remote = [piece for group in pieces for piece in group]
    receiver_stack, source_stack = pl.pallas_call(
        functools.partial(receiver_kernel, (ties, blocks, per_device, chunks, factor)),
        out_shape=(stack, stack),
        in_specs=[VMEM] * (3 + 2 * len(chunks) + len(remote)),
        out_specs=(HBM, HBM),
        scratch_shapes=scratch(len(ties), slots_of(ties, blocks) + 1, channels),
        compiler_params=params(24),
        cost_estimate=LONG,
        name="receiver_order",
    )(pair_list, turned_own, mask_row, *owns, *whites, *remote)
    slots = slots_of(ties[1:], blocks)
    for (start, size), back in zip(chunks, arrived):
        source_stack = pl.pallas_call(
            functools.partial(source_kernel, (ties[1:], blocks, per_device, start)),
            out_shape=stack,
            in_specs=[VMEM] * (1 + len(back)) + [HBM],
            out_specs=HBM,
            scratch_shapes=scratch(len(back), slots, size),
            input_output_aliases={1 + len(back): 0},
            compiler_params=params(16),
            cost_estimate=SHORT,
            name="source_order",
        )(pair_list, *back, source_stack)
    order = (2, 0, 1, 3)
    return (jnp.transpose(receiver_stack, order), jnp.transpose(source_stack, order))


def solution(mesh):
    in_specs = (
        P(("groups", "win"), "chan", None),
        P(("groups", "chan")),
        P(),
        P("groups"),
        P("groups", None),
    )
    out_specs = (
        P(("win", "sub"), None, None, ("groups", "chan")),
        P(("groups", "chan", "win", "sub"), None, None, None),
    )
    return jax.shard_map(
        on_device, mesh=mesh, in_specs=in_specs, out_specs=out_specs, check_vma=False
    )
```

```python
import functools
import math

import jax
import jax.numpy as jnp
import numpy as np
from jax import lax
from jax.experimental import pallas as pl
from jax.experimental.pallas import tpu as pltpu
from jax.sharding import PartitionSpec as P

NB = 512
MAXLAG = 50
STRIDE = 8
REACH = 2
VS = 8
OFFS = 5
LAGS = 2 * MAXLAG + 1
FLOOR = 0.25
TABLE_PARTS = 4
LANES = 128
VMEM = pl.BlockSpec(memory_space=pltpu.VMEM)
SMEM = pl.BlockSpec(memory_space=pltpu.SMEM)
HBM = pl.BlockSpec(memory_space=pltpu.HBM)
NT = (((1,), (1,)), ((), ()))


def dft_table(samples):
    phases = np.arange(samples)[:, None] * np.arange(NB)[None, :] % samples
    angles = phases * (2.0 * math.pi / samples)
    table = np.concatenate([np.cos(angles), -np.sin(angles)], axis=1)
    return jnp.asarray(table.astype(np.float32), jnp.bfloat16)


def side_rows(per_device):
    return -(-(MAXLAG + 1) * per_device // 8) * 8


def lag_row(tau, per_device):
    return abs(tau) * per_device + (0 if tau >= 0 else side_rows(per_device))


def lag_table(samples, per_device):
    lag = np.arange(side_rows(per_device)) // per_device
    angles = (lag[:, None] * np.arange(NB)[None, :] % samples) * (2.0 * math.pi / samples)
    table = np.concatenate([np.cos(angles), np.sin(angles)], axis=1)
    return jnp.asarray(table, jnp.float32)


def params(mib):
    return pltpu.CompilerParams(vmem_limit_bytes=mib << 20)


def cost(flops, moved):
    return pl.CostEstimate(flops=flops, bytes_accessed=moved, transcendentals=0)


SHORT, LONG = cost(1 << 20, 1 << 18), cost(1 << 33, 1 << 26)


def whiten(rows, table, weights, share):
    samples = rows.shape[1]
    spectrum = jnp.dot(rows, table, preferred_element_type=jnp.float32) * samples ** (-0.5)
    real, imag = spectrum[:, :NB], spectrum[:, NB:]
    amplitude = jnp.sqrt(real * real + imag * imag)
    high = amplitude.astype(jnp.bfloat16)
    low = (amplitude - high.astype(jnp.float32)).astype(jnp.bfloat16)
    total = jnp.dot(high, weights, preferred_element_type=jnp.float32)
    total += jnp.dot(low, weights, preferred_element_type=jnp.float32)
    gain = 1.0 / jnp.maximum(total * share, FLOOR)
    return (real * gain).astype(jnp.bfloat16), (imag * gain).astype(jnp.bfloat16)


def near_kernel(layout, phases, mask, *refs):
    windows, subs, per_device = layout
    halves, out = refs[:-1], refs[-1]
    block_at, win_at, sub_at = lax.axis_index("chan"), lax.axis_index("win"), lax.axis_index("sub")
    group = per_device * STRIDE
    rows, width = out.shape[0], halves[0].shape[0]
    phase = phases[block_at]

    def ones_at(first, width):
        row = lax.broadcasted_iota(jnp.int32, (rows, width), 0)
        place = lax.broadcasted_iota(jnp.int32, (rows, width), 1)
        return row, place == first + phase + STRIDE * (row % per_device)

    row, here = ones_at((win_at * subs + sub_at) * group, mask.shape[1])
    alive = jnp.sum(jnp.where(here, mask[...].astype(jnp.float32), 0.0), axis=1, keepdims=True)
    row, here = ones_at(win_at * group, width)
    total = jnp.zeros(out.shape, jnp.float32)
    for behind in range(windows):
        chosen = jnp.where(here & (row // per_device == behind), 1.0, 0.0).astype(jnp.bfloat16)
        total += jnp.dot(chosen, halves[behind][...], preferred_element_type=jnp.float32)
    out[...] = total * alive


def setup_kernel(chunks, traces, table, widths, *refs):
    owns, (weights, share, rows_kept, table_kept, sems, *scratch) = refs[:len(chunks)], refs[len(chunks):]
    depth = table.shape[0] // TABLE_PARTS
    needed = chunks[-1][0] + chunks[-1][1]
    rest = rows_kept.shape[0] - needed
    first_rows = pltpu.make_async_copy(traces.at[0, pl.ds(0, needed)], rows_kept.at[pl.ds(0, needed)], sems.at[TABLE_PARTS])
    first_rows.start()
    parts = []
    for i in range(TABLE_PARTS):
        span = pl.ds(i * depth, depth)
        parts.append(pltpu.make_async_copy(table.at[span], table_kept.at[span], sems.at[i]))
        parts[-1].start()
    if rest:
        span = pl.ds(needed, rest)
        last_rows = pltpu.make_async_copy(traces.at[0, span], rows_kept.at[span], sems.at[TABLE_PARTS + 1])
        last_rows.start()
    widths_kept, = scratch
    fetched = pltpu.make_async_copy(widths, widths_kept, sems.at[TABLE_PARTS + 2])
    fetched.start()
    fetched.wait()
    reach = widths_kept[...]
    near = lax.broadcasted_iota(jnp.int32, (NB, NB), 0)
    here = lax.broadcasted_iota(jnp.int32, (NB, NB), 1)
    weights[...] = jnp.where(jnp.abs(near - here) <= reach, 1.0, 0.0).astype(jnp.bfloat16)
    bins = lax.broadcasted_iota(jnp.int32, (1, NB), 1)
    count = jnp.minimum(bins + reach, NB - 1) - jnp.maximum(bins - reach, 0) + 1
    share[...] = 1.0 / count.astype(jnp.float32)
    first_rows.wait()
    for part in parts:
        part.wait()
    for (start, size), own in zip(chunks, owns):
        own_kernel(start, rows_kept, table_kept, weights, share, own)
    if rest:
        last_rows.wait()


def own_kernel(start, rows, table, weights, share, out):
    real, imag = whiten(rows[start:start + out.shape[0], :], table[...], weights[...], share[...])
    out[:, :NB] = real
    out[:, NB:] = imag


def turn_kernel(layout, table, weights, share, lags, *refs):
    per_device, windows, count = layout
    picked, turned, spectra = refs[:-2], refs[-2], refs[-1]
    rows = jnp.concatenate([p[...].astype(jnp.float32) for p in picked], axis=0).astype(jnp.bfloat16)
    real, imag = whiten(rows, table[...], weights[...], share[...])
    spectra[:, :NB] = real.astype(jnp.float32)
    spectra[:, NB:] = imag.astype(jnp.float32)
    side = side_rows(per_device)
    span = 2 * side
    which = lax.broadcasted_iota(jnp.int32, (8, LANES), 0) % per_device

    def rows_of(first, lane):
        tiled = jnp.zeros((8, LANES), jnp.float32)
        for v in range(per_device):
            row = spectra[first + v:first + v + 1, lane:lane + LANES]
            tiled = jnp.where(which == v, row, tiled)
        return tiled[None]

    for lane in range(0, NB, LANES):
        cosine = lags[:, lane:lane + LANES].reshape(side // 8, 8, LANES)
        sine = lags[:, NB + lane:NB + lane + LANES].reshape(side // 8, 8, LANES)
        for at in range(count):
            for behind in range(windows):
                first = (at * windows + behind) * per_device
                real, imag = rows_of(first, lane), rows_of(first, NB + lane)
                cr, si, sr, ci = cosine * real, sine * imag, sine * real, cosine * imag
                up = jnp.concatenate([cr - si, cr + si], axis=0).reshape(span, LANES)
                down = jnp.concatenate([ci + sr, ci - sr], axis=0).reshape(span, LANES)
                spot = pl.ds(at * span, span)
                turned[behind, spot, lane:lane + LANES] = up.astype(jnp.bfloat16)
                turned[behind, spot, NB + lane:NB + lane + LANES] = down.astype(jnp.bfloat16)


def others_kernel(table, weights, share, *refs):
    parts, (white, raw) = refs[:-2], refs[-2:]
    sub_at = lax.axis_index("sub")
    groups, _, group, samples = raw.shape
    each = len(parts) // white.shape[0]
    for i in range(white.shape[0]):
        if each == 1:
            rows = parts[i][...]
        else:
            for half, place in ((parts[2 * i], sub_at), (parts[2 * i + 1], 1 - sub_at)):
                raw[:, pl.ds(place, 1)] = half[...].reshape(groups, 1, group, samples)
            rows = raw[...].reshape(white.shape[1], samples)
        real, imag = whiten(rows, table[...], weights[...], share[...])
        white[i, :, :NB] = real
        white[i, :, NB:] = imag


def lag_product(turned, own, white):
    total = lax.dot_general(turned[0], own[...], NT, preferred_element_type=jnp.float32)
    for i in range(white.shape[0]):
        total += lax.dot_general(turned[1 + i], white[i], NT, preferred_element_type=jnp.float32)
    return total


def lag_kernel(factor, turned, own, white, mask, *pieces):
    result = lag_product(turned, own, white) * (mask[...].astype(jnp.float32) * factor)
    span = result.shape[0] // len(pieces)
    for at, piece in enumerate(pieces):
        piece[...] = result[at * span:(at + 1) * span, :].astype(jnp.bfloat16)


def put_slots(layout, listed, wide, out, stage, sems, slot):
    tie, blocks, per_device, first, reverse = layout
    block_at = lax.axis_index("chan")
    row = lax.broadcasted_iota(jnp.int32, listed.shape, 0)
    column = lax.broadcasted_iota(jnp.int32, listed.shape, 1)
    width = stage.shape[3]
    block = block_at if reverse else partner(block_at, blocks, tie)
    copies = []
    for e in offsets_of(block_at, blocks, tie, reverse):
        chosen = jnp.where((row == block) & (column == e), listed, 0.0)
        pair = jnp.broadcast_to(jnp.sum(chosen, keepdims=True), (per_device, width))
        for t in range(LAGS):
            tau = MAXLAG - t if reverse else t - MAXLAG
            spot = lag_row(tau, per_device)
            stage[slot, t] = wide[spot:spot + per_device, :] * pair
        target = out.at[e, :, :, pl.ds(first, width)]
        copies.append(pltpu.make_async_copy(stage.at[slot], target, sems.at[slot]))
        copies[-1].start()
        slot += 1
    return copies


def receiver_kernel(layout, pairs, turned, mask, *refs):
    ties, blocks, per_device, chunks, factor = layout
    count = len(chunks)
    owns, whites, pieces = refs[:count], refs[count:2 * count], refs[2 * count:-5]
    out, source_out, wide, stage, sems = refs[-5:]
    listed = pairs[...].astype(jnp.float32)
    copies = []
    for at, tie in enumerate(ties):
        for i, (start, size) in enumerate(chunks):
            lanes = slice(start, start + size)
            if at:
                wide[at, :, lanes] = pieces[i * (len(ties) - 1) + at - 1][...].astype(jnp.float32)
            else:
                wide[at, :, lanes] = lag_product(turned, owns[i], whites[i]) * (mask[:, lanes].astype(jnp.float32) * factor)
        turns = [(out, False)] + ([] if at else [(source_out, True)])
        for target, reverse in turns:
            part = (tie, blocks, per_device, 0, reverse)
            copies += put_slots(part, listed, wide.at[at], target, stage, sems, len(copies))
    for copy in copies:
        copy.wait()


def source_kernel(layout, pairs, *refs):
    ties, blocks, per_device, first = layout
    pieces, (_, out, wide, stage, sems) = refs[:len(ties)], refs[len(ties):]
    listed = pairs[...].astype(jnp.float32)
    copies = []
    for at, tie in enumerate(ties):
        wide[at] = pieces[at][...].astype(jnp.float32)
        part = (tie, blocks, per_device, first, True)
        copies += put_slots(part, listed, wide.at[at], out, stage, sems, len(copies))
    for copy in copies:
        copy.wait()


def ties_of(blocks):
    if blocks == 4:
        return [("xor", i) for i in range(4)]
    ties = []
    for moved in (0, 1, -1, 2, -2):
        if all((m - moved) % blocks for _, m in ties):
            ties.append(("shift", moved))
    return ties


def partner(block, blocks, tie, back=False):
    kind, step = tie
    if kind == "xor":
        return block ^ step
    return (block + (step if back else -step) + blocks) % blocks


def offsets_of(block, blocks, tie, back):
    kind, step = tie
    if kind == "shift":
        return [e for e in range(OFFS) if (e - REACH - step) % blocks == 0]
    if step % 2 == 0:
        return [e for e in range(OFFS) if abs(e - REACH) == step]
    ahead = (block ^ step) - block if back else block - (block ^ step)
    return [jnp.where((ahead + blocks) % blocks == 1, REACH + 1, REACH - 1)]


def exchange(value, blocks, tie, back=False):
    return lax.ppermute(value, "chan", [(partner(b, blocks, tie, back), b) for b in range(blocks)])


def chunks_of(channels):
    if channels < 2 * LANES or channels % LANES:
        return [(0, channels)]
    first = channels * 2 // 5 // LANES * LANES
    return [(0, first), (first, channels - first)]


def shift(block, axis, distance):
    count = lax.axis_size(axis)
    return lax.ppermute(block, axis, [(i, (i + distance) % count) for i in range(count)])


def slots_of(ties, blocks):
    return sum(len(offsets_of(0, blocks, tie, False)) for tie in ties)


def in_hbm(value):
    return pltpu.with_memory_space_constraint(value, pltpu.HBM)


def after(value, *others):
    return lax.optimization_barrier((value, *others))[0]


def on_device(traces, channel_mask, smooth_width, source_phase, pair_list):
    _, channels, samples = traces.shape
    blocks, windows, subs = (lax.axis_size(a) for a in ("chan", "win", "sub"))
    sub_at = lax.axis_index("sub")
    per_device = VS // (windows * subs)
    group = per_device * STRIDE
    ties = ties_of(blocks)
    span = 2 * side_rows(per_device)
    chunks = chunks_of(channels)
    table, lags = dft_table(samples), lag_table(samples, per_device)
    factor = (NB * windows) ** (-0.5)
    bf16, f32 = jnp.bfloat16, jnp.float32
    like = jax.ShapeDtypeStruct
    mask_row = channel_mask.reshape(1, channels)

    def half_of(rows, start, size):
        grouped = rows.reshape(channels // (subs * group), subs, group, samples)
        first, count = start // (subs * group), size // (subs * group)
        half = lax.dynamic_slice(grouped, (first, sub_at, 0, 0), (count, 1, group, samples))
        return half.reshape(size // subs, samples)

    def from_windows(half):
        return [shift(half, "win", d) for d in range(1, windows)]

    def with_other_core(received):
        return [side for piece in received for side in (piece, shift(piece, "sub", 1))]

    def whiten_others(size, both, hint):
        return pl.pallas_call(
            others_kernel,
            out_shape=like((windows - 1, size, 2 * NB), bf16),
            in_specs=[VMEM] * (3 + len(both)),
            out_specs=VMEM,
            scratch_shapes=[pltpu.VMEM((size // (subs * group), subs, group, samples), bf16)],
            compiler_params=params(24),
            cost_estimate=hint,
            name="whiten_others",
        )(table, weights, share, *both)

    def correlate(start, size, turned, own, white, hint):
        count = turned.shape[1] // span
        return pl.pallas_call(
            functools.partial(lag_kernel, factor),
            out_shape=tuple(like((span, size), bf16) for _ in range(count)),
            in_specs=[VMEM] * 4,
            out_specs=(VMEM,) * count,
            compiler_params=params(24),
            cost_estimate=hint,
            name="lag_pieces",
        )(turned, own, white, mask_row[:, start:start + size])

    half = half_of(traces, *chunks[0])
    received = [from_windows(half)]
    *owns, weights, share, rows, table = pl.pallas_call(
        functools.partial(setup_kernel, chunks),
        out_shape=tuple(like((size, 2 * NB), bf16) for _, size in chunks)
        + (like((NB, NB), bf16), like((1, NB), f32))
        + (like((channels, samples), bf16), like(table.shape, bf16)),
        in_specs=[HBM, HBM, HBM],
        out_specs=(VMEM,) * (len(chunks) + 4),
        scratch_shapes=[pltpu.SemaphoreType.DMA((TABLE_PARTS + 3,)), pltpu.VMEM((1, NB), jnp.int32)],
        compiler_params=params(24),
        cost_estimate=SHORT,
        name="whiten_own",
    )(in_hbm(traces), in_hbm(table), in_hbm(after(smooth_width, half).reshape(1, NB)))
    received += [from_windows(after(rows, share)[a:a + n]) for a, n in chunks[1:]]
    near = pl.pallas_call(
        functools.partial(near_kernel, (windows, subs, per_device)),
        out_shape=like((windows * per_device, samples), f32),
        in_specs=[SMEM] + [VMEM] * (1 + windows),
        out_specs=VMEM,
        compiler_params=params(16),
        cost_estimate=SHORT,
        name="pick_sources",
    )(source_phase, after(mask_row, weights), half, *received[0])

    def turn(sources, which, hint, *first):
        rows_each = windows * per_device
        return pl.pallas_call(
            functools.partial(turn_kernel, (per_device, windows, len(which))),
            out_shape=like((windows, len(which) * span, 2 * NB), bf16),
            in_specs=[VMEM] * (4 + len(sources)),
            out_specs=VMEM,
            scratch_shapes=[pltpu.VMEM((len(which) * rows_each, 2 * NB), f32)],
            compiler_params=params(24),
            cost_estimate=hint,
            name="turn_sources",
        )(table, weights, after(share, *first), lags, *sources)

    turned_own = turn([near], ties[:1], LONG)
    inbound = with_other_core(received[0])
    white = whiten_others(chunks[0][1], inbound, SHORT)
    if ties[1][0] == "xor":
        beside = exchange(near, blocks, ties[1])
        two = jnp.concatenate([after(near, turned_own), beside], axis=0).astype(bf16)
        sources = [beside, exchange(two, blocks, ties[2])]
    else:
        sources = [exchange(near, blocks, tie) for tie in ties[1:]]
    turned = turn(sources, ties[1:], SHORT, white)
    pieces, arrived, whites = [], [], [white]
    for i, (start, size) in enumerate(chunks):
        if i:
            whites.append(whiten_others(size, [after(r, *pieces[-1]) for r in received[i]], LONG))
        pieces.append(correlate(start, size, turned, owns[i], whites[i], LONG if i else SHORT))
        ahead = arrived[-1][-1:] if i else []
        sent = [after(p, *ahead) for p in pieces[-1]]
        arrived.append([exchange(p, blocks, tie, True) for tie, p in zip(ties[1:], sent)])
    stack = like((OFFS, LAGS, per_device, channels), f32)

    def scratch(count, slots, width):
        return [
            pltpu.VMEM((count, span, width), f32),
            pltpu.VMEM((slots, LAGS, per_device, width), f32),
            pltpu.SemaphoreType.DMA((slots,)),
        ]

    remote = [piece for group in pieces for piece in group]
    receiver_stack, source_stack = pl.pallas_call(
        functools.partial(receiver_kernel, (ties, blocks, per_device, chunks, factor)),
        out_shape=(stack, stack),
        in_specs=[VMEM] * (3 + 2 * len(chunks) + len(remote)),
        out_specs=(HBM, HBM),
        scratch_shapes=scratch(len(ties), slots_of(ties, blocks) + 1, channels),
        compiler_params=params(24),
        cost_estimate=LONG,
        name="receiver_order",
    )(pair_list, turned_own, mask_row, *owns, *whites, *remote)
    slots = slots_of(ties[1:], blocks)
    for (start, size), back in zip(chunks, arrived):
        source_stack = pl.pallas_call(
            functools.partial(source_kernel, (ties[1:], blocks, per_device, start)),
            out_shape=stack,
            in_specs=[VMEM] * (1 + len(back)) + [HBM],
            out_specs=HBM,
            scratch_shapes=scratch(len(back), slots, size),
            input_output_aliases={1 + len(back): 0},
            compiler_params=params(16),
            cost_estimate=SHORT,
            name="source_order",
        )(pair_list, *back, source_stack)
    order = (2, 0, 1, 3)
    return (jnp.transpose(receiver_stack, order), jnp.transpose(source_stack, order))


def solution(mesh):
    in_specs = (
        P(("groups", "win"), "chan", None),
        P(("groups", "chan")),
        P(),
        P("groups"),
        P("groups", None),
    )
    out_specs = (
        P(("win", "sub"), None, None, ("groups", "chan")),
        P(("groups", "chan", "win", "sub"), None, None, None),
    )
    return jax.shard_map(
        on_device, mesh=mesh, in_specs=in_specs, out_specs=out_specs, check_vma=False
    )
```

```python
import functools
import math

import jax
import jax.numpy as jnp
import numpy as np
from jax import lax
from jax.experimental import pallas as pl
from jax.experimental.pallas import tpu as pltpu
from jax.sharding import PartitionSpec as P

NB = 512
MAXLAG = 50
STRIDE = 8
REACH = 2
VS = 8
OFFS = 5
LAGS = 2 * MAXLAG + 1
FLOOR = 0.25
TABLE_PARTS = 4
LANES = 128
VMEM = pl.BlockSpec(memory_space=pltpu.VMEM)
SMEM = pl.BlockSpec(memory_space=pltpu.SMEM)
HBM = pl.BlockSpec(memory_space=pltpu.HBM)
NT = (((1,), (1,)), ((), ()))


def dft_table(samples):
    phases = np.arange(samples)[:, None] * np.arange(NB)[None, :] % samples
    angles = phases * (2.0 * math.pi / samples)
    table = np.concatenate([np.cos(angles), -np.sin(angles)], axis=1)
    return jnp.asarray(table.astype(np.float32), jnp.bfloat16)


def side_rows(per_device):
    return -(-(MAXLAG + 1) * per_device // 8) * 8


def lag_row(tau, per_device):
    return abs(tau) * per_device + (0 if tau >= 0 else side_rows(per_device))


def lag_table(samples, per_device):
    lag = np.arange(side_rows(per_device)) // per_device
    angles = (lag[:, None] * np.arange(NB)[None, :] % samples) * (2.0 * math.pi / samples)
    table = np.concatenate([np.cos(angles), np.sin(angles)], axis=1)
    return jnp.asarray(table, jnp.float32)


def params(mib):
    return pltpu.CompilerParams(vmem_limit_bytes=mib << 20)


def cost(flops, moved):
    return pl.CostEstimate(flops=flops, bytes_accessed=moved, transcendentals=0)


SHORT, LONG = cost(1 << 20, 1 << 18), cost(1 << 33, 1 << 26)


def whiten(rows, table, weights, share):
    samples = rows.shape[1]
    spectrum = jnp.dot(rows, table, preferred_element_type=jnp.float32) * samples ** (-0.5)
    real, imag = spectrum[:, :NB], spectrum[:, NB:]
    amplitude = jnp.sqrt(real * real + imag * imag)
    high = amplitude.astype(jnp.bfloat16)
    low = (amplitude - high.astype(jnp.float32)).astype(jnp.bfloat16)
    total = jnp.dot(high, weights, preferred_element_type=jnp.float32)
    total += jnp.dot(low, weights, preferred_element_type=jnp.float32)
    gain = 1.0 / jnp.maximum(total * share, FLOOR)
    return (real * gain).astype(jnp.bfloat16), (imag * gain).astype(jnp.bfloat16)


def near_kernel(layout, phases, mask, *refs):
    windows, subs, per_device = layout
    halves, out = refs[:-1], refs[-1]
    block_at, win_at, sub_at = lax.axis_index("chan"), lax.axis_index("win"), lax.axis_index("sub")
    group = per_device * STRIDE
    rows, width = out.shape[0], halves[0].shape[0]
    phase = phases[block_at]

    def ones_at(first, width):
        row = lax.broadcasted_iota(jnp.int32, (rows, width), 0)
        place = lax.broadcasted_iota(jnp.int32, (rows, width), 1)
        return row, place == first + phase + STRIDE * (row % per_device)

    row, here = ones_at((win_at * subs + sub_at) * group, mask.shape[1])
    alive = jnp.sum(jnp.where(here, mask[...].astype(jnp.float32), 0.0), axis=1, keepdims=True)
    row, here = ones_at(win_at * group, width)
    total = jnp.zeros(out.shape, jnp.float32)
    for behind in range(windows):
        chosen = jnp.where(here & (row // per_device == behind), 1.0, 0.0).astype(jnp.bfloat16)
        total += jnp.dot(chosen, halves[behind][...], preferred_element_type=jnp.float32)
    out[...] = total * alive


def setup_kernel(chunks, traces, table, widths, *refs):
    owns, (weights, share, rows_kept, table_kept, sems, *scratch) = refs[:len(chunks)], refs[len(chunks):]
    depth = table.shape[0] // TABLE_PARTS
    needed = chunks[-1][0] + chunks[-1][1]
    rest = rows_kept.shape[0] - needed
    first_rows = pltpu.make_async_copy(traces.at[0, pl.ds(0, needed)], rows_kept.at[pl.ds(0, needed)], sems.at[TABLE_PARTS])
    first_rows.start()
    parts = []
    for i in range(TABLE_PARTS):
        span = pl.ds(i * depth, depth)
        parts.append(pltpu.make_async_copy(table.at[span], table_kept.at[span], sems.at[i]))
        parts[-1].start()
    if rest:
        span = pl.ds(needed, rest)
        last_rows = pltpu.make_async_copy(traces.at[0, span], rows_kept.at[span], sems.at[TABLE_PARTS + 1])
        last_rows.start()
    widths_kept, = scratch
    fetched = pltpu.make_async_copy(widths, widths_kept, sems.at[TABLE_PARTS + 2])
    fetched.start()
    fetched.wait()
    reach = widths_kept[...]
    near = lax.broadcasted_iota(jnp.int32, (NB, NB), 0)
    here = lax.broadcasted_iota(jnp.int32, (NB, NB), 1)
    weights[...] = jnp.where(jnp.abs(near - here) <= reach, 1.0, 0.0).astype(jnp.bfloat16)
    bins = lax.broadcasted_iota(jnp.int32, (1, NB), 1)
    count = jnp.minimum(bins + reach, NB - 1) - jnp.maximum(bins - reach, 0) + 1
    share[...] = 1.0 / count.astype(jnp.float32)
    first_rows.wait()
    for part in parts:
        part.wait()
    for (start, size), own in zip(chunks, owns):
        own_kernel(start, rows_kept, table_kept, weights, share, own)
    if rest:
        last_rows.wait()


def own_kernel(start, rows, table, weights, share, out):
    real, imag = whiten(rows[start:start + out.shape[0], :], table[...], weights[...], share[...])
    out[:, :NB] = real
    out[:, NB:] = imag


def turn_kernel(layout, table, weights, share, lags, *refs):
    per_device, windows, places = layout
    even = lax.axis_index("sub") % 2 == 0
    picked, turned, spectra = refs[:-2], refs[-2], refs[-1]
    rows = jnp.concatenate([p[...].astype(jnp.float32) for p in picked], axis=0).astype(jnp.bfloat16)
    real, imag = whiten(rows, table[...], weights[...], share[...])
    spectra[:, :NB] = real.astype(jnp.float32)
    spectra[:, NB:] = imag.astype(jnp.float32)
    side = side_rows(per_device)
    span = 2 * side
    which = lax.broadcasted_iota(jnp.int32, (8, LANES), 0) % per_device

    def rows_of(first, lane):
        tiled = jnp.zeros((8, LANES), jnp.float32)
        for v in range(per_device):
            rows = [spectra[f + v:f + v + 1, lane:lane + LANES] for f in first]
            row = rows[0] if first[0] == first[-1] else jnp.where(even, rows[0], rows[-1])
            tiled = jnp.where(which == v, row, tiled)
        return tiled[None]

    for lane in range(0, NB, LANES):
        cosine = lags[:, lane:lane + LANES].reshape(side // 8, 8, LANES)
        sine = lags[:, NB + lane:NB + lane + LANES].reshape(side // 8, 8, LANES)
        for at, place in enumerate(places):
            for behind in range(windows):
                first = [(here * windows + behind) * per_device for here in place]
                real, imag = rows_of(first, lane), rows_of(first, NB + lane)
                cr, si, sr, ci = cosine * real, sine * imag, sine * real, cosine * imag
                up = jnp.concatenate([cr - si, cr + si], axis=0).reshape(span, LANES)
                down = jnp.concatenate([ci + sr, ci - sr], axis=0).reshape(span, LANES)
                spot = pl.ds(at * span, span)
                turned[behind, spot, lane:lane + LANES] = up.astype(jnp.bfloat16)
                turned[behind, spot, NB + lane:NB + lane + LANES] = down.astype(jnp.bfloat16)


def others_kernel(table, weights, share, *refs):
    parts, (white, raw) = refs[:-2], refs[-2:]
    sub_at = lax.axis_index("sub")
    groups, _, group, samples = raw.shape
    each = len(parts) // white.shape[0]
    for i in range(white.shape[0]):
        if each == 1:
            rows = parts[i][...]
        else:
            for half, place in ((parts[2 * i], sub_at), (parts[2 * i + 1], 1 - sub_at)):
                raw[:, pl.ds(place, 1)] = half[...].reshape(groups, 1, group, samples)
            rows = raw[...].reshape(white.shape[1], samples)
        real, imag = whiten(rows, table[...], weights[...], share[...])
        white[i, :, :NB] = real
        white[i, :, NB:] = imag


def lag_product(turned, own, white):
    total = lax.dot_general(turned[0], own[...], NT, preferred_element_type=jnp.float32)
    for i in range(white.shape[0]):
        total += lax.dot_general(turned[1 + i], white[i], NT, preferred_element_type=jnp.float32)
    return total


def lag_kernel(factor, turned, own, white, mask, *pieces):
    result = lag_product(turned, own, white) * (mask[...].astype(jnp.float32) * factor)
    span = result.shape[0] // len(pieces)
    for at, piece in enumerate(pieces):
        piece[...] = result[at * span:(at + 1) * span, :].astype(jnp.bfloat16)


def put_slots(layout, listed, wide, out, stage, sems, slot):
    tie, blocks, per_device, first, reverse = layout
    block_at, tie = lax.axis_index("chan"), on_core(tie, lax.axis_index("sub"))
    row = lax.broadcasted_iota(jnp.int32, listed.shape, 0)
    column = lax.broadcasted_iota(jnp.int32, listed.shape, 1)
    width = stage.shape[3]
    block = block_at if reverse else partner(block_at, blocks, tie)
    copies = []
    for e in offsets_of(block_at, blocks, tie, reverse):
        chosen = jnp.where((row == block) & (column == e), listed, 0.0)
        pair = jnp.broadcast_to(jnp.sum(chosen, keepdims=True), (per_device, width))
        for t in range(LAGS):
            tau = MAXLAG - t if reverse else t - MAXLAG
            spot = lag_row(tau, per_device)
            stage[slot, t] = wide[spot:spot + per_device, :] * pair
        target = out.at[e, :, :, pl.ds(first, width)]
        copies.append(pltpu.make_async_copy(stage.at[slot], target, sems.at[slot]))
        copies[-1].start()
        slot += 1
    return copies


def receiver_kernel(layout, pairs, turned, mask, *refs):
    ties, blocks, per_device, chunks, factor = layout
    count = len(chunks)
    owns, whites, pieces = refs[:count], refs[count:2 * count], refs[2 * count:-5]
    out, source_out, wide, stage, sems = refs[-5:]
    listed = pairs[...].astype(jnp.float32)
    copies = []
    for at, tie in enumerate(ties):
        for i, (start, size) in enumerate(chunks):
            lanes = slice(start, start + size)
            if at:
                wide[at, :, lanes] = pieces[i * (len(ties) - 1) + at - 1][...].astype(jnp.float32)
            else:
                wide[at, :, lanes] = lag_product(turned, owns[i], whites[i]) * (mask[:, lanes].astype(jnp.float32) * factor)
        turns = [(out, False)] + ([] if at else [(source_out, True)])
        for target, reverse in turns:
            part = (tie, blocks, per_device, 0, reverse)
            copies += put_slots(part, listed, wide.at[at], target, stage, sems, len(copies))
    for copy in copies:
        copy.wait()


def source_kernel(layout, pairs, *refs):
    ties, blocks, per_device, first = layout
    pieces, (_, out, wide, stage, sems) = refs[:len(ties)], refs[len(ties):]
    listed = pairs[...].astype(jnp.float32)
    copies = []
    for at, tie in enumerate(ties):
        wide[at] = pieces[at][...].astype(jnp.float32)
        part = (tie, blocks, per_device, first, True)
        copies += put_slots(part, listed, wide.at[at], out, stage, sems, len(copies))
    for copy in copies:
        copy.wait()


def ties_of(blocks, subs):
    if blocks == 4:
        own = [("xor", (0,) * subs)]
        return own + [("xor", tuple(4 - step if c % 2 else step for c in range(subs))) for step in (1, 2, 3)]
    ties = []
    for moved in (0, 1, -1, 2, -2):
        if all((m[0] - moved) % blocks for _, m in ties):
            ties.append(("shift", (moved,) * subs))
    return ties


def on_core(tie, core):
    kind, steps = tie
    if len(set(steps)) == 1:
        return kind, steps[0]
    return kind, jnp.where(core % 2 == 0, steps[0], steps[1])


def partner(block, blocks, tie, back=False):
    kind, step = tie
    if kind == "xor":
        return block ^ step
    return (block + (step if back else -step) + blocks) % blocks


def offsets_of(block, blocks, tie, back):
    kind, step = tie
    if kind == "shift":
        return [e for e in range(OFFS) if (e - REACH - step) % blocks == 0]
    if isinstance(step, int) and step % 2 == 0:
        return [e for e in range(OFFS) if abs(e - REACH) == step]
    ahead = (block ^ step) - block if back else block - (block ^ step)
    return [jnp.where((ahead + blocks) % blocks == 1, REACH + 1, REACH - 1)]


def exchange(value, blocks, subs, tie, back=False):
    kind, steps = tie
    route = [
        (partner(b, blocks, (kind, steps[c]), back) * subs + c, b * subs + c)
        for b in range(blocks)
        for c in range(subs)
    ]
    return lax.ppermute(value, ("chan", "sub"), route)


def chunks_of(channels):
    if channels < 2 * LANES or channels % LANES:
        return [(0, channels)]
    first = channels * 2 // 5 // LANES * LANES
    return [(0, first), (first, channels - first)]


def shift(block, axis, distance):
    count = lax.axis_size(axis)
    return lax.ppermute(block, axis, [(i, (i + distance) % count) for i in range(count)])


def slots_of(ties, blocks):
    return sum(len(offsets_of(0, blocks, (kind, steps[0]), False)) for kind, steps in ties)


def in_hbm(value):
    return pltpu.with_memory_space_constraint(value, pltpu.HBM)


def after(value, *others):
    return lax.optimization_barrier((value, *others))[0]


def on_device(traces, channel_mask, smooth_width, source_phase, pair_list):
    _, channels, samples = traces.shape
    blocks, windows, subs = (lax.axis_size(a) for a in ("chan", "win", "sub"))
    sub_at = lax.axis_index("sub")
    per_device = VS // (windows * subs)
    group = per_device * STRIDE
    ties = ties_of(blocks, subs)
    span = 2 * side_rows(per_device)
    chunks = chunks_of(channels)
    table, lags = dft_table(samples), lag_table(samples, per_device)
    factor = (NB * windows) ** (-0.5)
    bf16, f32 = jnp.bfloat16, jnp.float32
    like = jax.ShapeDtypeStruct
    mask_row = channel_mask.reshape(1, channels)

    def half_of(rows, start, size):
        grouped = rows.reshape(channels // (subs * group), subs, group, samples)
        first, count = start // (subs * group), size // (subs * group)
        half = lax.dynamic_slice(grouped, (first, sub_at, 0, 0), (count, 1, group, samples))
        return half.reshape(size // subs, samples)

    def from_windows(half):
        return [shift(half, "win", d) for d in range(1, windows)]

    def with_other_core(received):
        return [side for piece in received for side in (piece, shift(piece, "sub", 1))]

    def whiten_others(size, both, hint):
        return pl.pallas_call(
            others_kernel,
            out_shape=like((windows - 1, size, 2 * NB), bf16),
            in_specs=[VMEM] * (3 + len(both)),
            out_specs=VMEM,
            scratch_shapes=[pltpu.VMEM((size // (subs * group), subs, group, samples), bf16)],
            compiler_params=params(24),
            cost_estimate=hint,
            name="whiten_others",
        )(table, weights, share, *both)

    def correlate(start, size, turned, own, white, hint):
        count = turned.shape[1] // span
        return pl.pallas_call(
            functools.partial(lag_kernel, factor),
            out_shape=tuple(like((span, size), bf16) for _ in range(count)),
            in_specs=[VMEM] * 4,
            out_specs=(VMEM,) * count,
            compiler_params=params(24),
            cost_estimate=hint,
            name="lag_pieces",
        )(turned, own, white, mask_row[:, start:start + size])

    half = half_of(traces, *chunks[0])
    received = [from_windows(half)]
    *owns, weights, share, rows, table = pl.pallas_call(
        functools.partial(setup_kernel, chunks),
        out_shape=tuple(like((size, 2 * NB), bf16) for _, size in chunks)
        + (like((NB, NB), bf16), like((1, NB), f32))
        + (like((channels, samples), bf16), like(table.shape, bf16)),
        in_specs=[HBM, HBM, HBM],
        out_specs=(VMEM,) * (len(chunks) + 4),
        scratch_shapes=[pltpu.SemaphoreType.DMA((TABLE_PARTS + 3,)), pltpu.VMEM((1, NB), jnp.int32)],
        compiler_params=params(24),
        cost_estimate=SHORT,
        name="whiten_own",
    )(in_hbm(traces), in_hbm(table), in_hbm(after(smooth_width, half).reshape(1, NB)))
    received += [from_windows(after(rows, share)[a:a + n]) for a, n in chunks[1:]]
    near = pl.pallas_call(
        functools.partial(near_kernel, (windows, subs, per_device)),
        out_shape=like((windows * per_device, samples), f32),
        in_specs=[SMEM] + [VMEM] * (1 + windows),
        out_specs=VMEM,
        compiler_params=params(16),
        cost_estimate=SHORT,
        name="pick_sources",
    )(source_phase, after(mask_row, weights), half, *received[0])

    def turn(sources, places, hint, *first):
        rows_each = windows * per_device
        return pl.pallas_call(
            functools.partial(turn_kernel, (per_device, windows, places)),
            out_shape=like((windows, len(places) * span, 2 * NB), bf16),
            in_specs=[VMEM] * (4 + len(sources)),
            out_specs=VMEM,
            scratch_shapes=[pltpu.VMEM((len(places) * rows_each, 2 * NB), f32)],
            compiler_params=params(24),
            cost_estimate=hint,
            name="turn_sources",
        )(table, weights, after(share, *first), lags, *sources)

    turned_own = turn([near], [(0,)], LONG)
    inbound = with_other_core(received[0])
    white = whiten_others(chunks[0][1], inbound, SHORT)
    if ties[1][0] == "xor":
        beside = exchange(near, blocks, subs, ("xor", (1,) * subs))
        two = jnp.concatenate([after(near, turned_own), beside], axis=0).astype(bf16)
        sources = [beside, exchange(two, blocks, subs, ("xor", (2,) * subs))]
        places = [tuple(step - 1 for step in steps) for _, steps in ties[1:]]
    else:
        sources = [exchange(near, blocks, subs, tie) for tie in ties[1:]]
        places = [(at,) for at in range(len(sources))]
    turned = turn(sources, places, SHORT, white)
    pieces, arrived, whites = [], [], [white]
    for i, (start, size) in enumerate(chunks):
        if i:
            whites.append(whiten_others(size, [after(r, *pieces[-1]) for r in received[i]], LONG))
        pieces.append(correlate(start, size, turned, owns[i], whites[i], LONG if i else SHORT))
        ahead = arrived[-1][-1:] if i else []
        sent = [after(p, *ahead) for p in pieces[-1]]
        arrived.append([exchange(p, blocks, subs, tie, True) for tie, p in zip(ties[1:], sent)])
    stack = like((OFFS, LAGS, per_device, channels), f32)

    def scratch(count, slots, width):
        return [
            pltpu.VMEM((count, span, width), f32),
            pltpu.VMEM((slots, LAGS, per_device, width), f32),
            pltpu.SemaphoreType.DMA((slots,)),
        ]

    remote = [piece for group in pieces for piece in group]
    receiver_stack, source_stack = pl.pallas_call(
        functools.partial(receiver_kernel, (ties, blocks, per_device, chunks, factor)),
        out_shape=(stack, stack),
        in_specs=[VMEM] * (3 + 2 * len(chunks) + len(remote)),
        out_specs=(HBM, HBM),
        scratch_shapes=scratch(len(ties), slots_of(ties, blocks) + 1, channels),
        compiler_params=params(24),
        cost_estimate=LONG,
        name="receiver_order",
    )(pair_list, turned_own, mask_row, *owns, *whites, *remote)
    slots = slots_of(ties[1:], blocks)
    for (start, size), back in zip(chunks, arrived):
        source_stack = pl.pallas_call(
            functools.partial(source_kernel, (ties[1:], blocks, per_device, start)),
            out_shape=stack,
            in_specs=[VMEM] * (1 + len(back)) + [HBM],
            out_specs=HBM,
            scratch_shapes=scratch(len(back), slots, size),
            input_output_aliases={1 + len(back): 0},
            compiler_params=params(16),
            cost_estimate=SHORT,
            name="source_order",
        )(pair_list, *back, source_stack)
    order = (2, 0, 1, 3)
    return (jnp.transpose(receiver_stack, order), jnp.transpose(source_stack, order))


def solution(mesh):
    in_specs = (
        P(("groups", "win"), "chan", None),
        P(("groups", "chan")),
        P(),
        P("groups"),
        P("groups", None),
    )
    out_specs = (
        P(("win", "sub"), None, None, ("groups", "chan")),
        P(("groups", "chan", "win", "sub"), None, None, None),
    )
    return jax.shard_map(
        on_device, mesh=mesh, in_specs=in_specs, out_specs=out_specs, check_vma=False
    )
```

```python
import functools
import math

import jax
import jax.numpy as jnp
import numpy as np
from jax import lax
from jax.experimental import pallas as pl
from jax.experimental.pallas import tpu as pltpu
from jax.sharding import PartitionSpec as P

NB = 512
MAXLAG = 50
STRIDE = 8
REACH = 2
VS = 8
OFFS = 5
LAGS = 2 * MAXLAG + 1
FLOOR = 0.25
TABLE_PARTS = 4
LANES = 128
VMEM = pl.BlockSpec(memory_space=pltpu.VMEM)
SMEM = pl.BlockSpec(memory_space=pltpu.SMEM)
HBM = pl.BlockSpec(memory_space=pltpu.HBM)
NT = (((1,), (1,)), ((), ()))


def dft_table(samples):
    phases = np.arange(samples)[:, None] * np.arange(NB)[None, :] % samples
    angles = phases * (2.0 * math.pi / samples)
    table = np.concatenate([np.cos(angles), -np.sin(angles)], axis=1)
    return jnp.asarray(table.astype(np.float32), jnp.bfloat16)


def side_rows(per_device):
    return -(-(MAXLAG + 1) * per_device // 8) * 8


def lag_row(tau, per_device):
    return abs(tau) * per_device + (0 if tau >= 0 else side_rows(per_device))


def lag_table(samples, per_device):
    lag = np.arange(side_rows(per_device)) // per_device
    angles = (lag[:, None] * np.arange(NB)[None, :] % samples) * (2.0 * math.pi / samples)
    table = np.concatenate([np.cos(angles), np.sin(angles)], axis=1)
    return jnp.asarray(table, jnp.float32)


def params(mib):
    return pltpu.CompilerParams(vmem_limit_bytes=mib << 20)


def cost(flops, moved):
    return pl.CostEstimate(flops=flops, bytes_accessed=moved, transcendentals=0)


SHORT, LONG = cost(1 << 20, 1 << 18), cost(1 << 33, 1 << 26)


def whiten(rows, table, weights, share):
    samples = rows.shape[1]
    spectrum = jnp.dot(rows, table, preferred_element_type=jnp.float32) * samples ** (-0.5)
    real, imag = spectrum[:, :NB], spectrum[:, NB:]
    amplitude = jnp.sqrt(real * real + imag * imag)
    high = amplitude.astype(jnp.bfloat16)
    low = (amplitude - high.astype(jnp.float32)).astype(jnp.bfloat16)
    total = jnp.dot(high, weights, preferred_element_type=jnp.float32)
    total += jnp.dot(low, weights, preferred_element_type=jnp.float32)
    gain = 1.0 / jnp.maximum(total * share, FLOOR)
    return (real * gain).astype(jnp.bfloat16), (imag * gain).astype(jnp.bfloat16)


def near_kernel(layout, phases, mask, *refs):
    windows, subs, per_device = layout
    halves, out = refs[:-1], refs[-1]
    block_at, win_at, sub_at = lax.axis_index("chan"), lax.axis_index("win"), lax.axis_index("sub")
    group = per_device * STRIDE
    rows, width = out.shape[0], halves[0].shape[0]
    phase = phases[block_at]

    def ones_at(first, width):
        row = lax.broadcasted_iota(jnp.int32, (rows, width), 0)
        place = lax.broadcasted_iota(jnp.int32, (rows, width), 1)
        return row, place == first + phase + STRIDE * (row % per_device)

    row, here = ones_at((win_at * subs + sub_at) * group, mask.shape[1])
    alive = jnp.sum(jnp.where(here, mask[...].astype(jnp.float32), 0.0), axis=1, keepdims=True)
    row, here = ones_at(win_at * group, width)
    total = jnp.zeros(out.shape, jnp.float32)
    for behind in range(windows):
        chosen = jnp.where(here & (row // per_device == behind), 1.0, 0.0).astype(jnp.bfloat16)
        total += jnp.dot(chosen, halves[behind][...], preferred_element_type=jnp.float32)
    out[...] = total * alive


def setup_kernel(chunks, traces, table, widths, *refs):
    owns, (weights, share, rows_kept, table_kept, sems, *scratch) = refs[:len(chunks)], refs[len(chunks):]
    depth = table.shape[0] // TABLE_PARTS
    needed = chunks[-1][0] + chunks[-1][1]
    rest = rows_kept.shape[0] - needed
    first_rows = pltpu.make_async_copy(traces.at[0, pl.ds(0, needed)], rows_kept.at[pl.ds(0, needed)], sems.at[TABLE_PARTS])
    first_rows.start()
    parts = []
    for i in range(TABLE_PARTS):
        span = pl.ds(i * depth, depth)
        parts.append(pltpu.make_async_copy(table.at[span], table_kept.at[span], sems.at[i]))
        parts[-1].start()
    if rest:
        span = pl.ds(needed, rest)
        last_rows = pltpu.make_async_copy(traces.at[0, span], rows_kept.at[span], sems.at[TABLE_PARTS + 1])
        last_rows.start()
    widths_kept, = scratch
    fetched = pltpu.make_async_copy(widths, widths_kept, sems.at[TABLE_PARTS + 2])
    fetched.start()
    fetched.wait()
    reach = widths_kept[...]
    near = lax.broadcasted_iota(jnp.int32, (NB, NB), 0)
    here = lax.broadcasted_iota(jnp.int32, (NB, NB), 1)
    weights[...] = jnp.where(jnp.abs(near - here) <= reach, 1.0, 0.0).astype(jnp.bfloat16)
    bins = lax.broadcasted_iota(jnp.int32, (1, NB), 1)
    count = jnp.minimum(bins + reach, NB - 1) - jnp.maximum(bins - reach, 0) + 1
    share[...] = 1.0 / count.astype(jnp.float32)
    first_rows.wait()
    for part in parts:
        part.wait()
    for (start, size), own in zip(chunks, owns):
        own_kernel(start, rows_kept, table_kept, weights, share, own)
    if rest:
        last_rows.wait()


def own_kernel(start, rows, table, weights, share, out):
    real, imag = whiten(rows[start:start + out.shape[0], :], table[...], weights[...], share[...])
    out[:, :NB] = real
    out[:, NB:] = imag


def turn_kernel(layout, table, weights, share, lags, *refs):
    per_device, windows, places = layout
    even = lax.axis_index("sub") % 2 == 0
    picked, turned, spectra = refs[:-2], refs[-2], refs[-1]
    rows = jnp.concatenate([p[...].astype(jnp.float32) for p in picked], axis=0).astype(jnp.bfloat16)
    real, imag = whiten(rows, table[...], weights[...], share[...])
    spectra[:, :NB] = real.astype(jnp.float32)
    spectra[:, NB:] = imag.astype(jnp.float32)
    side = side_rows(per_device)
    span = 2 * side
    which = lax.broadcasted_iota(jnp.int32, (8, LANES), 0) % per_device

    def rows_of(first, lane):
        tiled = jnp.zeros((8, LANES), jnp.float32)
        for v in range(per_device):
            rows = [spectra[f + v:f + v + 1, lane:lane + LANES] for f in first]
            row = rows[0] if first[0] == first[-1] else jnp.where(even, rows[0], rows[-1])
            tiled = jnp.where(which == v, row, tiled)
        return tiled[None]

    for lane in range(0, NB, LANES):
        cosine = lags[:, lane:lane + LANES].reshape(side // 8, 8, LANES)
        sine = lags[:, NB + lane:NB + lane + LANES].reshape(side // 8, 8, LANES)
        for at, place in enumerate(places):
            for behind in range(windows):
                first = [(here * windows + behind) * per_device for here in place]
                real, imag = rows_of(first, lane), rows_of(first, NB + lane)
                cr, si, sr, ci = cosine * real, sine * imag, sine * real, cosine * imag
                up = jnp.concatenate([cr - si, cr + si], axis=0).reshape(span, LANES)
                down = jnp.concatenate([ci + sr, ci - sr], axis=0).reshape(span, LANES)
                spot = pl.ds(at * span, span)
                turned[behind, spot, lane:lane + LANES] = up.astype(jnp.bfloat16)
                turned[behind, spot, NB + lane:NB + lane + LANES] = down.astype(jnp.bfloat16)


def others_kernel(table, weights, share, *refs):
    parts, (white, raw) = refs[:-2], refs[-2:]
    sub_at = lax.axis_index("sub")
    groups, _, group, samples = raw.shape
    each = len(parts) // white.shape[0]
    for i in range(white.shape[0]):
        if each == 1:
            rows = parts[i][...]
        else:
            for half, place in ((parts[2 * i], sub_at), (parts[2 * i + 1], 1 - sub_at)):
                raw[:, pl.ds(place, 1)] = half[...].reshape(groups, 1, group, samples)
            rows = raw[...].reshape(white.shape[1], samples)
        real, imag = whiten(rows, table[...], weights[...], share[...])
        white[i, :, :NB] = real
        white[i, :, NB:] = imag


def lag_product(turned, own, white):
    total = lax.dot_general(turned[0], own[...], NT, preferred_element_type=jnp.float32)
    for i in range(white.shape[0]):
        total += lax.dot_general(turned[1 + i], white[i], NT, preferred_element_type=jnp.float32)
    return total


def base_kernel(turned, own, base):
    base[...] = lax.dot_general(turned[0], own[...], NT, preferred_element_type=jnp.float32)


def lag_kernel(factor, based, turned, own, white, mask, *pieces):
    if based:
        total = own[...]
        for i in range(white.shape[0]):
            total += lax.dot_general(turned[1 + i], white[i], NT, preferred_element_type=jnp.float32)
    else:
        total = lag_product(turned, own, white)
    result = total * (mask[...].astype(jnp.float32) * factor)
    span = result.shape[0] // len(pieces)
    for at, piece in enumerate(pieces):
        piece[...] = result[at * span:(at + 1) * span, :].astype(jnp.bfloat16)


def put_slots(layout, listed, wide, out, stage, sems, slot):
    tie, blocks, per_device, first, reverse = layout
    block_at, tie = lax.axis_index("chan"), on_core(tie, lax.axis_index("sub"))
    row = lax.broadcasted_iota(jnp.int32, listed.shape, 0)
    column = lax.broadcasted_iota(jnp.int32, listed.shape, 1)
    width = stage.shape[3]
    block = block_at if reverse else partner(block_at, blocks, tie)
    copies = []
    for e in offsets_of(block_at, blocks, tie, reverse):
        chosen = jnp.where((row == block) & (column == e), listed, 0.0)
        pair = jnp.broadcast_to(jnp.sum(chosen, keepdims=True), (per_device, width))
        for t in range(LAGS):
            tau = MAXLAG - t if reverse else t - MAXLAG
            spot = lag_row(tau, per_device)
            stage[slot, t] = wide[spot:spot + per_device, :] * pair
        target = out.at[e, :, :, pl.ds(first, width)]
        copies.append(pltpu.make_async_copy(stage.at[slot], target, sems.at[slot]))
        copies[-1].start()
        slot += 1
    return copies


def receiver_kernel(layout, pairs, turned, mask, *refs):
    ties, blocks, per_device, chunks, factor = layout
    count = len(chunks)
    owns, whites, pieces = refs[:count], refs[count:2 * count], refs[2 * count:-5]
    out, source_out, wide, stage, sems = refs[-5:]
    listed = pairs[...].astype(jnp.float32)
    copies = []
    for at, tie in enumerate(ties):
        for i, (start, size) in enumerate(chunks):
            lanes = slice(start, start + size)
            if at:
                wide[at, :, lanes] = pieces[i * (len(ties) - 1) + at - 1][...].astype(jnp.float32)
            else:
                wide[at, :, lanes] = lag_product(turned, owns[i], whites[i]) * (mask[:, lanes].astype(jnp.float32) * factor)
        turns = [(out, False)] + ([] if at else [(source_out, True)])
        for target, reverse in turns:
            part = (tie, blocks, per_device, 0, reverse)
            copies += put_slots(part, listed, wide.at[at], target, stage, sems, len(copies))
    for copy in copies:
        copy.wait()


def source_kernel(layout, pairs, *refs):
    ties, blocks, per_device, first = layout
    pieces, (_, out, wide, stage, sems) = refs[:len(ties)], refs[len(ties):]
    listed = pairs[...].astype(jnp.float32)
    copies = []
    for at, tie in enumerate(ties):
        wide[at] = pieces[at][...].astype(jnp.float32)
        part = (tie, blocks, per_device, first, True)
        copies += put_slots(part, listed, wide.at[at], out, stage, sems, len(copies))
    for copy in copies:
        copy.wait()


def ties_of(blocks, subs):
    if blocks == 4:
        own = [("xor", (0,) * subs)]
        return own + [("xor", tuple(4 - step if c % 2 else step for c in range(subs))) for step in (1, 2, 3)]
    ties = []
    for moved in (0, 1, -1, 2, -2):
        if all((m[0] - moved) % blocks for _, m in ties):
            ties.append(("shift", (moved,) * subs))
    return ties


def on_core(tie, core):
    kind, steps = tie
    if len(set(steps)) == 1:
        return kind, steps[0]
    return kind, jnp.where(core % 2 == 0, steps[0], steps[1])


def partner(block, blocks, tie, back=False):
    kind, step = tie
    if kind == "xor":
        return block ^ step
    return (block + (step if back else -step) + blocks) % blocks


def offsets_of(block, blocks, tie, back):
    kind, step = tie
    if kind == "shift":
        return [e for e in range(OFFS) if (e - REACH - step) % blocks == 0]
    if isinstance(step, int) and step % 2 == 0:
        return [e for e in range(OFFS) if abs(e - REACH) == step]
    ahead = (block ^ step) - block if back else block - (block ^ step)
    return [jnp.where((ahead + blocks) % blocks == 1, REACH + 1, REACH - 1)]


def exchange(value, blocks, subs, tie, back=False):
    kind, steps = tie
    route = [
        (partner(b, blocks, (kind, steps[c]), back) * subs + c, b * subs + c)
        for b in range(blocks)
        for c in range(subs)
    ]
    return lax.ppermute(value, ("chan", "sub"), route)


def chunks_of(channels):
    if channels < 2 * LANES or channels % LANES:
        return [(0, channels)]
    first = channels * 2 // 5 // LANES * LANES
    return [(0, first), (first, channels - first)]


def shift(block, axis, distance):
    count = lax.axis_size(axis)
    return lax.ppermute(block, axis, [(i, (i + distance) % count) for i in range(count)])


def slots_of(ties, blocks):
    return sum(len(offsets_of(0, blocks, (kind, steps[0]), False)) for kind, steps in ties)


def in_hbm(value):
    return pltpu.with_memory_space_constraint(value, pltpu.HBM)


def after(value, *others):
    return lax.optimization_barrier((value, *others))[0]


def on_device(traces, channel_mask, smooth_width, source_phase, pair_list):
    _, channels, samples = traces.shape
    blocks, windows, subs = (lax.axis_size(a) for a in ("chan", "win", "sub"))
    sub_at = lax.axis_index("sub")
    per_device = VS // (windows * subs)
    group = per_device * STRIDE
    ties = ties_of(blocks, subs)
    span = 2 * side_rows(per_device)
    chunks = chunks_of(channels)
    table, lags = dft_table(samples), lag_table(samples, per_device)
    factor = (NB * windows) ** (-0.5)
    bf16, f32 = jnp.bfloat16, jnp.float32
    like = jax.ShapeDtypeStruct
    mask_row = channel_mask.reshape(1, channels)

    def half_of(rows, start, size):
        grouped = rows.reshape(channels // (subs * group), subs, group, samples)
        first, count = start // (subs * group), size // (subs * group)
        half = lax.dynamic_slice(grouped, (first, sub_at, 0, 0), (count, 1, group, samples))
        return half.reshape(size // subs, samples)

    def from_windows(half):
        return [shift(half, "win", d) for d in range(1, windows)]

    def with_other_core(received):
        return [side for piece in received for side in (piece, shift(piece, "sub", 1))]

    def whiten_others(size, both, hint):
        return pl.pallas_call(
            others_kernel,
            out_shape=like((windows - 1, size, 2 * NB), bf16),
            in_specs=[VMEM] * (3 + len(both)),
            out_specs=VMEM,
            scratch_shapes=[pltpu.VMEM((size // (subs * group), subs, group, samples), bf16)],
            compiler_params=params(24),
            cost_estimate=hint,
            name="whiten_others",
        )(table, weights, share, *both)

    def correlate(start, size, turned, own, white, hint, based=False):
        count = turned.shape[1] // span
        return pl.pallas_call(
            functools.partial(lag_kernel, factor, based),
            out_shape=tuple(like((span, size), bf16) for _ in range(count)),
            in_specs=[VMEM] * 4,
            out_specs=(VMEM,) * count,
            compiler_params=params(24),
            cost_estimate=hint,
            name="lag_pieces",
        )(turned, own, white, mask_row[:, start:start + size])

    half = half_of(traces, *chunks[0])
    received = [from_windows(half)]
    *owns, weights, share, rows, table = pl.pallas_call(
        functools.partial(setup_kernel, chunks),
        out_shape=tuple(like((size, 2 * NB), bf16) for _, size in chunks)
        + (like((NB, NB), bf16), like((1, NB), f32))
        + (like((channels, samples), bf16), like(table.shape, bf16)),
        in_specs=[HBM, HBM, HBM],
        out_specs=(VMEM,) * (len(chunks) + 4),
        scratch_shapes=[pltpu.SemaphoreType.DMA((TABLE_PARTS + 3,)), pltpu.VMEM((1, NB), jnp.int32)],
        compiler_params=params(24),
        cost_estimate=SHORT,
        name="whiten_own",
    )(in_hbm(traces), in_hbm(table), in_hbm(after(smooth_width, half).reshape(1, NB)))
    received += [from_windows(after(rows, share)[a:a + n]) for a, n in chunks[1:]]
    near = pl.pallas_call(
        functools.partial(near_kernel, (windows, subs, per_device)),
        out_shape=like((windows * per_device, samples), f32),
        in_specs=[SMEM] + [VMEM] * (1 + windows),
        out_specs=VMEM,
        compiler_params=params(16),
        cost_estimate=SHORT,
        name="pick_sources",
    )(source_phase, after(mask_row, weights), half, *received[0])

    def turn(sources, places, hint, *first):
        rows_each = windows * per_device
        return pl.pallas_call(
            functools.partial(turn_kernel, (per_device, windows, places)),
            out_shape=like((windows, len(places) * span, 2 * NB), bf16),
            in_specs=[VMEM] * (4 + len(sources)),
            out_specs=VMEM,
            scratch_shapes=[pltpu.VMEM((len(places) * rows_each, 2 * NB), f32)],
            compiler_params=params(24),
            cost_estimate=hint,
            name="turn_sources",
        )(table, weights, after(share, *first), lags, *sources)

    turned_own = turn([near], [(0,)], LONG)
    inbound = with_other_core(received[0])
    white = whiten_others(chunks[0][1], inbound, SHORT)
    if ties[1][0] == "xor":
        beside = exchange(near, blocks, subs, ("xor", (1,) * subs))
        two = jnp.concatenate([after(near, turned_own), beside], axis=0).astype(bf16)
        sources = [beside, exchange(two, blocks, subs, ("xor", (2,) * subs))]
        places = [tuple(step - 1 for step in steps) for _, steps in ties[1:]]
    else:
        sources = [exchange(near, blocks, subs, tie) for tie in ties[1:]]
        places = [(at,) for at in range(len(sources))]
    turned = turn(sources, places, SHORT, white)
    pieces, arrived, whites = [], [], [white]
    for i, (start, size) in enumerate(chunks):
        if i:
            whites.append(whiten_others(size, [after(r, *pieces[-1]) for r in received[i]], LONG))
        own = owns[i]
        if i:
            own = pl.pallas_call(
                base_kernel,
                out_shape=like((turned.shape[1], size), f32),
                in_specs=[VMEM, VMEM],
                out_specs=VMEM,
                compiler_params=params(24),
                cost_estimate=SHORT,
                name="lag_base",
            )(after(turned, *pieces[-1]), own)
        pieces.append(correlate(start, size, turned, own, whites[i], LONG if i else SHORT, i > 0))
        ahead = arrived[-1][-1:] if i else []
        sent = [after(p, *ahead) for p in pieces[-1]]
        arrived.append([exchange(p, blocks, subs, tie, True) for tie, p in zip(ties[1:], sent)])
    stack = like((OFFS, LAGS, per_device, channels), f32)

    def scratch(count, slots, width):
        return [
            pltpu.VMEM((count, span, width), f32),
            pltpu.VMEM((slots, LAGS, per_device, width), f32),
            pltpu.SemaphoreType.DMA((slots,)),
        ]

    remote = [piece for group in pieces for piece in group]
    receiver_stack, source_stack = pl.pallas_call(
        functools.partial(receiver_kernel, (ties, blocks, per_device, chunks, factor)),
        out_shape=(stack, stack),
        in_specs=[VMEM] * (3 + 2 * len(chunks) + len(remote)),
        out_specs=(HBM, HBM),
        scratch_shapes=scratch(len(ties), slots_of(ties, blocks) + 1, channels),
        compiler_params=params(24),
        cost_estimate=LONG,
        name="receiver_order",
    )(pair_list, turned_own, mask_row, *owns, *whites, *remote)
    slots = slots_of(ties[1:], blocks)
    for (start, size), back in zip(chunks, arrived):
        source_stack = pl.pallas_call(
            functools.partial(source_kernel, (ties[1:], blocks, per_device, start)),
            out_shape=stack,
            in_specs=[VMEM] * (1 + len(back)) + [HBM],
            out_specs=HBM,
            scratch_shapes=scratch(len(back), slots, size),
            input_output_aliases={1 + len(back): 0},
            compiler_params=params(16),
            cost_estimate=SHORT,
            name="source_order",
        )(pair_list, *back, source_stack)
    order = (2, 0, 1, 3)
    return (jnp.transpose(receiver_stack, order), jnp.transpose(source_stack, order))


def solution(mesh):
    in_specs = (
        P(("groups", "win"), "chan", None),
        P(("groups", "chan")),
        P(),
        P("groups"),
        P("groups", None),
    )
    out_specs = (
        P(("win", "sub"), None, None, ("groups", "chan")),
        P(("groups", "chan", "win", "sub"), None, None, None),
    )
    return jax.shard_map(
        on_device, mesh=mesh, in_specs=in_specs, out_specs=out_specs, check_vma=False
    )
```

```python
import functools
import math

import jax
import jax.numpy as jnp
import numpy as np
from jax import lax
from jax.experimental import pallas as pl
from jax.experimental.pallas import tpu as pltpu
from jax.sharding import PartitionSpec as P

NB = 512
MAXLAG = 50
STRIDE = 8
REACH = 2
VS = 8
OFFS = 5
LAGS = 2 * MAXLAG + 1
FLOOR = 0.25
TABLE_PARTS = 4
LANES = 128
VMEM = pl.BlockSpec(memory_space=pltpu.VMEM)
SMEM = pl.BlockSpec(memory_space=pltpu.SMEM)
HBM = pl.BlockSpec(memory_space=pltpu.HBM)
NT = (((1,), (1,)), ((), ()))


def dft_table(samples):
    phases = np.arange(samples)[:, None] * np.arange(NB)[None, :] % samples
    angles = phases * (2.0 * math.pi / samples)
    table = np.concatenate([np.cos(angles), -np.sin(angles)], axis=1)
    return jnp.asarray(table.astype(np.float32), jnp.bfloat16)


def side_rows(per_device):
    return -(-(MAXLAG + 1) * per_device // 8) * 8


def lag_row(tau, per_device):
    return abs(tau) * per_device + (0 if tau >= 0 else side_rows(per_device))


def lag_table(samples, per_device):
    lag = np.arange(side_rows(per_device)) // per_device
    angles = (lag[:, None] * np.arange(NB)[None, :] % samples) * (2.0 * math.pi / samples)
    table = np.concatenate([np.cos(angles), np.sin(angles)], axis=1)
    return jnp.asarray(table, jnp.float32)


def params(mib):
    return pltpu.CompilerParams(vmem_limit_bytes=mib << 20)


def cost(flops, moved):
    return pl.CostEstimate(flops=flops, bytes_accessed=moved, transcendentals=0)


SHORT, LONG = cost(1 << 20, 1 << 18), cost(1 << 33, 1 << 26)


def whiten(rows, table, weights, share):
    samples = rows.shape[1]
    spectrum = jnp.dot(rows, table, preferred_element_type=jnp.float32) * samples ** (-0.5)
    real, imag = spectrum[:, :NB], spectrum[:, NB:]
    amplitude = jnp.sqrt(real * real + imag * imag)
    high = amplitude.astype(jnp.bfloat16)
    low = (amplitude - high.astype(jnp.float32)).astype(jnp.bfloat16)
    total = jnp.dot(high, weights, preferred_element_type=jnp.float32)
    total += jnp.dot(low, weights, preferred_element_type=jnp.float32)
    gain = 1.0 / jnp.maximum(total * share, FLOOR)
    return (real * gain).astype(jnp.bfloat16), (imag * gain).astype(jnp.bfloat16)


def near_kernel(layout, phases, mask, *refs):
    windows, subs, per_device = layout
    halves, out = refs[:-1], refs[-1]
    block_at, win_at, sub_at = lax.axis_index("chan"), lax.axis_index("win"), lax.axis_index("sub")
    group = per_device * STRIDE
    rows, width = out.shape[0], halves[0].shape[0]
    phase = phases[block_at]

    def ones_at(first, width):
        row = lax.broadcasted_iota(jnp.int32, (rows, width), 0)
        place = lax.broadcasted_iota(jnp.int32, (rows, width), 1)
        return row, place == first + phase + STRIDE * (row % per_device)

    row, here = ones_at((win_at * subs + sub_at) * group, mask.shape[1])
    alive = jnp.sum(jnp.where(here, mask[...].astype(jnp.float32), 0.0), axis=1, keepdims=True)
    row, here = ones_at(win_at * group, width)
    total = jnp.zeros(out.shape, jnp.float32)
    for behind in range(windows):
        chosen = jnp.where(here & (row // per_device == behind), 1.0, 0.0).astype(jnp.bfloat16)
        total += jnp.dot(chosen, halves[behind][...], preferred_element_type=jnp.float32)
    out[...] = total * alive


def setup_kernel(chunks, traces, table, widths, *refs):
    owns, (weights, share, rows_kept, table_kept, sems, *scratch) = refs[:len(chunks)], refs[len(chunks):]
    depth = table.shape[0] // TABLE_PARTS
    needed = chunks[-1][0] + chunks[-1][1]
    rest = rows_kept.shape[0] - needed
    first_rows = pltpu.make_async_copy(traces.at[0, pl.ds(0, needed)], rows_kept.at[pl.ds(0, needed)], sems.at[TABLE_PARTS])
    first_rows.start()
    parts = []
    for i in range(TABLE_PARTS):
        span = pl.ds(i * depth, depth)
        parts.append(pltpu.make_async_copy(table.at[span], table_kept.at[span], sems.at[i]))
        parts[-1].start()
    if rest:
        span = pl.ds(needed, rest)
        last_rows = pltpu.make_async_copy(traces.at[0, span], rows_kept.at[span], sems.at[TABLE_PARTS + 1])
        last_rows.start()
    widths_kept, = scratch
    fetched = pltpu.make_async_copy(widths, widths_kept, sems.at[TABLE_PARTS + 2])
    fetched.start()
    fetched.wait()
    reach = widths_kept[...]
    near = lax.broadcasted_iota(jnp.int32, (NB, NB), 0)
    here = lax.broadcasted_iota(jnp.int32, (NB, NB), 1)
    weights[...] = jnp.where(jnp.abs(near - here) <= reach, 1.0, 0.0).astype(jnp.bfloat16)
    bins = lax.broadcasted_iota(jnp.int32, (1, NB), 1)
    count = jnp.minimum(bins + reach, NB - 1) - jnp.maximum(bins - reach, 0) + 1
    share[...] = 1.0 / count.astype(jnp.float32)
    first_rows.wait()
    for part in parts:
        part.wait()
    for (start, size), own in zip(chunks, owns):
        own_kernel(start, rows_kept, table_kept, weights, share, own)
    if rest:
        last_rows.wait()


def own_kernel(start, rows, table, weights, share, out):
    real, imag = whiten(rows[start:start + out.shape[0], :], table[...], weights[...], share[...])
    out[:, :NB] = real
    out[:, NB:] = imag


def turn_kernel(layout, table, weights, share, lags, *refs):
    per_device, windows, places = layout
    even = lax.axis_index("sub") % 2 == 0
    picked, turned, spectra = refs[:-2], refs[-2], refs[-1]
    rows = jnp.concatenate([p[...].astype(jnp.float32) for p in picked], axis=0).astype(jnp.bfloat16)
    real, imag = whiten(rows, table[...], weights[...], share[...])
    spectra[:, :NB] = real.astype(jnp.float32)
    spectra[:, NB:] = imag.astype(jnp.float32)
    side = side_rows(per_device)
    span = 2 * side
    which = lax.broadcasted_iota(jnp.int32, (8, LANES), 0) % per_device

    def rows_of(first, lane):
        tiled = jnp.zeros((8, LANES), jnp.float32)
        for v in range(per_device):
            rows = [spectra[f + v:f + v + 1, lane:lane + LANES] for f in first]
            row = rows[0] if first[0] == first[-1] else jnp.where(even, rows[0], rows[-1])
            tiled = jnp.where(which == v, row, tiled)
        return tiled[None]

    for lane in range(0, NB, LANES):
        cosine = lags[:, lane:lane + LANES].reshape(side // 8, 8, LANES)
        sine = lags[:, NB + lane:NB + lane + LANES].reshape(side // 8, 8, LANES)
        for at, place in enumerate(places):
            for behind in range(windows):
                first = [(here * windows + behind) * per_device for here in place]
                real, imag = rows_of(first, lane), rows_of(first, NB + lane)
                cr, si, sr, ci = cosine * real, sine * imag, sine * real, cosine * imag
                up = jnp.concatenate([cr - si, cr + si], axis=0).reshape(span, LANES)
                down = jnp.concatenate([ci + sr, ci - sr], axis=0).reshape(span, LANES)
                spot = pl.ds(at * span, span)
                turned[behind, spot, lane:lane + LANES] = up.astype(jnp.bfloat16)
                turned[behind, spot, NB + lane:NB + lane + LANES] = down.astype(jnp.bfloat16)


def others_kernel(table, weights, share, *refs):
    parts, (white, raw) = refs[:-2], refs[-2:]
    sub_at = lax.axis_index("sub")
    groups, _, group, samples = raw.shape
    each = len(parts) // white.shape[0]
    for i in range(white.shape[0]):
        if each == 1:
            rows = parts[i][...]
        else:
            for half, place in ((parts[2 * i], sub_at), (parts[2 * i + 1], 1 - sub_at)):
                raw[:, pl.ds(place, 1)] = half[...].reshape(groups, 1, group, samples)
            rows = raw[...].reshape(white.shape[1], samples)
        real, imag = whiten(rows, table[...], weights[...], share[...])
        white[i, :, :NB] = real
        white[i, :, NB:] = imag


def lag_product(turned, own, white):
    total = lax.dot_general(turned[0], own[...], NT, preferred_element_type=jnp.float32)
    for i in range(white.shape[0]):
        total += lax.dot_general(turned[1 + i], white[i], NT, preferred_element_type=jnp.float32)
    return total


def base_kernel(turned, own, base):
    base[...] = lax.dot_general(turned[0], own[...], NT, preferred_element_type=jnp.float32)


def lag_kernel(factor, based, turned, own, white, mask, *pieces):
    if based:
        total = own[...]
        for i in range(white.shape[0]):
            total += lax.dot_general(turned[1 + i], white[i], NT, preferred_element_type=jnp.float32)
    else:
        total = lag_product(turned, own, white)
    result = total * (mask[...].astype(jnp.float32) * factor)
    span = result.shape[0] // len(pieces)
    for at, piece in enumerate(pieces):
        piece[...] = result[at * span:(at + 1) * span, :].astype(jnp.bfloat16)


def put_slots(layout, listed, wide, out, stage, sems, slot):
    tie, blocks, per_device, first, reverse = layout
    block_at, tie = lax.axis_index("chan"), on_core(tie, lax.axis_index("sub"))
    row = lax.broadcasted_iota(jnp.int32, listed.shape, 0)
    column = lax.broadcasted_iota(jnp.int32, listed.shape, 1)
    width = stage.shape[3]
    block = block_at if reverse else partner(block_at, blocks, tie)
    copies = []
    for e in offsets_of(block_at, blocks, tie, reverse):
        chosen = jnp.where((row == block) & (column == e), listed, 0.0)
        pair = jnp.broadcast_to(jnp.sum(chosen, keepdims=True), (per_device, width))
        for t in range(LAGS):
            tau = MAXLAG - t if reverse else t - MAXLAG
            spot = lag_row(tau, per_device)
            stage[slot, t] = wide[spot:spot + per_device, :] * pair
        target = out.at[e, :, :, pl.ds(first, width)]
        copies.append(pltpu.make_async_copy(stage.at[slot], target, sems.at[slot]))
        copies[-1].start()
        slot += 1
    return copies


def receiver_kernel(layout, pairs, turned, mask, *refs):
    ties, blocks, per_device, chunks, factor = layout
    count = len(chunks)
    owns, whites, pieces = refs[:count], refs[count:2 * count], refs[2 * count:-5]
    out, source_out, wide, stage, sems = refs[-5:]
    listed = pairs[...].astype(jnp.float32)
    copies = []
    for at, tie in enumerate(ties):
        for i, (start, size) in enumerate(chunks):
            lanes = slice(start, start + size)
            if at:
                wide[at, :, lanes] = pieces[i * (len(ties) - 1) + at - 1][...].astype(jnp.float32)
            else:
                wide[at, :, lanes] = lag_product(turned, owns[i], whites[i]) * (mask[:, lanes].astype(jnp.float32) * factor)
        turns = [(out, False)] + ([] if at else [(source_out, True)])
        for target, reverse in turns:
            part = (tie, blocks, per_device, 0, reverse)
            copies += put_slots(part, listed, wide.at[at], target, stage, sems, len(copies))
    for copy in copies:
        copy.wait()


def source_kernel(layout, pairs, *refs):
    ties, blocks, per_device, first = layout
    pieces, (_, out, wide, stage, sems) = refs[:len(ties)], refs[len(ties):]
    listed = pairs[...].astype(jnp.float32)
    copies = []
    for at, tie in enumerate(ties):
        wide[at] = pieces[at][...].astype(jnp.float32)
        part = (tie, blocks, per_device, first, True)
        copies += put_slots(part, listed, wide.at[at], out, stage, sems, len(copies))
    for copy in copies:
        copy.wait()


def ties_of(blocks, subs):
    if blocks == 4:
        return [("xor", (step,) * subs) for step in (0, 3, 2, 1)]
    ties = []
    for moved in (0, 1, -1, 2, -2):
        if all((m[0] - moved) % blocks for _, m in ties):
            ties.append(("shift", (moved,) * subs))
    return ties


def on_core(tie, core):
    kind, steps = tie
    if len(set(steps)) == 1:
        return kind, steps[0]
    return kind, jnp.where(core % 2 == 0, steps[0], steps[1])


def partner(block, blocks, tie, back=False):
    kind, step = tie
    if kind == "xor":
        return block ^ step
    return (block + (step if back else -step) + blocks) % blocks


def offsets_of(block, blocks, tie, back):
    kind, step = tie
    if kind == "shift":
        return [e for e in range(OFFS) if (e - REACH - step) % blocks == 0]
    if isinstance(step, int) and step % 2 == 0:
        return [e for e in range(OFFS) if abs(e - REACH) == step]
    ahead = (block ^ step) - block if back else block - (block ^ step)
    return [jnp.where((ahead + blocks) % blocks == 1, REACH + 1, REACH - 1)]


def exchange(value, blocks, subs, tie, back=False):
    kind, steps = tie
    route = [
        (partner(b, blocks, (kind, steps[c]), back) * subs + c, b * subs + c)
        for b in range(blocks)
        for c in range(subs)
    ]
    return lax.ppermute(value, ("chan", "sub"), route)


def chunks_of(channels):
    if channels < 2 * LANES or channels % LANES:
        return [(0, channels)]
    first = channels * 2 // 5 // LANES * LANES
    return [(0, first), (first, channels - first)]


def shift(block, axis, distance):
    count = lax.axis_size(axis)
    return lax.ppermute(block, axis, [(i, (i + distance) % count) for i in range(count)])


def slots_of(ties, blocks):
    return sum(len(offsets_of(0, blocks, (kind, steps[0]), False)) for kind, steps in ties)


def in_hbm(value):
    return pltpu.with_memory_space_constraint(value, pltpu.HBM)


def after(value, *others):
    return lax.optimization_barrier((value, *others))[0]


def on_device(traces, channel_mask, smooth_width, source_phase, pair_list):
    _, channels, samples = traces.shape
    blocks, windows, subs = (lax.axis_size(a) for a in ("chan", "win", "sub"))
    sub_at = lax.axis_index("sub")
    per_device = VS // (windows * subs)
    group = per_device * STRIDE
    ties = ties_of(blocks, subs)
    span = 2 * side_rows(per_device)
    chunks = chunks_of(channels)
    table, lags = dft_table(samples), lag_table(samples, per_device)
    factor = (NB * windows) ** (-0.5)
    bf16, f32 = jnp.bfloat16, jnp.float32
    like = jax.ShapeDtypeStruct
    mask_row = channel_mask.reshape(1, channels)

    def half_of(rows, start, size):
        grouped = rows.reshape(channels // (subs * group), subs, group, samples)
        first, count = start // (subs * group), size // (subs * group)
        half = lax.dynamic_slice(grouped, (first, sub_at, 0, 0), (count, 1, group, samples))
        return half.reshape(size // subs, samples)

    def from_windows(half):
        return [shift(half, "win", d) for d in range(1, windows)]

    def with_other_core(received):
        return [side for piece in received for side in (piece, shift(piece, "sub", 1))]

    def whiten_others(size, both, hint):
        return pl.pallas_call(
            others_kernel,
            out_shape=like((windows - 1, size, 2 * NB), bf16),
            in_specs=[VMEM] * (3 + len(both)),
            out_specs=VMEM,
            scratch_shapes=[pltpu.VMEM((size // (subs * group), subs, group, samples), bf16)],
            compiler_params=params(24),
            cost_estimate=hint,
            name="whiten_others",
        )(table, weights, share, *both)

    def correlate(start, size, turned, own, white, hint, based=False):
        count = turned.shape[1] // span
        return pl.pallas_call(
            functools.partial(lag_kernel, factor, based),
            out_shape=tuple(like((span, size), bf16) for _ in range(count)),
            in_specs=[VMEM] * 4,
            out_specs=(VMEM,) * count,
            compiler_params=params(24),
            cost_estimate=hint,
            name="lag_pieces",
        )(turned, own, white, mask_row[:, start:start + size])

    half = half_of(traces, *chunks[0])
    received = [from_windows(half)]
    *owns, weights, share, rows, table = pl.pallas_call(
        functools.partial(setup_kernel, chunks),
        out_shape=tuple(like((size, 2 * NB), bf16) for _, size in chunks)
        + (like((NB, NB), bf16), like((1, NB), f32))
        + (like((channels, samples), bf16), like(table.shape, bf16)),
        in_specs=[HBM, HBM, HBM],
        out_specs=(VMEM,) * (len(chunks) + 4),
        scratch_shapes=[pltpu.SemaphoreType.DMA((TABLE_PARTS + 3,)), pltpu.VMEM((1, NB), jnp.int32)],
        compiler_params=params(24),
        cost_estimate=SHORT,
        name="whiten_own",
    )(in_hbm(traces), in_hbm(table), in_hbm(after(smooth_width, half).reshape(1, NB)))
    received += [from_windows(after(rows, share)[a:a + n]) for a, n in chunks[1:]]
    near = pl.pallas_call(
        functools.partial(near_kernel, (windows, subs, per_device)),
        out_shape=like((windows * per_device, samples), f32),
        in_specs=[SMEM] + [VMEM] * (1 + windows),
        out_specs=VMEM,
        compiler_params=params(16),
        cost_estimate=SHORT,
        name="pick_sources",
    )(source_phase, after(mask_row, weights), half, *received[0])

    def turn(sources, places, hint, *first):
        rows_each = windows * per_device
        return pl.pallas_call(
            functools.partial(turn_kernel, (per_device, windows, places)),
            out_shape=like((windows, len(places) * span, 2 * NB), bf16),
            in_specs=[VMEM] * (4 + len(sources)),
            out_specs=VMEM,
            scratch_shapes=[pltpu.VMEM((len(places) * rows_each, 2 * NB), f32)],
            compiler_params=params(24),
            cost_estimate=hint,
            name="turn_sources",
        )(table, weights, after(share, *first), lags, *sources)

    turned_own = turn([near], [(0,)], LONG)
    inbound = with_other_core(received[0])
    white = whiten_others(chunks[0][1], inbound, SHORT)
    if ties[1][0] == "xor":
        beside = exchange(near, blocks, subs, ("xor", (1,) * subs))
        two = jnp.concatenate([after(near, turned_own), beside], axis=0).astype(bf16)
        sources = [beside, exchange(two, blocks, subs, ("xor", (2,) * subs))]
        places = [tuple(step - 1 for step in steps) for _, steps in ties[1:]]
    else:
        sources = [exchange(near, blocks, subs, tie) for tie in ties[1:]]
        places = [(at,) for at in range(len(sources))]
    turned = turn(sources, places, SHORT, white)
    pieces, arrived, whites = [], [], [white]
    for i, (start, size) in enumerate(chunks):
        if i:
            whites.append(whiten_others(size, [after(r, *pieces[-1]) for r in received[i]], LONG))
        own = owns[i]
        if i:
            own = pl.pallas_call(
                base_kernel,
                out_shape=like((turned.shape[1], size), f32),
                in_specs=[VMEM, VMEM],
                out_specs=VMEM,
                compiler_params=params(24),
                cost_estimate=SHORT,
                name="lag_base",
            )(after(turned, *pieces[-1]), own)
        pieces.append(correlate(start, size, turned, own, whites[i], LONG if i else SHORT, i > 0))
        ahead = arrived[-1][:1] if i else []
        sent = [after(p, *ahead) for p in pieces[-1]]
        arrived.append([exchange(p, blocks, subs, tie, True) for tie, p in zip(ties[1:], sent)])
    stack = like((OFFS, LAGS, per_device, channels), f32)

    def scratch(count, slots, width):
        return [
            pltpu.VMEM((count, span, width), f32),
            pltpu.VMEM((slots, LAGS, per_device, width), f32),
            pltpu.SemaphoreType.DMA((slots,)),
        ]

    remote = [piece for group in pieces for piece in group]
    receiver_stack, source_stack = pl.pallas_call(
        functools.partial(receiver_kernel, (ties, blocks, per_device, chunks, factor)),
        out_shape=(stack, stack),
        in_specs=[VMEM] * (3 + 2 * len(chunks) + len(remote)),
        out_specs=(HBM, HBM),
        scratch_shapes=scratch(len(ties), slots_of(ties, blocks) + 1, channels),
        compiler_params=params(24),
        cost_estimate=LONG,
        name="receiver_order",
    )(pair_list, turned_own, mask_row, *owns, *whites, *remote)
    slots = slots_of(ties[1:], blocks)
    for (start, size), back in zip(chunks, arrived):
        source_stack = pl.pallas_call(
            functools.partial(source_kernel, (ties[1:], blocks, per_device, start)),
            out_shape=stack,
            in_specs=[VMEM] * (1 + len(back)) + [HBM],
            out_specs=HBM,
            scratch_shapes=scratch(len(back), slots, size),
            input_output_aliases={1 + len(back): 0},
            compiler_params=params(16),
            cost_estimate=SHORT,
            name="source_order",
        )(pair_list, *back, source_stack)
    order = (2, 0, 1, 3)
    return (jnp.transpose(receiver_stack, order), jnp.transpose(source_stack, order))


def solution(mesh):
    in_specs = (
        P(("groups", "win"), "chan", None),
        P(("groups", "chan")),
        P(),
        P("groups"),
        P("groups", None),
    )
    out_specs = (
        P(("win", "sub"), None, None, ("groups", "chan")),
        P(("groups", "chan", "win", "sub"), None, None, None),
    )
    return jax.shard_map(
        on_device, mesh=mesh, in_specs=in_specs, out_specs=out_specs, check_vma=False
    )
```

```python
import functools
import math

import jax
import jax.numpy as jnp
import numpy as np
from jax import lax
from jax.experimental import pallas as pl
from jax.experimental.pallas import tpu as pltpu
from jax.sharding import PartitionSpec as P

NB = 512
MAXLAG = 50
STRIDE = 8
REACH = 2
VS = 8
OFFS = 5
LAGS = 2 * MAXLAG + 1
FLOOR = 0.25
TABLE_PARTS = 4
LANES = 128
VMEM = pl.BlockSpec(memory_space=pltpu.VMEM)
SMEM = pl.BlockSpec(memory_space=pltpu.SMEM)
HBM = pl.BlockSpec(memory_space=pltpu.HBM)
NT = (((1,), (1,)), ((), ()))


def dft_table(samples):
    phases = np.arange(samples)[:, None] * np.arange(NB)[None, :] % samples
    angles = phases * (2.0 * math.pi / samples)
    table = np.concatenate([np.cos(angles), -np.sin(angles)], axis=1)
    return jnp.asarray(table.astype(np.float32), jnp.bfloat16)


def side_rows(per_device):
    return -(-(MAXLAG + 1) * per_device // 8) * 8


def lag_row(tau, per_device):
    return abs(tau) * per_device + (0 if tau >= 0 else side_rows(per_device))


def lag_table(samples, per_device):
    lag = np.arange(side_rows(per_device)) // per_device
    angles = (lag[:, None] * np.arange(NB)[None, :] % samples) * (2.0 * math.pi / samples)
    table = np.concatenate([np.cos(angles), np.sin(angles)], axis=1)
    return jnp.asarray(table, jnp.float32)


def params(mib):
    return pltpu.CompilerParams(vmem_limit_bytes=mib << 20)


def cost(flops, moved):
    return pl.CostEstimate(flops=flops, bytes_accessed=moved, transcendentals=0)


SHORT, LONG = cost(1 << 20, 1 << 18), cost(1 << 33, 1 << 26)


def whiten(rows, table, weights, share):
    samples = rows.shape[1]
    spectrum = jnp.dot(rows, table, preferred_element_type=jnp.float32) * samples ** (-0.5)
    real, imag = spectrum[:, :NB], spectrum[:, NB:]
    amplitude = jnp.sqrt(real * real + imag * imag)
    high = amplitude.astype(jnp.bfloat16)
    low = (amplitude - high.astype(jnp.float32)).astype(jnp.bfloat16)
    total = jnp.dot(high, weights, preferred_element_type=jnp.float32)
    total += jnp.dot(low, weights, preferred_element_type=jnp.float32)
    gain = 1.0 / jnp.maximum(total * share, FLOOR)
    return (real * gain).astype(jnp.bfloat16), (imag * gain).astype(jnp.bfloat16)


def near_kernel(layout, phases, mask, *refs):
    windows, subs, per_device = layout
    halves, out = refs[:-1], refs[-1]
    block_at, win_at, sub_at = lax.axis_index("chan"), lax.axis_index("win"), lax.axis_index("sub")
    group = per_device * STRIDE
    rows, width = out.shape[0], halves[0].shape[0]
    phase = phases[block_at]

    def ones_at(first, width):
        row = lax.broadcasted_iota(jnp.int32, (rows, width), 0)
        place = lax.broadcasted_iota(jnp.int32, (rows, width), 1)
        return row, place == first + phase + STRIDE * (row % per_device)

    row, here = ones_at((win_at * subs + sub_at) * group, mask.shape[1])
    alive = jnp.sum(jnp.where(here, mask[...].astype(jnp.float32), 0.0), axis=1, keepdims=True)
    row, here = ones_at(win_at * group, width)
    total = jnp.zeros(out.shape, jnp.float32)
    for behind in range(windows):
        chosen = jnp.where(here & (row // per_device == behind), 1.0, 0.0).astype(jnp.bfloat16)
        total += jnp.dot(chosen, halves[behind][...], preferred_element_type=jnp.float32)
    out[...] = total * alive


def setup_kernel(chunks, traces, table, widths, *refs):
    owns, (weights, share, rows_kept, table_kept, sems, *scratch) = refs[:len(chunks)], refs[len(chunks):]
    depth = table.shape[0] // TABLE_PARTS
    needed = chunks[-1][0] + chunks[-1][1]
    rest = rows_kept.shape[0] - needed
    first_rows = pltpu.make_async_copy(traces.at[0, pl.ds(0, needed)], rows_kept.at[pl.ds(0, needed)], sems.at[TABLE_PARTS])
    first_rows.start()
    parts = []
    for i in range(TABLE_PARTS):
        span = pl.ds(i * depth, depth)
        parts.append(pltpu.make_async_copy(table.at[span], table_kept.at[span], sems.at[i]))
        parts[-1].start()
    if rest:
        span = pl.ds(needed, rest)
        last_rows = pltpu.make_async_copy(traces.at[0, span], rows_kept.at[span], sems.at[TABLE_PARTS + 1])
        last_rows.start()
    widths_kept, = scratch
    fetched = pltpu.make_async_copy(widths, widths_kept, sems.at[TABLE_PARTS + 2])
    fetched.start()
    fetched.wait()
    reach = widths_kept[...]
    near = lax.broadcasted_iota(jnp.int32, (NB, NB), 0)
    here = lax.broadcasted_iota(jnp.int32, (NB, NB), 1)
    weights[...] = jnp.where(jnp.abs(near - here) <= reach, 1.0, 0.0).astype(jnp.bfloat16)
    bins = lax.broadcasted_iota(jnp.int32, (1, NB), 1)
    count = jnp.minimum(bins + reach, NB - 1) - jnp.maximum(bins - reach, 0) + 1
    share[...] = 1.0 / count.astype(jnp.float32)
    first_rows.wait()
    for part in parts:
        part.wait()
    for (start, size), own in zip(chunks, owns):
        own_kernel(start, rows_kept, table_kept, weights, share, own)
    if rest:
        last_rows.wait()


def own_kernel(start, rows, table, weights, share, out):
    real, imag = whiten(rows[start:start + out.shape[0], :], table[...], weights[...], share[...])
    out[:, :NB] = real
    out[:, NB:] = imag


def turn_kernel(layout, table, weights, share, lags, *refs):
    per_device, windows, places = layout
    even = lax.axis_index("sub") % 2 == 0
    picked, turned, spectra = refs[:-2], refs[-2], refs[-1]
    rows = jnp.concatenate([p[...].astype(jnp.float32) for p in picked], axis=0).astype(jnp.bfloat16)
    real, imag = whiten(rows, table[...], weights[...], share[...])
    spectra[:, :NB] = real.astype(jnp.float32)
    spectra[:, NB:] = imag.astype(jnp.float32)
    side = side_rows(per_device)
    span = 2 * side
    which = lax.broadcasted_iota(jnp.int32, (8, LANES), 0) % per_device

    def rows_of(first, lane):
        tiled = jnp.zeros((8, LANES), jnp.float32)
        for v in range(per_device):
            rows = [spectra[f + v:f + v + 1, lane:lane + LANES] for f in first]
            row = rows[0] if first[0] == first[-1] else jnp.where(even, rows[0], rows[-1])
            tiled = jnp.where(which == v, row, tiled)
        return tiled[None]

    for lane in range(0, NB, LANES):
        cosine = lags[:, lane:lane + LANES].reshape(side // 8, 8, LANES)
        sine = lags[:, NB + lane:NB + lane + LANES].reshape(side // 8, 8, LANES)
        for at, place in enumerate(places):
            for behind in range(windows):
                first = [(here * windows + behind) * per_device for here in place]
                real, imag = rows_of(first, lane), rows_of(first, NB + lane)
                cr, si, sr, ci = cosine * real, sine * imag, sine * real, cosine * imag
                up = jnp.concatenate([cr - si, cr + si], axis=0).reshape(span, LANES)
                down = jnp.concatenate([ci + sr, ci - sr], axis=0).reshape(span, LANES)
                spot = pl.ds(at * span, span)
                turned[behind, spot, lane:lane + LANES] = up.astype(jnp.bfloat16)
                turned[behind, spot, NB + lane:NB + lane + LANES] = down.astype(jnp.bfloat16)


def others_kernel(table, weights, share, *refs):
    parts, (white, raw) = refs[:-2], refs[-2:]
    sub_at = lax.axis_index("sub")
    groups, _, group, samples = raw.shape
    each = len(parts) // white.shape[0]
    for i in range(white.shape[0]):
        if each == 1:
            rows = parts[i][...]
        else:
            for half, place in ((parts[2 * i], sub_at), (parts[2 * i + 1], 1 - sub_at)):
                raw[:, pl.ds(place, 1)] = half[...].reshape(groups, 1, group, samples)
            rows = raw[...].reshape(white.shape[1], samples)
        real, imag = whiten(rows, table[...], weights[...], share[...])
        white[i, :, :NB] = real
        white[i, :, NB:] = imag


def lag_product(turned, own, white):
    total = lax.dot_general(turned[0], own[...], NT, preferred_element_type=jnp.float32)
    for i in range(white.shape[0]):
        total += lax.dot_general(turned[1 + i], white[i], NT, preferred_element_type=jnp.float32)
    return total


def base_kernel(turned, own, base):
    base[...] = lax.dot_general(turned[0], own[...], NT, preferred_element_type=jnp.float32)


def lag_kernel(factor, based, turned, own, white, mask, *pieces):
    if based:
        total = own[...]
        for i in range(white.shape[0]):
            total += lax.dot_general(turned[1 + i], white[i], NT, preferred_element_type=jnp.float32)
    else:
        total = lag_product(turned, own, white)
    result = total * (mask[...].astype(jnp.float32) * factor)
    span = result.shape[0] // len(pieces)
    for at, piece in enumerate(pieces):
        piece[...] = result[at * span:(at + 1) * span, :].astype(jnp.bfloat16)


def first_kernel(layout, factor, count, table, weights, share, lags, own, white, mask, *refs):
    sources, (turned, *pieces, spectra) = refs[:count], refs[count:]
    turn_kernel(layout, table, weights, share, lags, *sources, turned, spectra)
    lag_kernel(factor, False, turned, own, white, mask, *pieces)


def put_slots(layout, listed, wide, out, stage, sems, slot):
    tie, blocks, per_device, first, reverse = layout
    block_at, tie = lax.axis_index("chan"), on_core(tie, lax.axis_index("sub"))
    row = lax.broadcasted_iota(jnp.int32, listed.shape, 0)
    column = lax.broadcasted_iota(jnp.int32, listed.shape, 1)
    width = stage.shape[3]
    block = block_at if reverse else partner(block_at, blocks, tie)
    copies = []
    for e in offsets_of(block_at, blocks, tie, reverse):
        chosen = jnp.where((row == block) & (column == e), listed, 0.0)
        pair = jnp.broadcast_to(jnp.sum(chosen, keepdims=True), (per_device, width))
        for t in range(LAGS):
            tau = MAXLAG - t if reverse else t - MAXLAG
            spot = lag_row(tau, per_device)
            stage[slot, t] = wide[spot:spot + per_device, :] * pair
        target = out.at[e, :, :, pl.ds(first, width)]
        copies.append(pltpu.make_async_copy(stage.at[slot], target, sems.at[slot]))
        copies[-1].start()
        slot += 1
    return copies


def receiver_kernel(layout, pairs, turned, mask, *refs):
    ties, blocks, per_device, chunks, factor = layout
    count = len(chunks)
    owns, whites, pieces = refs[:count], refs[count:2 * count], refs[2 * count:-5]
    out, source_out, wide, stage, sems = refs[-5:]
    listed = pairs[...].astype(jnp.float32)
    copies = []
    for at, tie in enumerate(ties):
        for i, (start, size) in enumerate(chunks):
            lanes = slice(start, start + size)
            if at:
                wide[at, :, lanes] = pieces[i * (len(ties) - 1) + at - 1][...].astype(jnp.float32)
            else:
                wide[at, :, lanes] = lag_product(turned, owns[i], whites[i]) * (mask[:, lanes].astype(jnp.float32) * factor)
        turns = [(out, False)] + ([] if at else [(source_out, True)])
        for target, reverse in turns:
            part = (tie, blocks, per_device, 0, reverse)
            copies += put_slots(part, listed, wide.at[at], target, stage, sems, len(copies))
    for copy in copies:
        copy.wait()


def source_kernel(layout, pairs, *refs):
    ties, blocks, per_device, first = layout
    pieces, (_, out, wide, stage, sems) = refs[:len(ties)], refs[len(ties):]
    listed = pairs[...].astype(jnp.float32)
    copies = []
    for at, tie in enumerate(ties):
        wide[at] = pieces[at][...].astype(jnp.float32)
        part = (tie, blocks, per_device, first, True)
        copies += put_slots(part, listed, wide.at[at], out, stage, sems, len(copies))
    for copy in copies:
        copy.wait()


def ties_of(blocks, subs):
    if blocks == 4:
        return [("xor", (step,) * subs) for step in (0, 2, 3, 1)]
    ties = []
    for moved in (0, 1, -1, 2, -2):
        if all((m[0] - moved) % blocks for _, m in ties):
            ties.append(("shift", (moved,) * subs))
    return ties


def on_core(tie, core):
    kind, steps = tie
    if len(set(steps)) == 1:
        return kind, steps[0]
    return kind, jnp.where(core % 2 == 0, steps[0], steps[1])


def partner(block, blocks, tie, back=False):
    kind, step = tie
    if kind == "xor":
        return block ^ step
    return (block + (step if back else -step) + blocks) % blocks


def offsets_of(block, blocks, tie, back):
    kind, step = tie
    if kind == "shift":
        return [e for e in range(OFFS) if (e - REACH - step) % blocks == 0]
    if isinstance(step, int) and step % 2 == 0:
        return [e for e in range(OFFS) if abs(e - REACH) == step]
    ahead = (block ^ step) - block if back else block - (block ^ step)
    return [jnp.where((ahead + blocks) % blocks == 1, REACH + 1, REACH - 1)]


def exchange(value, blocks, subs, tie, back=False):
    kind, steps = tie
    route = [
        (partner(b, blocks, (kind, steps[c]), back) * subs + c, b * subs + c)
        for b in range(blocks)
        for c in range(subs)
    ]
    return lax.ppermute(value, ("chan", "sub"), route)


def chunks_of(channels):
    if channels < 2 * LANES or channels % LANES:
        return [(0, channels)]
    first = channels * 2 // 5 // LANES * LANES
    return [(0, first), (first, channels - first)]


def shift(block, axis, distance):
    count = lax.axis_size(axis)
    return lax.ppermute(block, axis, [(i, (i + distance) % count) for i in range(count)])


def slots_of(ties, blocks):
    return sum(len(offsets_of(0, blocks, (kind, steps[0]), False)) for kind, steps in ties)


def in_hbm(value):
    return pltpu.with_memory_space_constraint(value, pltpu.HBM)


def after(value, *others):
    return lax.optimization_barrier((value, *others))[0]


def on_device(traces, channel_mask, smooth_width, source_phase, pair_list):
    _, channels, samples = traces.shape
    blocks, windows, subs = (lax.axis_size(a) for a in ("chan", "win", "sub"))
    sub_at = lax.axis_index("sub")
    per_device = VS // (windows * subs)
    group = per_device * STRIDE
    ties = ties_of(blocks, subs)
    span = 2 * side_rows(per_device)
    chunks = chunks_of(channels)
    table, lags = dft_table(samples), lag_table(samples, per_device)
    factor = (NB * windows) ** (-0.5)
    bf16, f32 = jnp.bfloat16, jnp.float32
    like = jax.ShapeDtypeStruct
    mask_row = channel_mask.reshape(1, channels)

    def half_of(rows, start, size):
        grouped = rows.reshape(channels // (subs * group), subs, group, samples)
        first, count = start // (subs * group), size // (subs * group)
        half = lax.dynamic_slice(grouped, (first, sub_at, 0, 0), (count, 1, group, samples))
        return half.reshape(size // subs, samples)

    def from_windows(half):
        return [shift(half, "win", d) for d in range(1, windows)]

    def with_other_core(received):
        return [side for piece in received for side in (piece, shift(piece, "sub", 1))]

    def whiten_others(size, both, hint):
        return pl.pallas_call(
            others_kernel,
            out_shape=like((windows - 1, size, 2 * NB), bf16),
            in_specs=[VMEM] * (3 + len(both)),
            out_specs=VMEM,
            scratch_shapes=[pltpu.VMEM((size // (subs * group), subs, group, samples), bf16)],
            compiler_params=params(24),
            cost_estimate=hint,
            name="whiten_others",
        )(table, weights, share, *both)

    def correlate(start, size, turned, base, white):
        count = turned.shape[1] // span
        return pl.pallas_call(
            functools.partial(lag_kernel, factor, True),
            out_shape=tuple(like((span, size), bf16) for _ in range(count)),
            in_specs=[VMEM] * 4,
            out_specs=(VMEM,) * count,
            compiler_params=params(24),
            cost_estimate=LONG,
            name="lag_pieces",
        )(turned, base, white, mask_row[:, start:start + size])

    half = half_of(traces, *chunks[0])
    received = [from_windows(half)]
    *owns, weights, share, rows, table = pl.pallas_call(
        functools.partial(setup_kernel, chunks),
        out_shape=tuple(like((size, 2 * NB), bf16) for _, size in chunks)
        + (like((NB, NB), bf16), like((1, NB), f32))
        + (like((channels, samples), bf16), like(table.shape, bf16)),
        in_specs=[HBM, HBM, HBM],
        out_specs=(VMEM,) * (len(chunks) + 4),
        scratch_shapes=[pltpu.SemaphoreType.DMA((TABLE_PARTS + 3,)), pltpu.VMEM((1, NB), jnp.int32)],
        compiler_params=params(24),
        cost_estimate=SHORT,
        name="whiten_own",
    )(in_hbm(traces), in_hbm(table), in_hbm(after(smooth_width, half).reshape(1, NB)))
    received += [from_windows(after(rows, share)[a:a + n]) for a, n in chunks[1:]]
    near = pl.pallas_call(
        functools.partial(near_kernel, (windows, subs, per_device)),
        out_shape=like((windows * per_device, samples), f32),
        in_specs=[SMEM] + [VMEM] * (1 + windows),
        out_specs=VMEM,
        compiler_params=params(16),
        cost_estimate=SHORT,
        name="pick_sources",
    )(source_phase, after(mask_row, weights), half, *received[0])

    def turn(sources, places, hint, *first):
        rows_each = windows * per_device
        return pl.pallas_call(
            functools.partial(turn_kernel, (per_device, windows, places)),
            out_shape=like((windows, len(places) * span, 2 * NB), bf16),
            in_specs=[VMEM] * (4 + len(sources)),
            out_specs=VMEM,
            scratch_shapes=[pltpu.VMEM((len(places) * rows_each, 2 * NB), f32)],
            compiler_params=params(24),
            cost_estimate=hint,
            name="turn_sources",
        )(table, weights, after(share, *first), lags, *sources)

    turned_own = turn([near], [(0,)], LONG)
    inbound = with_other_core(received[0])
    white = whiten_others(chunks[0][1], inbound, SHORT)
    if ties[1][0] == "xor":
        beside = exchange(near, blocks, subs, ("xor", (1,) * subs))
        two = jnp.concatenate([after(near, turned_own), beside], axis=0).astype(bf16)
        sources = [beside, exchange(two, blocks, subs, ("xor", (2,) * subs))]
        places = [tuple(step - 1 for step in steps) for _, steps in ties[1:]]
    else:
        sources = [exchange(near, blocks, subs, tie) for tie in ties[1:]]
        places = [(at,) for at in range(len(sources))]
    start, size = chunks[0]
    count = len(places)
    turned, *first_pieces = pl.pallas_call(
        functools.partial(first_kernel, (per_device, windows, places), factor, len(sources)),
        out_shape=(like((windows, count * span, 2 * NB), bf16),) + (like((span, size), bf16),) * count,
        in_specs=[VMEM] * (7 + len(sources)),
        out_specs=(VMEM,) * (1 + count),
        scratch_shapes=[pltpu.VMEM((count * windows * per_device, 2 * NB), f32)],
        compiler_params=params(24),
        cost_estimate=SHORT,
        name="turn_and_lag",
    )(table, weights, share, lags, owns[0], white, mask_row[:, start:start + size], *sources)
    pieces, arrived, whites = [], [], [white]
    for i, (start, size) in enumerate(chunks):
        if i:
            whites.append(whiten_others(size, [after(r, *pieces[-1]) for r in received[i]], LONG))
            base = pl.pallas_call(
                base_kernel,
                out_shape=like((turned.shape[1], size), f32),
                in_specs=[VMEM, VMEM],
                out_specs=VMEM,
                compiler_params=params(24),
                cost_estimate=SHORT,
                name="lag_base",
            )(after(turned, *pieces[-1]), owns[i])
            pieces.append(correlate(start, size, turned, base, whites[i]))
        else:
            pieces.append(tuple(first_pieces))
        ahead = arrived[-1][:1] if i else []
        sent = [after(p, *ahead) for p in pieces[-1]]
        arrived.append([exchange(p, blocks, subs, tie, True) for tie, p in zip(ties[1:], sent)])
    stack = like((OFFS, LAGS, per_device, channels), f32)

    def scratch(count, slots, width):
        return [
            pltpu.VMEM((count, span, width), f32),
            pltpu.VMEM((slots, LAGS, per_device, width), f32),
            pltpu.SemaphoreType.DMA((slots,)),
        ]

    remote = [piece for group in pieces for piece in group]
    receiver_stack, source_stack = pl.pallas_call(
        functools.partial(receiver_kernel, (ties, blocks, per_device, chunks, factor)),
        out_shape=(stack, stack),
        in_specs=[VMEM] * (3 + 2 * len(chunks) + len(remote)),
        out_specs=(HBM, HBM),
        scratch_shapes=scratch(len(ties), slots_of(ties, blocks) + 1, channels),
        compiler_params=params(24),
        cost_estimate=LONG,
        name="receiver_order",
    )(pair_list, turned_own, mask_row, *owns, *whites, *remote)
    slots = slots_of(ties[1:], blocks)
    for (start, size), back in zip(chunks, arrived):
        source_stack = pl.pallas_call(
            functools.partial(source_kernel, (ties[1:], blocks, per_device, start)),
            out_shape=stack,
            in_specs=[VMEM] * (1 + count) + [HBM],
            out_specs=HBM,
            scratch_shapes=scratch(count, slots, size),
            input_output_aliases={1 + count: 0},
            compiler_params=params(16),
            cost_estimate=SHORT,
            name="source_order",
        )(pair_list, *back, source_stack)
    order = (2, 0, 1, 3)
    return (jnp.transpose(receiver_stack, order), jnp.transpose(source_stack, order))


def solution(mesh):
    in_specs = (
        P(("groups", "win"), "chan", None),
        P(("groups", "chan")),
        P(),
        P("groups"),
        P("groups", None),
    )
    out_specs = (
        P(("win", "sub"), None, None, ("groups", "chan")),
        P(("groups", "chan", "win", "sub"), None, None, None),
    )
    return jax.shard_map(
        on_device, mesh=mesh, in_specs=in_specs, out_specs=out_specs, check_vma=False
    )
```

```python
import functools
import math

import jax
import jax.numpy as jnp
import numpy as np
from jax import lax
from jax.experimental import pallas as pl
from jax.experimental.pallas import tpu as pltpu
from jax.sharding import PartitionSpec as P

NB = 512
MAXLAG = 50
STRIDE = 8
REACH = 2
VS = 8
OFFS = 5
LAGS = 2 * MAXLAG + 1
FLOOR = 0.25
TABLE_PARTS = 4
LANES = 128
VMEM = pl.BlockSpec(memory_space=pltpu.VMEM)
SMEM = pl.BlockSpec(memory_space=pltpu.SMEM)
HBM = pl.BlockSpec(memory_space=pltpu.HBM)
NT = (((1,), (1,)), ((), ()))


def dft_table(samples):
    phases = np.arange(samples)[:, None] * np.arange(NB)[None, :] % samples
    angles = phases * (2.0 * math.pi / samples)
    table = np.concatenate([np.cos(angles), -np.sin(angles)], axis=1)
    return jnp.asarray(table.astype(np.float32), jnp.bfloat16)


def side_rows(per_device):
    return -(-(MAXLAG + 1) * per_device // 8) * 8


def lag_row(tau, per_device):
    return abs(tau) * per_device + (0 if tau >= 0 else side_rows(per_device))


def lag_table(samples, per_device):
    lag = np.arange(side_rows(per_device)) // per_device
    angles = (lag[:, None] * np.arange(NB)[None, :] % samples) * (2.0 * math.pi / samples)
    table = np.concatenate([np.cos(angles), np.sin(angles)], axis=1)
    return jnp.asarray(table, jnp.float32)


def params(mib):
    return pltpu.CompilerParams(vmem_limit_bytes=mib << 20)


def cost(flops, moved):
    return pl.CostEstimate(flops=flops, bytes_accessed=moved, transcendentals=0)


SHORT, LONG = cost(1 << 20, 1 << 18), cost(1 << 33, 1 << 26)


def whiten(rows, table, weights, share):
    samples = rows.shape[1]
    spectrum = jnp.dot(rows, table, preferred_element_type=jnp.float32) * samples ** (-0.5)
    real, imag = spectrum[:, :NB], spectrum[:, NB:]
    amplitude = jnp.sqrt(real * real + imag * imag)
    high = amplitude.astype(jnp.bfloat16)
    low = (amplitude - high.astype(jnp.float32)).astype(jnp.bfloat16)
    total = jnp.dot(high, weights, preferred_element_type=jnp.float32)
    total += jnp.dot(low, weights, preferred_element_type=jnp.float32)
    gain = 1.0 / jnp.maximum(total * share, FLOOR)
    return (real * gain).astype(jnp.bfloat16), (imag * gain).astype(jnp.bfloat16)


def near_kernel(layout, phases, mask, *refs):
    windows, subs, per_device = layout
    halves, out = refs[:-1], refs[-1]
    block_at, win_at, sub_at = lax.axis_index("chan"), lax.axis_index("win"), lax.axis_index("sub")
    group = per_device * STRIDE
    rows, width = out.shape[0], halves[0].shape[0]
    phase = phases[block_at]

    def ones_at(first, width):
        row = lax.broadcasted_iota(jnp.int32, (rows, width), 0)
        place = lax.broadcasted_iota(jnp.int32, (rows, width), 1)
        return row, place == first + phase + STRIDE * (row % per_device)

    row, here = ones_at((win_at * subs + sub_at) * group, mask.shape[1])
    alive = jnp.sum(jnp.where(here, mask[...].astype(jnp.float32), 0.0), axis=1, keepdims=True)
    row, here = ones_at(win_at * group, width)
    total = jnp.zeros(out.shape, jnp.float32)
    for behind in range(windows):
        chosen = jnp.where(here & (row // per_device == behind), 1.0, 0.0).astype(jnp.bfloat16)
        total += jnp.dot(chosen, halves[behind][...], preferred_element_type=jnp.float32)
    out[...] = total * alive


def setup_kernel(chunks, traces, table, widths, *refs):
    owns, (weights, share, rows_kept, table_kept, sems, *scratch) = refs[:len(chunks)], refs[len(chunks):]
    depth = table.shape[0] // TABLE_PARTS
    needed = chunks[-1][0] + chunks[-1][1]
    rest = rows_kept.shape[0] - needed
    first_rows = pltpu.make_async_copy(traces.at[0, pl.ds(0, needed)], rows_kept.at[pl.ds(0, needed)], sems.at[TABLE_PARTS])
    first_rows.start()
    parts = []
    for i in range(TABLE_PARTS):
        span = pl.ds(i * depth, depth)
        parts.append(pltpu.make_async_copy(table.at[span], table_kept.at[span], sems.at[i]))
        parts[-1].start()
    if rest:
        span = pl.ds(needed, rest)
        last_rows = pltpu.make_async_copy(traces.at[0, span], rows_kept.at[span], sems.at[TABLE_PARTS + 1])
        last_rows.start()
    widths_kept, = scratch
    fetched = pltpu.make_async_copy(widths, widths_kept, sems.at[TABLE_PARTS + 2])
    fetched.start()
    fetched.wait()
    reach = widths_kept[...]
    near = lax.broadcasted_iota(jnp.int32, (NB, NB), 0)
    here = lax.broadcasted_iota(jnp.int32, (NB, NB), 1)
    weights[...] = jnp.where(jnp.abs(near - here) <= reach, 1.0, 0.0).astype(jnp.bfloat16)
    bins = lax.broadcasted_iota(jnp.int32, (1, NB), 1)
    count = jnp.minimum(bins + reach, NB - 1) - jnp.maximum(bins - reach, 0) + 1
    share[...] = 1.0 / count.astype(jnp.float32)
    first_rows.wait()
    for part in parts:
        part.wait()
    for (start, size), own in zip(chunks, owns):
        own_kernel(start, rows_kept, table_kept, weights, share, own)
    if rest:
        last_rows.wait()


def own_kernel(start, rows, table, weights, share, out):
    real, imag = whiten(rows[start:start + out.shape[0], :], table[...], weights[...], share[...])
    out[:, :NB] = real
    out[:, NB:] = imag


def turn_kernel(layout, table, weights, share, lags, *refs):
    per_device, windows, places = layout
    even = lax.axis_index("sub") % 2 == 0
    picked, turned, spectra = refs[:-2], refs[-2], refs[-1]
    rows = jnp.concatenate([p[...].astype(jnp.float32) for p in picked], axis=0).astype(jnp.bfloat16)
    real, imag = whiten(rows, table[...], weights[...], share[...])
    spectra[:, :NB] = real.astype(jnp.float32)
    spectra[:, NB:] = imag.astype(jnp.float32)
    side = side_rows(per_device)
    span = 2 * side
    which = lax.broadcasted_iota(jnp.int32, (8, LANES), 0) % per_device

    def rows_of(first, lane):
        tiled = jnp.zeros((8, LANES), jnp.float32)
        for v in range(per_device):
            rows = [spectra[f + v:f + v + 1, lane:lane + LANES] for f in first]
            row = rows[0] if first[0] == first[-1] else jnp.where(even, rows[0], rows[-1])
            tiled = jnp.where(which == v, row, tiled)
        return tiled[None]

    for lane in range(0, NB, LANES):
        cosine = lags[:, lane:lane + LANES].reshape(side // 8, 8, LANES)
        sine = lags[:, NB + lane:NB + lane + LANES].reshape(side // 8, 8, LANES)
        for at, place in enumerate(places):
            for behind in range(windows):
                first = [(here * windows + behind) * per_device for here in place]
                real, imag = rows_of(first, lane), rows_of(first, NB + lane)
                cr, si, sr, ci = cosine * real, sine * imag, sine * real, cosine * imag
                up = jnp.concatenate([cr - si, cr + si], axis=0).reshape(span, LANES)
                down = jnp.concatenate([ci + sr, ci - sr], axis=0).reshape(span, LANES)
                spot = pl.ds(at * span, span)
                turned[behind, spot, lane:lane + LANES] = up.astype(jnp.bfloat16)
                turned[behind, spot, NB + lane:NB + lane + LANES] = down.astype(jnp.bfloat16)


def others_kernel(table, weights, share, *refs):
    parts, (white, raw) = refs[:-2], refs[-2:]
    sub_at = lax.axis_index("sub")
    groups, _, group, samples = raw.shape
    each = len(parts) // white.shape[0]
    for i in range(white.shape[0]):
        if each == 1:
            rows = parts[i][...]
        else:
            for half, place in ((parts[2 * i], sub_at), (parts[2 * i + 1], 1 - sub_at)):
                raw[:, pl.ds(place, 1)] = half[...].reshape(groups, 1, group, samples)
            rows = raw[...].reshape(white.shape[1], samples)
        real, imag = whiten(rows, table[...], weights[...], share[...])
        white[i, :, :NB] = real
        white[i, :, NB:] = imag


def lag_product(turned, own, white):
    total = lax.dot_general(turned[0], own[...], NT, preferred_element_type=jnp.float32)
    for i in range(white.shape[0]):
        total += lax.dot_general(turned[1 + i], white[i], NT, preferred_element_type=jnp.float32)
    return total


def base_kernel(turned, own, base):
    base[...] = lax.dot_general(turned[0], own[...], NT, preferred_element_type=jnp.float32)


def lag_kernel(factor, based, turned, own, white, mask, *pieces):
    if based:
        total = own[...]
        for i in range(white.shape[0]):
            total += lax.dot_general(turned[1 + i], white[i], NT, preferred_element_type=jnp.float32)
    else:
        total = lag_product(turned, own, white)
    result = total * (mask[...].astype(jnp.float32) * factor)
    span = result.shape[0] // len(pieces)
    for at, piece in enumerate(pieces):
        piece[...] = result[at * span:(at + 1) * span, :].astype(jnp.bfloat16)


def first_kernel(layout, factor, count, table, weights, share, lags, own, white, mask, *refs):
    sources, (turned, *pieces, spectra) = refs[:count], refs[count:]
    turn_kernel(layout, table, weights, share, lags, *sources, turned, spectra)
    lag_kernel(factor, False, turned, own, white, mask, *pieces)


def later_kernel(factor, count, table, weights, share, turned, base, mask, *refs):
    parts, (white, *pieces, raw) = refs[:count], refs[count:]
    others_kernel(table, weights, share, *parts, white, raw)
    lag_kernel(factor, True, turned, base, white, mask, *pieces)


def put_slots(layout, listed, wide, out, stage, sems, slot):
    tie, blocks, per_device, first, reverse = layout
    block_at, tie = lax.axis_index("chan"), on_core(tie, lax.axis_index("sub"))
    row = lax.broadcasted_iota(jnp.int32, listed.shape, 0)
    column = lax.broadcasted_iota(jnp.int32, listed.shape, 1)
    width = stage.shape[3]
    block = block_at if reverse else partner(block_at, blocks, tie)
    copies = []
    for e in offsets_of(block_at, blocks, tie, reverse):
        chosen = jnp.where((row == block) & (column == e), listed, 0.0)
        pair = jnp.broadcast_to(jnp.sum(chosen, keepdims=True), (per_device, width))
        for t in range(LAGS):
            tau = MAXLAG - t if reverse else t - MAXLAG
            spot = lag_row(tau, per_device)
            stage[slot, t] = wide[spot:spot + per_device, :] * pair
        target = out.at[e, :, :, pl.ds(first, width)]
        copies.append(pltpu.make_async_copy(stage.at[slot], target, sems.at[slot]))
        copies[-1].start()
        slot += 1
    return copies


def receiver_kernel(layout, pairs, turned, mask, *refs):
    ties, blocks, per_device, chunks, factor = layout
    count = len(chunks)
    owns, whites, pieces = refs[:count], refs[count:2 * count], refs[2 * count:-5]
    out, source_out, wide, stage, sems = refs[-5:]
    listed = pairs[...].astype(jnp.float32)
    copies = []
    for at, tie in enumerate(ties):
        for i, (start, size) in enumerate(chunks):
            lanes = slice(start, start + size)
            if at:
                wide[at, :, lanes] = pieces[i * (len(ties) - 1) + at - 1][...].astype(jnp.float32)
            else:
                wide[at, :, lanes] = lag_product(turned, owns[i], whites[i]) * (mask[:, lanes].astype(jnp.float32) * factor)
        turns = [(out, False)] + ([] if at else [(source_out, True)])
        for target, reverse in turns:
            part = (tie, blocks, per_device, 0, reverse)
            copies += put_slots(part, listed, wide.at[at], target, stage, sems, len(copies))
    for copy in copies:
        copy.wait()


def source_kernel(layout, pairs, *refs):
    ties, blocks, per_device, first = layout
    pieces, (_, out, wide, stage, sems) = refs[:len(ties)], refs[len(ties):]
    listed = pairs[...].astype(jnp.float32)
    copies = []
    for at, tie in enumerate(ties):
        wide[at] = pieces[at][...].astype(jnp.float32)
        part = (tie, blocks, per_device, first, True)
        copies += put_slots(part, listed, wide.at[at], out, stage, sems, len(copies))
    for copy in copies:
        copy.wait()


def ties_of(blocks, subs):
    if blocks == 4:
        return [("xor", (step,) * subs) for step in (0, 1, 3, 2)]
    ties = []
    for moved in (0, 1, -1, 2, -2):
        if all((m[0] - moved) % blocks for _, m in ties):
            ties.append(("shift", (moved,) * subs))
    return ties


def on_core(tie, core):
    kind, steps = tie
    if len(set(steps)) == 1:
        return kind, steps[0]
    return kind, jnp.where(core % 2 == 0, steps[0], steps[1])


def partner(block, blocks, tie, back=False):
    kind, step = tie
    if kind == "xor":
        return block ^ step
    return (block + (step if back else -step) + blocks) % blocks


def offsets_of(block, blocks, tie, back):
    kind, step = tie
    if kind == "shift":
        return [e for e in range(OFFS) if (e - REACH - step) % blocks == 0]
    if isinstance(step, int) and step % 2 == 0:
        return [e for e in range(OFFS) if abs(e - REACH) == step]
    ahead = (block ^ step) - block if back else block - (block ^ step)
    return [jnp.where((ahead + blocks) % blocks == 1, REACH + 1, REACH - 1)]


def exchange(value, blocks, subs, tie, back=False):
    kind, steps = tie
    route = [
        (partner(b, blocks, (kind, steps[c]), back) * subs + c, b * subs + c)
        for b in range(blocks)
        for c in range(subs)
    ]
    return lax.ppermute(value, ("chan", "sub"), route)


def chunks_of(channels):
    if channels < 2 * LANES or channels % LANES:
        return [(0, channels)]
    first = channels * 2 // 5 // LANES * LANES
    return [(0, first), (first, channels - first)]


def shift(block, axis, distance):
    count = lax.axis_size(axis)
    return lax.ppermute(block, axis, [(i, (i + distance) % count) for i in range(count)])


def slots_of(ties, blocks):
    return sum(len(offsets_of(0, blocks, (kind, steps[0]), False)) for kind, steps in ties)


def in_hbm(value):
    return pltpu.with_memory_space_constraint(value, pltpu.HBM)


def after(value, *others):
    return lax.optimization_barrier((value, *others))[0]


def on_device(traces, channel_mask, smooth_width, source_phase, pair_list):
    _, channels, samples = traces.shape
    blocks, windows, subs = (lax.axis_size(a) for a in ("chan", "win", "sub"))
    sub_at = lax.axis_index("sub")
    per_device = VS // (windows * subs)
    group = per_device * STRIDE
    ties = ties_of(blocks, subs)
    span = 2 * side_rows(per_device)
    chunks = chunks_of(channels)
    table, lags = dft_table(samples), lag_table(samples, per_device)
    factor = (NB * windows) ** (-0.5)
    bf16, f32 = jnp.bfloat16, jnp.float32
    like = jax.ShapeDtypeStruct
    mask_row = channel_mask.reshape(1, channels)

    def half_of(rows, start, size):
        grouped = rows.reshape(channels // (subs * group), subs, group, samples)
        first, count = start // (subs * group), size // (subs * group)
        half = lax.dynamic_slice(grouped, (first, sub_at, 0, 0), (count, 1, group, samples))
        return half.reshape(size // subs, samples)

    def from_windows(half):
        return [shift(half, "win", d) for d in range(1, windows)]

    def with_other_core(received):
        return [side for piece in received for side in (piece, shift(piece, "sub", 1))]

    def whiten_others(size, both, hint):
        return pl.pallas_call(
            others_kernel,
            out_shape=like((windows - 1, size, 2 * NB), bf16),
            in_specs=[VMEM] * (3 + len(both)),
            out_specs=VMEM,
            scratch_shapes=[pltpu.VMEM((size // (subs * group), subs, group, samples), bf16)],
            compiler_params=params(24),
            cost_estimate=hint,
            name="whiten_others",
        )(table, weights, share, *both)

    def correlate(start, size, turned, base, parts):
        count = turned.shape[1] // span
        white, *made = pl.pallas_call(
            functools.partial(later_kernel, factor, len(parts)),
            out_shape=(like((windows - 1, size, 2 * NB), bf16),) + (like((span, size), bf16),) * count,
            in_specs=[VMEM] * (6 + len(parts)),
            out_specs=(VMEM,) * (1 + count),
            scratch_shapes=[pltpu.VMEM((size // (subs * group), subs, group, samples), bf16)],
            compiler_params=params(24),
            cost_estimate=LONG,
            name="whiten_and_lag",
        )(table, weights, share, turned, base, mask_row[:, start:start + size], *parts)
        return white, tuple(made)

    half = half_of(traces, *chunks[0])
    received = [from_windows(half)]
    *owns, weights, share, rows, table = pl.pallas_call(
        functools.partial(setup_kernel, chunks),
        out_shape=tuple(like((size, 2 * NB), bf16) for _, size in chunks)
        + (like((NB, NB), bf16), like((1, NB), f32))
        + (like((channels, samples), bf16), like(table.shape, bf16)),
        in_specs=[HBM, HBM, HBM],
        out_specs=(VMEM,) * (len(chunks) + 4),
        scratch_shapes=[pltpu.SemaphoreType.DMA((TABLE_PARTS + 3,)), pltpu.VMEM((1, NB), jnp.int32)],
        compiler_params=params(24),
        cost_estimate=SHORT,
        name="whiten_own",
    )(in_hbm(traces), in_hbm(table), in_hbm(after(smooth_width, half).reshape(1, NB)))
    received += [from_windows(after(rows, share)[a:a + n]) for a, n in chunks[1:]]
    near = pl.pallas_call(
        functools.partial(near_kernel, (windows, subs, per_device)),
        out_shape=like((windows * per_device, samples), f32),
        in_specs=[SMEM] + [VMEM] * (1 + windows),
        out_specs=VMEM,
        compiler_params=params(16),
        cost_estimate=SHORT,
        name="pick_sources",
    )(source_phase, after(mask_row, weights), half, *received[0])

    def turn(sources, places, hint, *first):
        rows_each = windows * per_device
        return pl.pallas_call(
            functools.partial(turn_kernel, (per_device, windows, places)),
            out_shape=like((windows, len(places) * span, 2 * NB), bf16),
            in_specs=[VMEM] * (4 + len(sources)),
            out_specs=VMEM,
            scratch_shapes=[pltpu.VMEM((len(places) * rows_each, 2 * NB), f32)],
            compiler_params=params(24),
            cost_estimate=hint,
            name="turn_sources",
        )(table, weights, after(share, *first), lags, *sources)

    turned_own = turn([near], [(0,)], LONG)
    inbound = with_other_core(received[0])
    white = whiten_others(chunks[0][1], inbound, SHORT)
    if ties[1][0] == "xor":
        beside = exchange(near, blocks, subs, ("xor", (1,) * subs))
        two = jnp.concatenate([after(near, turned_own), beside], axis=0).astype(bf16)
        sources = [beside, exchange(two, blocks, subs, ("xor", (2,) * subs))]
        places = [tuple(step - 1 for step in steps) for _, steps in ties[1:]]
    else:
        sources = [exchange(near, blocks, subs, tie) for tie in ties[1:]]
        places = [(at,) for at in range(len(sources))]
    start, size = chunks[0]
    count = len(places)
    turned, *first_pieces = pl.pallas_call(
        functools.partial(first_kernel, (per_device, windows, places), factor, len(sources)),
        out_shape=(like((windows, count * span, 2 * NB), bf16),) + (like((span, size), bf16),) * count,
        in_specs=[VMEM] * (7 + len(sources)),
        out_specs=(VMEM,) * (1 + count),
        scratch_shapes=[pltpu.VMEM((count * windows * per_device, 2 * NB), f32)],
        compiler_params=params(24),
        cost_estimate=SHORT,
        name="turn_and_lag",
    )(table, weights, share, lags, owns[0], white, mask_row[:, start:start + size], *sources)
    pieces, arrived, whites = [], [], [white]
    for i, (start, size) in enumerate(chunks):
        if i:
            base = pl.pallas_call(
                base_kernel,
                out_shape=like((turned.shape[1], size), f32),
                in_specs=[VMEM, VMEM],
                out_specs=VMEM,
                compiler_params=params(24),
                cost_estimate=SHORT,
                name="lag_base",
            )(after(turned, *pieces[-1]), owns[i])
            parts = [after(r, *pieces[-1]) for r in received[i]]
            white, made = correlate(start, size, turned, base, parts)
            whites.append(white)
            pieces.append(made)
        else:
            pieces.append(tuple(first_pieces))
        ahead = arrived[-1][-1:] if i else []
        sent = [after(p, *ahead) for p in pieces[-1]]
        arrived.append([exchange(p, blocks, subs, tie, True) for tie, p in zip(ties[1:], sent)])
    stack = like((OFFS, LAGS, per_device, channels), f32)

    def scratch(count, slots, width):
        return [
            pltpu.VMEM((count, span, width), f32),
            pltpu.VMEM((slots, LAGS, per_device, width), f32),
            pltpu.SemaphoreType.DMA((slots,)),
        ]

    remote = [piece for group in pieces for piece in group]
    receiver_stack, source_stack = pl.pallas_call(
        functools.partial(receiver_kernel, (ties, blocks, per_device, chunks, factor)),
        out_shape=(stack, stack),
        in_specs=[VMEM] * (3 + 2 * len(chunks) + len(remote)),
        out_specs=(HBM, HBM),
        scratch_shapes=scratch(len(ties), slots_of(ties, blocks) + 1, channels),
        compiler_params=params(24),
        cost_estimate=LONG,
        name="receiver_order",
    )(pair_list, turned_own, mask_row, *owns, *whites, *remote)
    slots = slots_of(ties[1:], blocks)
    for (start, size), back in zip(chunks, arrived):
        source_stack = pl.pallas_call(
            functools.partial(source_kernel, (ties[1:], blocks, per_device, start)),
            out_shape=stack,
            in_specs=[VMEM] * (1 + count) + [HBM],
            out_specs=HBM,
            scratch_shapes=scratch(count, slots, size),
            input_output_aliases={1 + count: 0},
            compiler_params=params(16),
            cost_estimate=SHORT,
            name="source_order",
        )(pair_list, *back, source_stack)
    order = (2, 0, 1, 3)
    return (jnp.transpose(receiver_stack, order), jnp.transpose(source_stack, order))


def solution(mesh):
    in_specs = (
        P(("groups", "win"), "chan", None),
        P(("groups", "chan")),
        P(),
        P("groups"),
        P("groups", None),
    )
    out_specs = (
        P(("win", "sub"), None, None, ("groups", "chan")),
        P(("groups", "chan", "win", "sub"), None, None, None),
    )
    return jax.shard_map(
        on_device, mesh=mesh, in_specs=in_specs, out_specs=out_specs, check_vma=False
    )
```

```python
import functools
import math

import jax
import jax.numpy as jnp
import numpy as np
from jax import lax
from jax.experimental import pallas as pl
from jax.experimental.pallas import tpu as pltpu
from jax.sharding import PartitionSpec as P

NB = 512
MAXLAG = 50
STRIDE = 8
REACH = 2
VS = 8
OFFS = 5
LAGS = 2 * MAXLAG + 1
FLOOR = 0.25
TABLE_PARTS = 4
LANES = 128
VMEM = pl.BlockSpec(memory_space=pltpu.VMEM)
SMEM = pl.BlockSpec(memory_space=pltpu.SMEM)
HBM = pl.BlockSpec(memory_space=pltpu.HBM)
NT = (((1,), (1,)), ((), ()))


def dft_table(samples):
    phases = np.arange(samples)[:, None] * np.arange(NB)[None, :] % samples
    angles = phases * (2.0 * math.pi / samples)
    table = np.concatenate([np.cos(angles), -np.sin(angles)], axis=1)
    return jnp.asarray(table.astype(np.float32), jnp.bfloat16)


def side_rows(per_device):
    return -(-(MAXLAG + 1) * per_device // 8) * 8


def lag_row(tau, per_device):
    return abs(tau) * per_device + (0 if tau >= 0 else side_rows(per_device))


def lag_table(samples, per_device):
    lag = np.arange(side_rows(per_device)) // per_device
    angles = (lag[:, None] * np.arange(NB)[None, :] % samples) * (2.0 * math.pi / samples)
    table = np.concatenate([np.cos(angles), np.sin(angles)], axis=1)
    return jnp.asarray(table, jnp.float32)


def params(mib):
    return pltpu.CompilerParams(vmem_limit_bytes=mib << 20)


def cost(flops, moved):
    return pl.CostEstimate(flops=flops, bytes_accessed=moved, transcendentals=0)


SHORT, LONG = cost(1 << 20, 1 << 18), cost(1 << 33, 1 << 26)


def whiten(rows, table, weights, share):
    samples = rows.shape[1]
    spectrum = jnp.dot(rows, table, preferred_element_type=jnp.float32) * samples ** (-0.5)
    real, imag = spectrum[:, :NB], spectrum[:, NB:]
    amplitude = jnp.sqrt(real * real + imag * imag)
    high = amplitude.astype(jnp.bfloat16)
    low = (amplitude - high.astype(jnp.float32)).astype(jnp.bfloat16)
    total = jnp.dot(high, weights, preferred_element_type=jnp.float32)
    total += jnp.dot(low, weights, preferred_element_type=jnp.float32)
    gain = 1.0 / jnp.maximum(total * share, FLOOR)
    return (real * gain).astype(jnp.bfloat16), (imag * gain).astype(jnp.bfloat16)


def near_kernel(layout, phases, mask, *refs):
    windows, subs, per_device = layout
    halves, out = refs[:-1], refs[-1]
    block_at, win_at, sub_at = lax.axis_index("chan"), lax.axis_index("win"), lax.axis_index("sub")
    group = per_device * STRIDE
    rows, width = out.shape[0], halves[0].shape[0]
    phase = phases[block_at]

    def ones_at(first, width):
        row = lax.broadcasted_iota(jnp.int32, (rows, width), 0)
        place = lax.broadcasted_iota(jnp.int32, (rows, width), 1)
        return row, place == first + phase + STRIDE * (row % per_device)

    row, here = ones_at((win_at * subs + sub_at) * group, mask.shape[1])
    alive = jnp.sum(jnp.where(here, mask[...].astype(jnp.float32), 0.0), axis=1, keepdims=True)
    row, here = ones_at(win_at * group, width)
    total = jnp.zeros(out.shape, jnp.float32)
    for behind in range(windows):
        chosen = jnp.where(here & (row // per_device == behind), 1.0, 0.0).astype(jnp.bfloat16)
        total += jnp.dot(chosen, halves[behind][...], preferred_element_type=jnp.float32)
    out[...] = total * alive


def setup_kernel(chunks, traces, table, widths, *refs):
    owns, (weights, share, rows_kept, table_kept, sems, *scratch) = refs[:len(chunks)], refs[len(chunks):]
    depth = table.shape[0] // TABLE_PARTS
    needed = chunks[-1][0] + chunks[-1][1]
    rest = rows_kept.shape[0] - needed
    first_rows = pltpu.make_async_copy(traces.at[0, pl.ds(0, needed)], rows_kept.at[pl.ds(0, needed)], sems.at[TABLE_PARTS])
    first_rows.start()
    parts = []
    for i in range(TABLE_PARTS):
        span = pl.ds(i * depth, depth)
        parts.append(pltpu.make_async_copy(table.at[span], table_kept.at[span], sems.at[i]))
        parts[-1].start()
    if rest:
        span = pl.ds(needed, rest)
        last_rows = pltpu.make_async_copy(traces.at[0, span], rows_kept.at[span], sems.at[TABLE_PARTS + 1])
        last_rows.start()
    widths_kept, = scratch
    fetched = pltpu.make_async_copy(widths, widths_kept, sems.at[TABLE_PARTS + 2])
    fetched.start()
    fetched.wait()
    reach = widths_kept[...]
    near = lax.broadcasted_iota(jnp.int32, (NB, NB), 0)
    here = lax.broadcasted_iota(jnp.int32, (NB, NB), 1)
    weights[...] = jnp.where(jnp.abs(near - here) <= reach, 1.0, 0.0).astype(jnp.bfloat16)
    bins = lax.broadcasted_iota(jnp.int32, (1, NB), 1)
    count = jnp.minimum(bins + reach, NB - 1) - jnp.maximum(bins - reach, 0) + 1
    share[...] = 1.0 / count.astype(jnp.float32)
    first_rows.wait()
    for part in parts:
        part.wait()
    for (start, size), own in zip(chunks, owns):
        own_kernel(start, rows_kept, table_kept, weights, share, own)
    if rest:
        last_rows.wait()


def own_kernel(start, rows, table, weights, share, out):
    real, imag = whiten(rows[start:start + out.shape[0], :], table[...], weights[...], share[...])
    out[:, :NB] = real
    out[:, NB:] = imag


def turn_kernel(layout, table, weights, share, lags, *refs):
    per_device, windows, places = layout
    even = lax.axis_index("sub") % 2 == 0
    picked, turned, spectra = refs[:-2], refs[-2], refs[-1]
    rows = jnp.concatenate([p[...].astype(jnp.float32) for p in picked], axis=0).astype(jnp.bfloat16)
    real, imag = whiten(rows, table[...], weights[...], share[...])
    spectra[:, :NB] = real.astype(jnp.float32)
    spectra[:, NB:] = imag.astype(jnp.float32)
    side = side_rows(per_device)
    span = 2 * side
    which = lax.broadcasted_iota(jnp.int32, (8, LANES), 0) % per_device

    def rows_of(first, lane):
        tiled = jnp.zeros((8, LANES), jnp.float32)
        for v in range(per_device):
            rows = [spectra[f + v:f + v + 1, lane:lane + LANES] for f in first]
            row = rows[0] if first[0] == first[-1] else jnp.where(even, rows[0], rows[-1])
            tiled = jnp.where(which == v, row, tiled)
        return tiled[None]

    for lane in range(0, NB, LANES):
        cosine = lags[:, lane:lane + LANES].reshape(side // 8, 8, LANES)
        sine = lags[:, NB + lane:NB + lane + LANES].reshape(side // 8, 8, LANES)
        for at, place in enumerate(places):
            for behind in range(windows):
                first = [(here * windows + behind) * per_device for here in place]
                real, imag = rows_of(first, lane), rows_of(first, NB + lane)
                cr, si, sr, ci = cosine * real, sine * imag, sine * real, cosine * imag
                up = jnp.concatenate([cr - si, cr + si], axis=0).reshape(span, LANES)
                down = jnp.concatenate([ci + sr, ci - sr], axis=0).reshape(span, LANES)
                spot = pl.ds(at * span, span)
                turned[behind, spot, lane:lane + LANES] = up.astype(jnp.bfloat16)
                turned[behind, spot, NB + lane:NB + lane + LANES] = down.astype(jnp.bfloat16)


def others_kernel(table, weights, share, *refs):
    parts, (white, raw) = refs[:-2], refs[-2:]
    sub_at = lax.axis_index("sub")
    groups, _, group, samples = raw.shape
    each = len(parts) // white.shape[0]
    for i in range(white.shape[0]):
        if each == 1:
            rows = parts[i][...]
        else:
            for half, place in ((parts[2 * i], sub_at), (parts[2 * i + 1], 1 - sub_at)):
                raw[:, pl.ds(place, 1)] = half[...].reshape(groups, 1, group, samples)
            rows = raw[...].reshape(white.shape[1], samples)
        block = rows.shape[0] // 2 if rows.shape[0] % 32 == 0 else rows.shape[0]
        for start in range(0, rows.shape[0], block):
            span = slice(start, start + block)
            real, imag = whiten(rows[span], table[...], weights[...], share[...])
            white[i, span, :NB] = real
            white[i, span, NB:] = imag


def lag_product(turned, own, white):
    total = lax.dot_general(turned[0], own[...], NT, preferred_element_type=jnp.float32)
    for i in range(white.shape[0]):
        total += lax.dot_general(turned[1 + i], white[i], NT, preferred_element_type=jnp.float32)
    return total


def base_kernel(turned, own, base):
    base[...] = lax.dot_general(turned[0], own[...], NT, preferred_element_type=jnp.float32)


def lag_kernel(factor, based, turned, own, white, mask, *pieces):
    if based:
        total = own[...]
        for i in range(white.shape[0]):
            total += lax.dot_general(turned[1 + i], white[i], NT, preferred_element_type=jnp.float32)
    else:
        total = lag_product(turned, own, white)
    result = total * (mask[...].astype(jnp.float32) * factor)
    span = result.shape[0] // len(pieces)
    for at, piece in enumerate(pieces):
        piece[...] = result[at * span:(at + 1) * span, :].astype(jnp.bfloat16)


def first_kernel(layout, factor, count, table, weights, share, lags, own, white, mask, *refs):
    sources, (turned, *pieces, spectra) = refs[:count], refs[count:]
    turn_kernel(layout, table, weights, share, lags, *sources, turned, spectra)
    lag_kernel(factor, False, turned, own, white, mask, *pieces)


def put_slots(layout, listed, wide, out, stage, sems, slot):
    tie, blocks, per_device, first, reverse = layout
    block_at, tie = lax.axis_index("chan"), on_core(tie, lax.axis_index("sub"))
    row = lax.broadcasted_iota(jnp.int32, listed.shape, 0)
    column = lax.broadcasted_iota(jnp.int32, listed.shape, 1)
    width = stage.shape[3]
    block = block_at if reverse else partner(block_at, blocks, tie)
    copies = []
    for e in offsets_of(block_at, blocks, tie, reverse):
        chosen = jnp.where((row == block) & (column == e), listed, 0.0)
        pair = jnp.broadcast_to(jnp.sum(chosen, keepdims=True), (per_device, width))
        for t in range(LAGS):
            tau = MAXLAG - t if reverse else t - MAXLAG
            spot = lag_row(tau, per_device)
            stage[slot, t] = wide[spot:spot + per_device, :] * pair
        target = out.at[e, :, :, pl.ds(first, width)]
        copies.append(pltpu.make_async_copy(stage.at[slot], target, sems.at[slot]))
        copies[-1].start()
        slot += 1
    return copies


def receiver_kernel(layout, pairs, turned, mask, *refs):
    ties, blocks, per_device, chunks, factor = layout
    count = len(chunks)
    owns, whites, pieces = refs[:count], refs[count:2 * count], refs[2 * count:-5]
    out, source_out, wide, stage, sems = refs[-5:]
    listed = pairs[...].astype(jnp.float32)
    copies = []
    for at, tie in enumerate(ties):
        for i, (start, size) in enumerate(chunks):
            lanes = slice(start, start + size)
            if at:
                wide[at, :, lanes] = pieces[i * (len(ties) - 1) + at - 1][...].astype(jnp.float32)
            else:
                wide[at, :, lanes] = lag_product(turned, owns[i], whites[i]) * (mask[:, lanes].astype(jnp.float32) * factor)
        turns = [(out, False)] + ([] if at else [(source_out, True)])
        for target, reverse in turns:
            part = (tie, blocks, per_device, 0, reverse)
            copies += put_slots(part, listed, wide.at[at], target, stage, sems, len(copies))
    for copy in copies:
        copy.wait()


def source_kernel(layout, pairs, *refs):
    ties, blocks, per_device, first = layout
    pieces, (_, out, wide, stage, sems) = refs[:len(ties)], refs[len(ties):]
    listed = pairs[...].astype(jnp.float32)
    copies = []
    for at, tie in enumerate(ties):
        wide[at] = pieces[at][...].astype(jnp.float32)
        part = (tie, blocks, per_device, first, True)
        copies += put_slots(part, listed, wide.at[at], out, stage, sems, len(copies))
    for copy in copies:
        copy.wait()


def ties_of(blocks, subs):
    if blocks == 4:
        return [("xor", (step,) * subs) for step in (0, 2, 3, 1)]
    ties = []
    for moved in (0, 1, -1, 2, -2):
        if all((m[0] - moved) % blocks for _, m in ties):
            ties.append(("shift", (moved,) * subs))
    return ties


def on_core(tie, core):
    kind, steps = tie
    if len(set(steps)) == 1:
        return kind, steps[0]
    return kind, jnp.where(core % 2 == 0, steps[0], steps[1])


def partner(block, blocks, tie, back=False):
    kind, step = tie
    if kind == "xor":
        return block ^ step
    return (block + (step if back else -step) + blocks) % blocks


def offsets_of(block, blocks, tie, back):
    kind, step = tie
    if kind == "shift":
        return [e for e in range(OFFS) if (e - REACH - step) % blocks == 0]
    if isinstance(step, int) and step % 2 == 0:
        return [e for e in range(OFFS) if abs(e - REACH) == step]
    ahead = (block ^ step) - block if back else block - (block ^ step)
    return [jnp.where((ahead + blocks) % blocks == 1, REACH + 1, REACH - 1)]


def exchange(value, blocks, subs, tie, back=False):
    kind, steps = tie
    route = [
        (partner(b, blocks, (kind, steps[c]), back) * subs + c, b * subs + c)
        for b in range(blocks)
        for c in range(subs)
    ]
    return lax.ppermute(value, ("chan", "sub"), route)


def chunks_of(channels):
    if channels < 2 * LANES or channels % LANES:
        return [(0, channels)]
    first = channels * 2 // 5 // LANES * LANES
    return [(0, first), (first, channels - first)]


def shift(block, axis, distance):
    count = lax.axis_size(axis)
    return lax.ppermute(block, axis, [(i, (i + distance) % count) for i in range(count)])


def slots_of(ties, blocks):
    return sum(len(offsets_of(0, blocks, (kind, steps[0]), False)) for kind, steps in ties)


def in_hbm(value):
    return pltpu.with_memory_space_constraint(value, pltpu.HBM)


def after(value, *others):
    return lax.optimization_barrier((value, *others))[0]


def on_device(traces, channel_mask, smooth_width, source_phase, pair_list):
    _, channels, samples = traces.shape
    blocks, windows, subs = (lax.axis_size(a) for a in ("chan", "win", "sub"))
    sub_at = lax.axis_index("sub")
    per_device = VS // (windows * subs)
    group = per_device * STRIDE
    ties = ties_of(blocks, subs)
    span = 2 * side_rows(per_device)
    chunks = chunks_of(channels)
    table, lags = dft_table(samples), lag_table(samples, per_device)
    factor = (NB * windows) ** (-0.5)
    bf16, f32 = jnp.bfloat16, jnp.float32
    like = jax.ShapeDtypeStruct
    mask_row = channel_mask.reshape(1, channels)

    def half_of(rows, start, size):
        grouped = rows.reshape(channels // (subs * group), subs, group, samples)
        first, count = start // (subs * group), size // (subs * group)
        half = lax.dynamic_slice(grouped, (first, sub_at, 0, 0), (count, 1, group, samples))
        return half.reshape(size // subs, samples)

    def from_windows(half):
        return [shift(half, "win", d) for d in range(1, windows)]

    def with_other_core(received):
        return [side for piece in received for side in (piece, shift(piece, "sub", 1))]

    def whiten_others(size, both, hint):
        return pl.pallas_call(
            others_kernel,
            out_shape=like((windows - 1, size, 2 * NB), bf16),
            in_specs=[VMEM] * (3 + len(both)),
            out_specs=VMEM,
            scratch_shapes=[pltpu.VMEM((size // (subs * group), subs, group, samples), bf16)],
            compiler_params=params(24),
            cost_estimate=hint,
            name="whiten_others",
        )(table, weights, share, *both)

    def correlate(start, size, turned, base, white):
        count = turned.shape[1] // span
        return pl.pallas_call(
            functools.partial(lag_kernel, factor, True),
            out_shape=tuple(like((span, size), bf16) for _ in range(count)),
            in_specs=[VMEM] * 4,
            out_specs=(VMEM,) * count,
            compiler_params=params(24),
            cost_estimate=LONG,
            name="lag_pieces",
        )(turned, base, white, mask_row[:, start:start + size])

    half = half_of(traces, *chunks[0])
    received = [from_windows(half)]
    *owns, weights, share, rows, table = pl.pallas_call(
        functools.partial(setup_kernel, chunks),
        out_shape=tuple(like((size, 2 * NB), bf16) for _, size in chunks)
        + (like((NB, NB), bf16), like((1, NB), f32))
        + (like((channels, samples), bf16), like(table.shape, bf16)),
        in_specs=[HBM, HBM, HBM],
        out_specs=(VMEM,) * (len(chunks) + 4),
        scratch_shapes=[pltpu.SemaphoreType.DMA((TABLE_PARTS + 3,)), pltpu.VMEM((1, NB), jnp.int32)],
        compiler_params=params(24),
        cost_estimate=SHORT,
        name="whiten_own",
    )(in_hbm(traces), in_hbm(table), in_hbm(after(smooth_width, half).reshape(1, NB)))
    received += [from_windows(after(rows, share)[a:a + n]) for a, n in chunks[1:]]
    near = pl.pallas_call(
        functools.partial(near_kernel, (windows, subs, per_device)),
        out_shape=like((windows * per_device, samples), f32),
        in_specs=[SMEM] + [VMEM] * (1 + windows),
        out_specs=VMEM,
        compiler_params=params(16),
        cost_estimate=SHORT,
        name="pick_sources",
    )(source_phase, after(mask_row, weights), half, *received[0])

    def turn(sources, places, hint, *first):
        rows_each = windows * per_device
        return pl.pallas_call(
            functools.partial(turn_kernel, (per_device, windows, places)),
            out_shape=like((windows, len(places) * span, 2 * NB), bf16),
            in_specs=[VMEM] * (4 + len(sources)),
            out_specs=VMEM,
            scratch_shapes=[pltpu.VMEM((len(places) * rows_each, 2 * NB), f32)],
            compiler_params=params(24),
            cost_estimate=hint,
            name="turn_sources",
        )(table, weights, after(share, *first), lags, *sources)

    turned_own = turn([near], [(0,)], LONG)
    inbound = with_other_core(received[0])
    white = whiten_others(chunks[0][1], inbound, SHORT)
    if ties[1][0] == "xor":
        beside = exchange(near, blocks, subs, ("xor", (1,) * subs))
        two = jnp.concatenate([after(near, turned_own), beside], axis=0).astype(bf16)
        sources = [beside, exchange(two, blocks, subs, ("xor", (2,) * subs))]
        places = [tuple(step - 1 for step in steps) for _, steps in ties[1:]]
    else:
        sources = [exchange(near, blocks, subs, tie) for tie in ties[1:]]
        places = [(at,) for at in range(len(sources))]
    start, size = chunks[0]
    count = len(places)
    turned, *first_pieces = pl.pallas_call(
        functools.partial(first_kernel, (per_device, windows, places), factor, len(sources)),
        out_shape=(like((windows, count * span, 2 * NB), bf16),) + (like((span, size), bf16),) * count,
        in_specs=[VMEM] * (7 + len(sources)),
        out_specs=(VMEM,) * (1 + count),
        scratch_shapes=[pltpu.VMEM((count * windows * per_device, 2 * NB), f32)],
        compiler_params=params(24),
        cost_estimate=SHORT,
        name="turn_and_lag",
    )(table, weights, share, lags, owns[0], white, mask_row[:, start:start + size], *sources)
    pieces, arrived, whites = [], [], [white]
    for i, (start, size) in enumerate(chunks):
        if i:
            whites.append(whiten_others(size, [after(r, *pieces[-1]) for r in received[i]], LONG))
            base = pl.pallas_call(
                base_kernel,
                out_shape=like((turned.shape[1], size), f32),
                in_specs=[VMEM, VMEM],
                out_specs=VMEM,
                compiler_params=params(24),
                cost_estimate=SHORT,
                name="lag_base",
            )(after(turned, *pieces[-1]), owns[i])
            pieces.append(correlate(start, size, turned, base, whites[i]))
        else:
            pieces.append(tuple(first_pieces))
        ahead = arrived[-1][:1] if i else []
        sent = [after(p, *ahead) for p in pieces[-1]]
        arrived.append([exchange(p, blocks, subs, tie, True) for tie, p in zip(ties[1:], sent)])
    stack = like((OFFS, LAGS, per_device, channels), f32)

    def scratch(count, slots, width):
        return [
            pltpu.VMEM((count, span, width), f32),
            pltpu.VMEM((slots, LAGS, per_device, width), f32),
            pltpu.SemaphoreType.DMA((slots,)),
        ]

    remote = [piece for group in pieces for piece in group]
    receiver_stack, source_stack = pl.pallas_call(
        functools.partial(receiver_kernel, (ties, blocks, per_device, chunks, factor)),
        out_shape=(stack, stack),
        in_specs=[VMEM] * (3 + 2 * len(chunks) + len(remote)),
        out_specs=(HBM, HBM),
        scratch_shapes=scratch(len(ties), slots_of(ties, blocks) + 1, channels),
        compiler_params=params(24),
        cost_estimate=LONG,
        name="receiver_order",
    )(pair_list, turned_own, mask_row, *owns, *whites, *remote)
    slots = slots_of(ties[1:], blocks)
    for (start, size), back in zip(chunks, arrived):
        source_stack = pl.pallas_call(
            functools.partial(source_kernel, (ties[1:], blocks, per_device, start)),
            out_shape=stack,
            in_specs=[VMEM] * (1 + count) + [HBM],
            out_specs=HBM,
            scratch_shapes=scratch(count, slots, size),
            input_output_aliases={1 + count: 0},
            compiler_params=params(16),
            cost_estimate=SHORT,
            name="source_order",
        )(pair_list, *back, source_stack)
    order = (2, 0, 1, 3)
    return (jnp.transpose(receiver_stack, order), jnp.transpose(source_stack, order))


def solution(mesh):
    in_specs = (
        P(("groups", "win"), "chan", None),
        P(("groups", "chan")),
        P(),
        P("groups"),
        P("groups", None),
    )
    out_specs = (
        P(("win", "sub"), None, None, ("groups", "chan")),
        P(("groups", "chan", "win", "sub"), None, None, None),
    )
    return jax.shard_map(
        on_device, mesh=mesh, in_specs=in_specs, out_specs=out_specs, check_vma=False
    )
```
